256 devices in a mesh: tok: 64 (over x, z, core), head: 4 (over y).
Axes of the slice: x: 4, y: 4, z: 8, core: 2. Of those that a mesh axis runs over, the one named last changes fastest.
Arguments:
- tokens: bfloat16 [65536, 1536], P('tok'), may hold values from -96 to 96
- qkv_weight: bfloat16 [1536, 4608], P(None, 'head'), may hold values from -0.15625 to 0.15625
- rate_weight: bfloat16 [1536, 12], P(None, 'head'), may hold values from -0.15625 to 0.15625
- first_fast: bfloat16 [4, 384, 768], P('head'), may hold values from -0.3125 to 0.3125
- gate_fast: bfloat16 [4, 384, 768], P('head'), may hold values from -0.3125 to 0.3125
- second_fast: bfloat16 [4, 768, 384], P('head'), may hold values from -0.21875 to 0.21875
- fast_gain: float32 [1536], P('head'), may hold values from 0.1 to 1.9
- out_weight: bfloat16 [1536, 1536], P('head'), may hold values from -0.15625 to 0.15625
- frame_lengths: int32 [128], replicated, may hold values from 1 to 1024, 65536 in all
Outputs:
- layer_out: bfloat16 [65536, 1536], P('tok', 'head')
The draws below stay inside these ranges and needn't reach their ends.
Inputs may be any that keep to these rules, and one draw needn't show every extreme that they name: `frame_lengths`: they sum to 65536; one frame has exactly 1024 tokens.
All inputs are finite; a program needn't handle non-finite values.
Results may differ from the reference program's by a relative error of at most 0.02.
The reference program's roundings to bfloat16 on the way count: a program that leaves them out, or rounds other values in their place, can miss the bound.
Values may be sent and summed in bfloat16 or wider, within the bound.
No kernel may reach another device: no remote copies, remote signals or barrier semaphores. Data moves between devices by JAX's collectives and lax.ppermute only.
A program may use at most 128 MiB of HBM per device.

```python
import math
import jax
import jax.numpy as jnp
import numpy as np
from jax import lax

D = 1536
HEADS = 4
DH = 384
HID = 768
FRAME = 1024
TOK_DEV = 1024
TOKENS = 65536
FRAMES = 128


def draw_tokens(key, part):
    key_base = jax.random.fold_in(jax.random.fold_in(key, 17), 0)
    key_rows = jax.random.fold_in(jax.random.fold_in(key, 17), 2)
    base = jnp.clip(jax.random.normal(key_base, (TOKENS, D), jnp.float32), -4.0, 4.0)
    row_scale = jnp.exp(jax.random.uniform(key_rows, (TOKENS, 1), jnp.float32, math.log(0.5), math.log(2.0)))
    values = row_scale * base
    return values.astype(jnp.bfloat16)


def levels(key, shape, cuts, least, top_value):
    level, own = 1.0, jax.random.fold_in(key, 6)
    for dim, blocks in cuts:
        steps = jnp.exp(jax.random.uniform(jax.random.fold_in(own, dim), (blocks,), jnp.float32, least / len(cuts), top_value / len(cuts)))
        level = level * jnp.repeat(steps, shape[dim] // blocks).reshape([-1 if axis == dim else 1 for axis in range(len(shape))])
    return level


def profile(amount, total, most, skew):
    weights = [(1 << 20) // math.isqrt(standing ** skew) + 1 for standing in range(2, amount + 1)]
    surplus, holding = total - most - (amount - 1), [1] * (amount - 1)
    while surplus > 0:
        movable = [i for i in range(amount - 1) if holding[i] < most]
        whole, budget = sum([weights[i] for i in movable]), surplus
        for i in movable:
            addition = min(most - holding[i], max(1, budget * weights[i] // whole), surplus)
            holding[i] = holding[i] + addition
            surplus = surplus - addition
    return np.array([most] + holding)


def ragged_sizes(stream_key, number_of, total, reach, skew):
    if number_of == 2:
        one = jax.random.randint(stream_key, (), max(1, total - reach), min(reach, total - 1) + 1)
        return jnp.stack([one, total - one])
    sizes = jnp.asarray(profile(number_of, total, reach, skew), jnp.int32)
    twos = (number_of - 1) // 2
    giver, receiver = sizes[1:1 + 2 * twos:2], sizes[2:2 + 2 * twos:2]
    margin = jnp.minimum(giver - 1, reach - receiver)
    shifted = jax.random.randint(jax.random.fold_in(stream_key, 1), (twos,), 0, 1 << 20) % (margin + 1)
    sizes = sizes.at[1:1 + 2 * twos:2].set(giver - shifted).at[2:2 + 2 * twos:2].set(receiver + shifted)
    return sizes[jax.random.permutation(jax.random.fold_in(stream_key, 2), number_of)]


def centred(stream_key, shape, spread, bound, shards=(), kind=jnp.bfloat16):
    loudness = levels(stream_key, shape, shards, -0.22, 0.18) if shards else 1.0
    entries = jax.random.normal(stream_key, shape, jnp.float32) * spread * loudness
    return jnp.minimum(jnp.maximum(entries, -bound), bound).astype(kind)


def setup_inputs(seed: int = 0) -> dict:
    seeds = jax.random.split(jax.random.key(seed), 10)
    tokens = draw_tokens(jax.random.fold_in(seeds[9], 71), 0)
    qkv_weight = centred(seeds[1], (D, 3 * D), D ** -0.5, 0.15625, ((1, 4),))
    rate_weight = centred(seeds[2], (D, 3 * HEADS), D ** -0.5, 0.15625, ((1, 4),))
    first_fast = centred(seeds[3], (HEADS, DH, HID), DH ** -0.5, 0.3125, ((0, 4),))
    gate_fast = centred(seeds[4], (HEADS, DH, HID), DH ** -0.5, 0.3125, ((0, 4),))
    second_fast = centred(seeds[5], (HEADS, HID, DH), HID ** -0.5, 0.21875, ((0, 4),))
    fast_gain = jnp.clip(1.0 + 0.18 * jax.random.normal(seeds[6], (D,), jnp.float32), 0.1, 1.9)
    out_weight = centred(seeds[7], (D, D), D ** -0.5, 0.15625, ((0, 4),))
    frame_lengths = ragged_sizes(seeds[8], FRAMES, TOKENS, FRAME, 2).astype(jnp.int32)
    return {"tokens": tokens, "qkv_weight": qkv_weight, "rate_weight": rate_weight, "first_fast": first_fast, "gate_fast": gate_fast, "second_fast": second_fast, "fast_gain": fast_gain, "out_weight": out_weight, "frame_lengths": frame_lengths}


def frame_attention(query, padded, key_ids, query_ids, block, frame):
    dim_head = query.shape[1]
    number = query.shape[0] // block

    def attend(index):
        offset = index * block
        q_blk = lax.dynamic_slice_in_dim(query, offset, block, 0)
        window = lax.dynamic_slice_in_dim(padded, offset, block + 2 * frame, 0)
        k_blk = window[:, :dim_head]
        v_blk = window[:, dim_head:]
        q_ids = lax.dynamic_slice_in_dim(query_ids, offset, block, 0)
        k_ids = lax.dynamic_slice_in_dim(key_ids, offset, block + 2 * frame, 0)
        scores = lax.dot_general(q_blk, k_blk, (((1,), (1,)), ((), ())), preferred_element_type=jnp.float32) / math.sqrt(dim_head)
        scores = jnp.where(q_ids[:, None] == k_ids[None, :], scores, -1e+30)
        highest = lax.optimization_barrier(jnp.max(scores, axis=1, keepdims=True))
        weights = jnp.exp(scores - highest)
        probs = (weights / lax.optimization_barrier(jnp.sum(weights, axis=1, keepdims=True))).astype(jnp.bfloat16)
        return jnp.dot(probs, v_blk, preferred_element_type=jnp.float32)
    blocks = lax.map(attend, jnp.arange(number, dtype=jnp.int32))
    return blocks.reshape(query.shape[0], dim_head)

def fast_update(key_part, value_part, rates, first_w, gate_w, second_w):
    first_act = jnp.dot(key_part, first_w, preferred_element_type=jnp.float32)
    gate_act = jnp.dot(key_part, gate_w, preferred_element_type=jnp.float32)
    sigma = jax.nn.sigmoid(first_act)
    silu_act = first_act * sigma
    hidden = (silu_act * gate_act).astype(jnp.bfloat16)
    back = lax.dot_general(value_part, second_w, (((1,), (1,)), ((), ())), preferred_element_type=jnp.float32)
    err_first = (rates[:, 0:1] * back * gate_act * sigma * (1.0 + first_act * (1.0 - sigma))).astype(jnp.bfloat16)
    err_gate = (rates[:, 1:2] * back * silu_act).astype(jnp.bfloat16)
    err_second = (rates[:, 2:3] * value_part.astype(jnp.float32)).astype(jnp.bfloat16)
    contract = (((0,), (0,)), ((), ()))
    upd_first = lax.dot_general(key_part, err_first, contract, preferred_element_type=jnp.float32)
    upd_gate = lax.dot_general(key_part, err_gate, contract, preferred_element_type=jnp.float32)
    upd_second = lax.dot_general(hidden, err_second, contract, preferred_element_type=jnp.float32)
    return (upd_first, upd_gate, upd_second)

def fast_renorm(old, update):
    old_wide = old.astype(jnp.float32)
    fresh = old_wide + update
    old_sq = lax.optimization_barrier(jnp.sum(old_wide * old_wide, axis=1, keepdims=True))
    fresh_sq = lax.optimization_barrier(jnp.sum(fresh * fresh, axis=1, keepdims=True))
    return (fresh * jnp.sqrt(old_sq) / jnp.sqrt(fresh_sq + 1e-06)).astype(jnp.bfloat16)

def fast_apply(query, first_new, gate_new, second_new, gain_part):
    first_act = jnp.dot(query, first_new, preferred_element_type=jnp.float32)
    gate_act = jnp.dot(query, gate_new, preferred_element_type=jnp.float32)
    hidden = (jax.nn.silu(first_act) * gate_act).astype(jnp.bfloat16)
    applied = jnp.dot(hidden, second_new, preferred_element_type=jnp.float32)
    scale = lax.rsqrt(lax.optimization_barrier(jnp.mean(applied * applied, axis=1, keepdims=True)) + 1e-06)
    return applied * scale * gain_part[None, :]

def reference(tokens, qkv_weight, rate_weight, first_fast, gate_fast, second_fast, fast_gain, out_weight, frame_lengths):
    qkv = jnp.dot(tokens, qkv_weight, preferred_element_type=jnp.float32).astype(jnp.bfloat16)
    rates = 0.25 / math.sqrt(TOKENS) * jax.nn.softplus(jnp.dot(tokens, rate_weight, preferred_element_type=jnp.float32))
    frame_ends = jnp.cumsum(frame_lengths).astype(jnp.int32)
    positions = jnp.arange(TOKENS, dtype=jnp.int32)
    frame_id = lax.optimization_barrier(jnp.sum((frame_ends[None, :] <= positions[:, None]).astype(jnp.int32), axis=1)).astype(jnp.int32)
    outside = jnp.full((FRAME,), -1, jnp.int32)
    key_ids = jnp.concatenate([outside, frame_id, outside]).astype(jnp.int32)
    block = min(512, TOK_DEV)
    pieces = []
    for head in range(HEADS):
        base = head * 3 * DH
        query = qkv[:, base:base + DH]
        key_part = qkv[:, base + DH:base + 2 * DH]
        value_part = qkv[:, base + 2 * DH:base + 3 * DH]
        key_value = qkv[:, base + DH:base + 3 * DH]
        zero_rim = jnp.zeros((FRAME, 2 * DH), jnp.bfloat16)
        padded = jnp.concatenate([zero_rim, key_value, zero_rim], axis=0)
        attended = frame_attention(query, padded, key_ids, frame_id, block, FRAME)
        head_rates = rates[:, 3 * head:3 * head + 3]
        ordered = jnp.stack([head_rates[:, 0], head_rates[:, 1], head_rates[:, 2]], axis=1)
        upd_first, upd_gate, upd_second = fast_update(key_part, value_part, ordered, first_fast[head], gate_fast[head], second_fast[head])
        first_new = fast_renorm(first_fast[head], upd_first)
        gate_new = fast_renorm(gate_fast[head], upd_gate)
        second_new = fast_renorm(second_fast[head], upd_second)
        normed = fast_apply(query, first_new, gate_new, second_new, fast_gain[head * DH:(head + 1) * DH])
        pieces.append((attended + normed).astype(jnp.bfloat16))
    mixed = jnp.concatenate(pieces, axis=1)
    return jnp.dot(mixed, out_weight, preferred_element_type=jnp.float32).astype(jnp.bfloat16)
```

```python
import functools
import math

import jax
import jax.numpy as jnp
from jax import lax
from jax.experimental import pallas as pl
from jax.experimental.pallas import tpu as pltpu
from jax.sharding import PartitionSpec as P

DH = 384
HID = 768
TOK = 1024
XS, ZS, CS, HS = 4, 8, 2, 4
SHARDS = XS * ZS * CS
TOKENS = TOK * SHARDS
XROWS = DH // XS
ZROWS = 16
OWNERS = XROWS // ZROWS
WIDE = HID + DH
KB = 256
QB = 256
BF, F32, I32 = jnp.bfloat16, jnp.float32, jnp.int32
NT = (((1,), (1,)), ((), ()))
VM = 56 * 1024 * 1024

SMEM = pl.BlockSpec(memory_space=pltpu.SMEM)
WHOLE = pl.BlockSpec(memory_space=pltpu.VMEM)
DEP = pl.BlockSpec(memory_space=pl.ANY)


def params():
    return pltpu.CompilerParams(vmem_limit_bytes=VM)


def mm(a, b):
    return jnp.dot(a, b, preferred_element_type=F32)


def sds(shape, dtype):
    return jax.ShapeDtypeStruct(shape, dtype)


def shift_x(d):
    return [(t, (t + d * ZS * CS) % SHARDS) for t in range(SHARDS)]


def shift_z(d, to_owner=False, from_owner=False):
    pairs = []
    for t in range(SHARDS):
        x, z, c = t // (ZS * CS), t // CS % ZS, t % CS
        other = (z + d) % ZS
        if (to_owner and other >= OWNERS) or (from_owner and z >= OWNERS):
            continue
        pairs.append((t, (x * ZS + other) * CS + c))
    return pairs


SWAP_C = [(t, t ^ 1) for t in range(SHARDS)]


def shift_h(d):
    return [(h, (h + d) % HS) for h in range(HS)]


def front_kernel(
    pos_ref, t_ref, wk_ref, wv_ref, wr_ref, w1_ref, w3_ref, w2_ref,
    kv_ref, send_ref, keep_ref, acc1, acc3, acc2,
):
    step = pl.program_id(0)

    @pl.when(step == 0)
    def _():
        acc1[...] = jnp.zeros_like(acc1)
        acc3[...] = jnp.zeros_like(acc3)
        acc2[...] = jnp.zeros_like(acc2)

    t = t_ref[...]
    k = mm(t, wk_ref[...]).astype(BF)
    v = mm(t, wv_ref[...]).astype(BF)
    kv_ref[:, :DH] = k
    kv_ref[:, DH:] = v
    raw = mm(t, wr_ref[...])
    rates = (0.25 / math.sqrt(TOKENS)) * (
        jnp.maximum(raw, 0.0) + jnp.log1p(jnp.exp(-jnp.abs(raw)))
    )
    a = mm(k, w1_ref[0])
    b = mm(k, w3_ref[0])
    back = lax.dot_general(v, w2_ref[0], NT, preferred_element_type=F32)
    sig = jax.nn.sigmoid(a)
    act = a * sig
    z = (act * b).astype(BF)
    e1 = (rates[:, 0:1] * back * b * sig * (1.0 + a * (1.0 - sig))).astype(BF)
    e3 = (rates[:, 1:2] * back * act).astype(BF)
    e2 = (rates[:, 2:3] * v.astype(F32)).astype(BF)
    k_t = k.T
    acc1[...] += mm(k_t, e1)
    acc3[...] += mm(k_t, e3)
    acc2[...] += mm(e2.T, z)

    @pl.when(step == pl.num_programs(0) - 1)
    def _():
        core = pos_ref[2]
        low = acc2[:, :DH].T
        high = acc2[:, DH:].T

        @pl.when(core == 0)
        def _():
            keep_ref[:, :HID] = acc1[...]
            keep_ref[:, HID:] = low
            send_ref[:, :HID] = acc3[...].astype(BF)
            send_ref[:, HID:] = high.astype(BF)

        @pl.when(core == 1)
        def _():
            keep_ref[:, :HID] = acc3[...]
            keep_ref[:, HID:] = high
            send_ref[:, :HID] = acc1[...].astype(BF)
            send_ref[:, HID:] = low.astype(BF)


def front(pos, tokens, qkv_weight, rate_weight, first_fast, gate_fast, second_fast):
    rows, wide = tokens.shape
    block = 256
    fixed3 = lambda i: (0, 0, 0)
    return pl.pallas_call(
        front_kernel,
        grid=(rows // block,),
        in_specs=[
            SMEM,
            pl.BlockSpec((block, wide), lambda i: (i, 0)),
            pl.BlockSpec((wide, DH), lambda i: (0, 1)),
            pl.BlockSpec((wide, DH), lambda i: (0, 2)),
            pl.BlockSpec((wide, 3), lambda i: (0, 0)),
            pl.BlockSpec((1, DH, HID), fixed3),
            pl.BlockSpec((1, DH, HID), fixed3),
            pl.BlockSpec((1, HID, DH), fixed3),
        ],
        out_specs=[
            pl.BlockSpec((block, 2 * DH), lambda i: (i, 0)),
            pl.BlockSpec((DH, WIDE), lambda i: (0, 0)),
            pl.BlockSpec((DH, WIDE), lambda i: (0, 0)),
        ],
        out_shape=[sds((rows, 2 * DH), BF), sds((DH, WIDE), BF), sds((DH, WIDE), F32)],
        scratch_shapes=[pltpu.VMEM((DH, HID), F32)] * 3,
        compiler_params=params(),
        name="front",
    )(pos, tokens, qkv_weight, qkv_weight, rate_weight, first_fast, gate_fast, second_fast)


def rs_x_kernel(pos_ref, keep_ref, got_ref, own_ref, *outs):
    x = pos_ref[0]
    for d, out in enumerate((own_ref, *outs)):
        rows = pl.ds(pl.multiple_of(lax.rem(x + d, XS) * XROWS, XROWS), XROWS)
        out[...] = (keep_ref[rows, :] + got_ref[rows, :].astype(F32)).astype(out.dtype)


def rs_x(pos, keep, got):
    return pl.pallas_call(
        rs_x_kernel,
        in_specs=[SMEM, WHOLE, WHOLE],
        out_specs=[WHOLE] * XS,
        out_shape=[sds((XROWS, WIDE), F32)] + [sds((XROWS, WIDE), BF)] * (XS - 1),
        compiler_params=params(),
        name="rs_x",
    )(pos, keep, got)


def rs_z_kernel(pos_ref, own_ref, g1, g2, g3, *rest):
    outs, total = rest[-ZS - 1 : -1], rest[-1]
    z = pos_ref[1]
    total[...] = (own_ref[...] + g1[...].astype(F32)) + (
        g2[...].astype(F32) + g3[...].astype(F32)
    )
    for d, out in enumerate(outs):
        owner = jnp.minimum(lax.rem(z + d, ZS), OWNERS - 1)
        rows = pl.ds(pl.multiple_of(owner * ZROWS, ZROWS), ZROWS)
        out[...] = total[rows, :].astype(out.dtype)


def rs_z(pos, own, got, deps):
    return pl.pallas_call(
        rs_z_kernel,
        in_specs=[SMEM] + [WHOLE] * XS + [DEP] * len(deps),
        out_specs=[WHOLE] * ZS,
        out_shape=[sds((ZROWS, WIDE), F32)] + [sds((ZROWS, WIDE), BF)] * (ZS - 1),
        scratch_shapes=[pltpu.VMEM((XROWS, WIDE), F32)],
        compiler_params=params(),
        name="rs_z",
    )(pos, own, *got, *deps)


def renorm_kernel(old_ref, own_ref, *rest):
    got, out = rest[: ZS - 1], rest[-1]
    update = own_ref[...]
    for g in got:
        update = update + g[...].astype(F32)
    old = old_ref[...]
    fresh = old + update
    for cols in (slice(0, HID), slice(HID, WIDE)):
        w, f = old[:, cols], fresh[:, cols]
        w_sq = jnp.sum(w * w, axis=1, keepdims=True)
        f_sq = jnp.sum(f * f, axis=1, keepdims=True)
        out[:, cols] = (f * (jnp.sqrt(w_sq) / jnp.sqrt(f_sq + 1e-6))).astype(BF)


def renorm(old, own, got, deps):
    return pl.pallas_call(
        renorm_kernel,
        in_specs=[WHOLE] * (ZS + 1) + [DEP] * len(deps),
        out_specs=WHOLE,
        out_shape=sds((ZROWS, WIDE), BF),
        compiler_params=params(),
        name="renorm",
    )(old, own, *got, *deps)


def ag_z_kernel(pos_ref, *rest):
    blocks, out = rest[:ZS], rest[-1]
    z = pos_ref[1]
    for d, block in enumerate(blocks):
        owner = lax.rem(z - d + ZS, ZS)

        @pl.when(owner < OWNERS)
        def _():
            out[pl.ds(pl.multiple_of(owner * ZROWS, ZROWS), ZROWS), :] = block[...]


def ag_z(pos, blocks, deps):
    return pl.pallas_call(
        ag_z_kernel,
        in_specs=[SMEM] + [WHOLE] * ZS + [DEP] * len(deps),
        out_specs=WHOLE,
        out_shape=sds((XROWS, WIDE), BF),
        compiler_params=params(),
        name="ag_z",
    )(pos, *blocks, *deps)


def ag_x_kernel(pos_ref, *rest):
    blocks, out = rest[:XS], rest[-1]
    x = pos_ref[0]
    for d, block in enumerate(blocks):
        owner = lax.rem(x - d + XS, XS)
        out[pl.ds(pl.multiple_of(owner * XROWS, XROWS), XROWS), :] = block[...]


def ag_x(pos, blocks, deps):
    return pl.pallas_call(
        ag_x_kernel,
        in_specs=[SMEM] + [WHOLE] * XS + [DEP] * len(deps),
        out_specs=WHOLE,
        out_shape=sds((DH, WIDE), BF),
        compiler_params=params(),
        name="ag_x",
    )(pos, *blocks, *deps)


def project_kernel(t_ref, w_ref, dep_ref, q_ref):
    q_ref[...] = mm(t_ref[...], w_ref[...]).astype(BF)


def project(tokens, qkv_weight, dep):
    rows, wide = tokens.shape
    block = 256
    return pl.pallas_call(
        project_kernel,
        grid=(rows // block,),
        in_specs=[
            pl.BlockSpec((block, wide), lambda i: (i, 0)),
            pl.BlockSpec((wide, DH), lambda i: (0, 0)),
            DEP,
        ],
        out_specs=pl.BlockSpec((block, DH), lambda i: (i, 0)),
        out_shape=sds((rows, DH), BF),
        compiler_params=params(),
        name="project",
    )(tokens, qkv_weight, dep)


def attend_kernel(piece, bounds_ref, rows_ref, q_ref, before, mine, after, dep_ref, out_ref, s_ref):
    low, high = bounds_ref[2 * piece], bounds_ref[2 * piece + 1]
    first = lax.div(low, KB)
    last = lax.div(high + KB - 1, KB)
    q = q_ref[...]
    begin, end = rows_ref[:, 0:1], rows_ref[:, 1:2]
    per = TOK // KB
    scale = 1.0 / math.sqrt(DH)

    def segments(step, carry):
        for s, ref in enumerate((before, mine, after)):
            lo = jnp.clip(first, s * per, (s + 1) * per)
            hi = jnp.clip(last, s * per, (s + 1) * per)
            carry = lax.fori_loop(lo, hi, functools.partial(step, s, ref), carry)
        return carry

    def scores(s, ref, kb, top):
        k = ref[pl.ds(pl.multiple_of((kb - s * per) * KB, KB), KB), :DH]
        sc = lax.dot_general(q, k, NT, preferred_element_type=F32) * scale
        col = lax.broadcasted_iota(I32, (QB, KB), 1) + kb * KB
        sc = jnp.where((col >= begin) & (col < end), sc, -1e30)
        s_ref[kb] = sc
        return jnp.maximum(top, jnp.max(sc, axis=1, keepdims=True))

    top = segments(scores, jnp.full((QB, 1), -1e30, F32))

    def weigh(kb, total):
        w = jnp.exp(s_ref[kb] - top)
        s_ref[kb] = w
        return total + jnp.sum(w, axis=1, keepdims=True)

    total = lax.fori_loop(first, last, weigh, jnp.zeros((QB, 1), F32))
    inverse = 1.0 / total
    out_ref[...] = jnp.zeros_like(out_ref)

    def gather(s, ref, kb, carry):
        v = ref[pl.ds(pl.multiple_of((kb - s * per) * KB, KB), KB), DH:]
        probs = (s_ref[kb] * inverse).astype(BF)
        out_ref[...] += mm(probs, v)
        return carry

    segments(gather, 0)


def attend(piece, bounds, row_bounds, query, before, mine, after, dep):
    return pl.pallas_call(
        functools.partial(attend_kernel, piece),
        grid=(1,),
        in_specs=[
            SMEM,
            pl.BlockSpec((QB, 2), lambda i: (piece, 0)),
            pl.BlockSpec((QB, DH), lambda i: (piece, 0)),
            WHOLE,
            WHOLE,
            WHOLE,
            DEP,
        ],
        out_specs=pl.BlockSpec((QB, DH), lambda i: (0, 0)),
        out_shape=sds((QB, DH), F32),
        scratch_shapes=[pltpu.VMEM((3 * TOK // KB, QB, KB), F32)],
        compiler_params=params(),
        name=f"attend_{piece}",
    )(bounds, row_bounds, query, before, mine, after, dep)


def apply_kernel(pos_ref, q_ref, own_ref, other_ref, att_ref, gain_ref, out_ref, *rest):
    core = pos_ref[2]
    q = q_ref[...]
    mine = mm(q, own_ref[:, :HID])
    theirs = mm(q, other_ref[:, :HID])
    even = core == 0
    a = jnp.where(even, mine, theirs)
    b = jnp.where(even, theirs, mine)
    hidden = (a * jax.nn.sigmoid(a) * b).astype(BF)
    h0, h1 = hidden[:, :DH], hidden[:, DH:]
    h_own = jnp.where(even, h0, h1)
    h_other = jnp.where(even, h1, h0)
    applied = mm(h_own, own_ref[:, HID:]) + mm(h_other, other_ref[:, HID:])
    mean = jnp.mean(applied * applied, axis=1, keepdims=True)
    normed = applied * lax.rsqrt(mean + 1e-6) * gain_ref[...]
    out_ref[...] = (att_ref[...] + normed).astype(BF)


def apply(piece, pos, query, own, other, attended, gain):
    return pl.pallas_call(
        apply_kernel,
        grid=(1,),
        in_specs=[
            SMEM,
            pl.BlockSpec((QB, DH), lambda i: (piece, 0)),
            WHOLE,
            WHOLE,
            WHOLE,
            WHOLE,
        ],
        out_specs=pl.BlockSpec((QB, DH), lambda i: (0, 0)),
        out_shape=sds((QB, DH), BF),
        compiler_params=params(),
        name=f"apply_{piece}",
    )(pos, query, own, other, attended, gain)


def output_kernel(*refs):
    parts, weights, out = refs[:HS], refs[HS : 2 * HS], refs[-1]
    total = mm(parts[0][...], weights[0][...])
    for part, weight in zip(parts[1:], weights[1:]):
        total = total + mm(part[...], weight[...])
    out[...] = total.astype(BF)


def output(piece, parts, weights, buffer):
    extra = [] if buffer is None else [buffer]
    return pl.pallas_call(
        output_kernel,
        grid=(1,),
        in_specs=[WHOLE] * (2 * HS) + [DEP] * len(extra),
        out_specs=pl.BlockSpec((QB, DH), lambda i: (piece, 0)),
        out_shape=sds((TOK, DH), BF),
        input_output_aliases={2 * HS: 0} if extra else {},
        compiler_params=params(),
        name=f"output_{piece}",
    )(*parts, *weights, *extra)


def body(
    tokens,
    qkv_weight,
    rate_weight,
    first_fast,
    gate_fast,
    second_fast,
    fast_gain,
    out_weight,
    frame_lengths,
):
    mine = lax.axis_index("tok")
    head = lax.axis_index("head")
    x, z, core = mine // (ZS * CS), mine // CS % ZS, mine % CS
    pos = jnp.stack([x, z, core]).astype(I32)
    send = lambda value, pairs: lax.ppermute(value, "tok", pairs)

    kv, give, keep = front(
        pos, tokens, qkv_weight, rate_weight, first_fast, gate_fast, second_fast
    )
    got = send(give, SWAP_C)
    up = [(i, i + 1) for i in range(SHARDS - 1)]
    before = send(kv, up)
    after = send(kv, [(j, i) for i, j in up])

    order = jnp.arange(frame_lengths.shape[0], dtype=I32)
    ends = jnp.sum(
        jnp.where(order[:, None] <= order[None, :], frame_lengths[:, None], 0), axis=0
    )
    places = mine * TOK + jnp.arange(TOK, dtype=I32)
    passed = ends[None, :] <= places[:, None]
    begin = jnp.max(jnp.where(passed, ends[None, :], 0), axis=1)
    end = jnp.min(jnp.where(passed, TOKENS, ends[None, :]), axis=1)
    shift = (mine - 1) * TOK
    row_bounds = jnp.stack([begin - shift, end - shift], axis=1)
    bounds = jnp.stack(
        [row_bounds[::QB, 0], row_bounds[QB - 1 :: QB, 1]], axis=1
    ).reshape(-1)

    weights = []
    for d in range(HS):
        cols = lax.dynamic_slice_in_dim(out_weight, (head + d) % HS * DH, DH, 1)
        weights.append(lax.ppermute(cols, "head", shift_h(d)) if d else cols)

    row = jnp.minimum(x * XROWS + z * ZROWS, DH - ZROWS)
    pick = lambda w, at: lax.dynamic_slice_in_dim(w[0], at, ZROWS, 0)
    old = jnp.concatenate(
        [
            jnp.where(core == 0, pick(first_fast, row), pick(gate_fast, row)),
            pick(second_fast, core * DH + row),
        ],
        axis=1,
    ).astype(F32)

    own, *gives = rs_x(pos, keep, got)
    got = [send(g, shift_x(d + 1)) for d, g in enumerate(gives)]
    query = project(tokens, qkv_weight, own)
    att = functools.partial(
        lambda p, dep: attend(p, bounds, row_bounds, query, before, kv, after, dep)
    )

    own, *gives = rs_z(pos, own, got, [query])
    got = [send(g, shift_z(d + 1, to_owner=True)) for d, g in enumerate(gives)]
    att0 = att(0, own)

    fresh = renorm(old, own, got, [att0])
    got = [send(fresh, shift_z(d, from_owner=True)) for d in range(1, ZS)]
    att1 = att(1, fresh)

    block = ag_z(pos, [fresh, *got], [att1])
    got = [send(block, shift_x(d)) for d in range(1, XS)]
    att2 = att(2, block)
    att3 = att(3, block)

    half = ag_x(pos, [block, *got], [att2, att3])
    other = send(half, SWAP_C)

    gain = fast_gain[None, :]
    result = None
    mixed = [
        apply(p, pos, query, half, other, a, gain)
        for p, a in enumerate((att0, att1, att2, att3))
    ]
    for p, part in enumerate(mixed):
        parts = [part] + [
            lax.ppermute(part, "head", shift_h(d)) for d in range(1, HS)
        ]
        result = output(p, parts, weights, result)
    return result


def solution(mesh):
    placed = (
        P("tok", None),
        P(None, "head"),
        P(None, "head"),
        P("head", None, None),
        P("head", None, None),
        P("head", None, None),
        P("head"),
        P("head", None),
        P(),
    )
    return jax.shard_map(
        body, mesh=mesh, in_specs=placed, out_specs=P("tok", "head"), check_vma=False
    )
```

```python
import functools
import math

import jax
import jax.numpy as jnp
from jax import lax
from jax.experimental import pallas as pl
from jax.experimental.pallas import tpu as pltpu
from jax.sharding import PartitionSpec as P

DH = 384
HID = 768
TOK = 1024
XS, ZS, CS, HS = 4, 8, 2, 4
SHARDS = XS * ZS * CS
TOKENS = TOK * SHARDS
SLOTS = XS * ZS
ZROWS = 16
WIDE = HID + DH
KB = 256
QB = 256
BF, F32, I32 = jnp.bfloat16, jnp.float32, jnp.int32
NT = (((1,), (1,)), ((), ()))
VM = 56 * 1024 * 1024

SMEM = pl.BlockSpec(memory_space=pltpu.SMEM)
WHOLE = pl.BlockSpec(memory_space=pltpu.VMEM)
DEP = pl.BlockSpec(memory_space=pl.ANY)


def params():
    return pltpu.CompilerParams(vmem_limit_bytes=VM)


def mm(a, b):
    return jnp.dot(a, b, preferred_element_type=F32)


def sds(shape, dtype):
    return jax.ShapeDtypeStruct(shape, dtype)


SWAP_C = [(t, t ^ 1) for t in range(SHARDS)]
CHIPS = [[chip * CS + c for chip in range(SHARDS // CS)] for c in range(CS)]


def shift_h(d):
    return [(h, (h + d) % HS) for h in range(HS)]


def full(shape):
    return pl.BlockSpec(shape, lambda i: (0,) * len(shape))


def front_kernel(
    pos_ref, t_ref, wk_ref, wv_ref, wr_ref, w1_ref, w3_ref, w2_ref,
    kv_ref, send_ref, keep_ref, acc1, acc3, acc2,
):
    step = pl.program_id(0)

    @pl.when(step == 0)
    def _():
        acc1[...] = jnp.zeros_like(acc1)
        acc3[...] = jnp.zeros_like(acc3)
        acc2[...] = jnp.zeros_like(acc2)

    t = t_ref[...]
    k = mm(t, wk_ref[...]).astype(BF)
    v = mm(t, wv_ref[...]).astype(BF)
    kv_ref[:, :DH] = k
    kv_ref[:, DH:] = v
    raw = mm(t, wr_ref[...])
    rates = (0.25 / math.sqrt(TOKENS)) * (
        jnp.maximum(raw, 0.0) + jnp.log1p(jnp.exp(-jnp.abs(raw)))
    )
    a = mm(k, w1_ref[0])
    b = mm(k, w3_ref[0])
    back = lax.dot_general(v, w2_ref[0], NT, preferred_element_type=F32)
    sig = jax.nn.sigmoid(a)
    act = a * sig
    z = (act * b).astype(BF)
    e1 = (rates[:, 0:1] * back * b * sig * (1.0 + a * (1.0 - sig))).astype(BF)
    e3 = (rates[:, 1:2] * back * act).astype(BF)
    e2 = (rates[:, 2:3] * v.astype(F32)).astype(BF)
    k_t = k.T
    acc1[...] += mm(k_t, e1)
    acc3[...] += mm(k_t, e3)
    acc2[...] += mm(e2.T, z)

    @pl.when(step == pl.num_programs(0) - 1)
    def _():
        core = pos_ref[2]
        low = acc2[:, :DH].T
        high = acc2[:, DH:].T

        @pl.when(core == 0)
        def _():
            keep_ref[:, :HID] = acc1[...]
            keep_ref[:, HID:] = low
            send_ref[:, :HID] = acc3[...].astype(BF)
            send_ref[:, HID:] = high.astype(BF)

        @pl.when(core == 1)
        def _():
            keep_ref[:, :HID] = acc3[...]
            keep_ref[:, HID:] = high
            send_ref[:, :HID] = acc1[...].astype(BF)
            send_ref[:, HID:] = low.astype(BF)


def front(pos, tokens, qkv_weight, rate_weight, first_fast, gate_fast, second_fast):
    rows, wide = tokens.shape
    block = 256
    fixed3 = lambda i: (0, 0, 0)
    return pl.pallas_call(
        front_kernel,
        grid=(rows // block,),
        in_specs=[
            SMEM,
            pl.BlockSpec((block, wide), lambda i: (i, 0)),
            pl.BlockSpec((wide, DH), lambda i: (0, 1)),
            pl.BlockSpec((wide, DH), lambda i: (0, 2)),
            pl.BlockSpec((wide, 3), lambda i: (0, 0)),
            pl.BlockSpec((1, DH, HID), fixed3),
            pl.BlockSpec((1, DH, HID), fixed3),
            pl.BlockSpec((1, HID, DH), fixed3),
        ],
        out_specs=[
            pl.BlockSpec((block, 2 * DH), lambda i: (i, 0)),
            pl.BlockSpec((DH, WIDE), lambda i: (0, 0)),
            pl.BlockSpec((DH, WIDE), lambda i: (0, 0)),
        ],
        out_shape=[sds((rows, 2 * DH), BF), sds((DH, WIDE), BF), sds((DH, WIDE), F32)],
        scratch_shapes=[pltpu.VMEM((DH, HID), F32)] * 3,
        compiler_params=params(),
        name="front",
    )(pos, tokens, qkv_weight, qkv_weight, rate_weight, first_fast, gate_fast, second_fast)


def join_kernel(keep_ref, got_ref, out_ref):
    out_ref[:DH, :] = (keep_ref[...] + got_ref[...].astype(F32)).astype(BF)
    out_ref[DH:, :] = jnp.zeros((SLOTS * ZROWS - DH, WIDE), BF)


def join(keep, got):
    return pl.pallas_call(
        join_kernel,
        grid=(1,),
        in_specs=[full((DH, WIDE)), full((DH, WIDE))],
        out_specs=full((SLOTS * ZROWS, WIDE)),
        out_shape=sds((SLOTS * ZROWS, WIDE), BF),
        compiler_params=params(),
        name="join",
    )(keep, got)


def renorm_kernel(old_ref, got_ref, *rest):
    out = rest[-1]
    update = got_ref[0].astype(F32)
    for s in range(1, SLOTS):
        update = update + got_ref[s].astype(F32)
    old = old_ref[...]
    fresh = old + update
    for cols in (slice(0, HID), slice(HID, WIDE)):
        w, f = old[:, cols], fresh[:, cols]
        w_sq = jnp.sum(w * w, axis=1, keepdims=True)
        f_sq = jnp.sum(f * f, axis=1, keepdims=True)
        new = (f * (jnp.sqrt(w_sq) / jnp.sqrt(f_sq + 1e-6))).astype(BF)
        for s in range(SLOTS):
            out[s, :, cols] = new


def renorm(old, got, deps):
    shape = (SLOTS, ZROWS, WIDE)
    return pl.pallas_call(
        renorm_kernel,
        grid=(1,),
        in_specs=[full((ZROWS, WIDE)), full(shape)] + [DEP] * len(deps),
        out_specs=full(shape),
        out_shape=sds(shape, BF),
        compiler_params=params(),
        name="renorm",
    )(old, got, *deps)


def hold_kernel(value_ref, dep_ref, out_ref):
    pass


def hold(value, dep):
    return pl.pallas_call(
        hold_kernel,
        in_specs=[DEP, DEP],
        out_specs=DEP,
        out_shape=sds(value.shape, value.dtype),
        input_output_aliases={0: 0},
        compiler_params=params(),
        name="hold",
    )(value, dep)


def project_kernel(t_ref, w_ref, dep_ref, q_ref):
    q_ref[...] = mm(t_ref[...], w_ref[...]).astype(BF)


def project(tokens, qkv_weight, dep):
    rows, wide = tokens.shape
    block = 256
    return pl.pallas_call(
        project_kernel,
        grid=(rows // block,),
        in_specs=[
            pl.BlockSpec((block, wide), lambda i: (i, 0)),
            pl.BlockSpec((wide, DH), lambda i: (0, 0)),
            DEP,
        ],
        out_specs=pl.BlockSpec((block, DH), lambda i: (i, 0)),
        out_shape=sds((rows, DH), BF),
        compiler_params=params(),
        name="project",
    )(tokens, qkv_weight, dep)


def attend_kernel(start, bounds_ref, rows_ref, q_ref, before, mine, after, dep_ref, out_ref, s_ref):
    piece = pl.program_id(0) + start
    low, high = bounds_ref[2 * piece], bounds_ref[2 * piece + 1]
    first = lax.div(low, KB)
    last = lax.div(high + KB - 1, KB)
    q = q_ref[...]
    begin, end = rows_ref[:, 0:1], rows_ref[:, 1:2]
    per = TOK // KB
    scale = 1.0 / math.sqrt(DH)

    def segments(step, carry):
        for s, ref in enumerate((before, mine, after)):
            lo = jnp.clip(first, s * per, (s + 1) * per)
            hi = jnp.clip(last, s * per, (s + 1) * per)
            carry = lax.fori_loop(lo, hi, functools.partial(step, s, ref), carry)
        return carry

    def scores(s, ref, kb, top):
        k = ref[pl.ds(pl.multiple_of((kb - s * per) * KB, KB), KB), :DH]
        sc = lax.dot_general(q, k, NT, preferred_element_type=F32) * scale
        col = lax.broadcasted_iota(I32, (QB, KB), 1) + kb * KB
        sc = jnp.where((col >= begin) & (col < end), sc, -1e30)
        s_ref[kb] = sc
        return jnp.maximum(top, jnp.max(sc, axis=1, keepdims=True))

    top = segments(scores, jnp.full((QB, 1), -1e30, F32))

    def weigh(kb, total):
        w = jnp.exp(s_ref[kb] - top)
        s_ref[kb] = w
        return total + jnp.sum(w, axis=1, keepdims=True)

    total = lax.fori_loop(first, last, weigh, jnp.zeros((QB, 1), F32))
    inverse = 1.0 / total
    out_ref[...] = jnp.zeros_like(out_ref)

    def gather(s, ref, kb, carry):
        v = ref[pl.ds(pl.multiple_of((kb - s * per) * KB, KB), KB), DH:]
        probs = (s_ref[kb] * inverse).astype(BF)
        out_ref[...] += mm(probs, v)
        return carry

    segments(gather, 0)


def attend(start, count, bounds, row_bounds, query, before, mine, after, dep):
    whole = full((TOK, 2 * DH))
    return pl.pallas_call(
        functools.partial(attend_kernel, start),
        grid=(count,),
        in_specs=[
            SMEM,
            pl.BlockSpec((QB, 2), lambda i: (i + start, 0)),
            pl.BlockSpec((QB, DH), lambda i: (i + start, 0)),
            whole,
            whole,
            whole,
            DEP,
        ],
        out_specs=pl.BlockSpec((QB, DH), lambda i: (i, 0)),
        out_shape=sds((count * QB, DH), F32),
        scratch_shapes=[pltpu.VMEM((3 * TOK // KB, QB, KB), F32)],
        compiler_params=params(),
        name=f"attend_{start}",
    )(bounds, row_bounds, query, before, mine, after, dep)


def apply_kernel(pos_ref, q_ref, own_ref, other_ref, att_ref, gain_ref, dep_ref, out_ref):
    core = pos_ref[2]
    q = q_ref[...]
    mine = mm(q, own_ref[:, :HID])
    theirs = mm(q, other_ref[:, :HID])
    even = core == 0
    a = jnp.where(even, mine, theirs)
    b = jnp.where(even, theirs, mine)
    hidden = (a * jax.nn.sigmoid(a) * b).astype(BF)
    h0, h1 = hidden[:, :DH], hidden[:, DH:]
    h_own = jnp.where(even, h0, h1)
    h_other = jnp.where(even, h1, h0)
    applied = mm(h_own, own_ref[:, HID:]) + mm(h_other, other_ref[:, HID:])
    mean = jnp.mean(applied * applied, axis=1, keepdims=True)
    normed = applied * lax.rsqrt(mean + 1e-6) * gain_ref[...]
    out_ref[...] = (att_ref[...] + normed).astype(BF)


def apply(start, count, pos, query, own, other, attended, att_start, gain, dep):
    weight = full((DH, WIDE))
    return pl.pallas_call(
        apply_kernel,
        grid=(count,),
        in_specs=[
            SMEM,
            pl.BlockSpec((QB, DH), lambda i: (i + start, 0)),
            weight,
            weight,
            pl.BlockSpec((QB, DH), lambda i: (i + att_start, 0)),
            full((1, DH)),
            DEP,
        ],
        out_specs=pl.BlockSpec((QB, DH), lambda i: (i, 0)),
        out_shape=sds((count * QB, DH), BF),
        compiler_params=params(),
        name=f"apply_{start}",
    )(pos, query, own, other, attended, gain, dep)


def output_kernel(*refs):
    parts, weights, out = refs[:HS], refs[HS : 2 * HS], refs[-1]
    total = mm(parts[0][...], weights[0][...])
    for part, weight in zip(parts[1:], weights[1:]):
        total = total + mm(part[...], weight[...])
    out[...] = total.astype(BF)


def output(start, count, parts, weights, buffer):
    extra = [] if buffer is None else [buffer]
    return pl.pallas_call(
        output_kernel,
        grid=(count,),
        in_specs=[pl.BlockSpec((QB, DH), lambda i: (i, 0))] * HS
        + [full((DH, DH))] * HS
        + [DEP] * len(extra),
        out_specs=pl.BlockSpec((QB, DH), lambda i: (i + start, 0)),
        out_shape=sds((TOK, DH), BF),
        input_output_aliases={2 * HS: 0} if extra else {},
        compiler_params=params(),
        name=f"output_{start}",
    )(*parts, *weights, *extra)


def body(
    tokens,
    qkv_weight,
    rate_weight,
    first_fast,
    gate_fast,
    second_fast,
    fast_gain,
    out_weight,
    frame_lengths,
):
    mine = lax.axis_index("tok")
    head = lax.axis_index("head")
    x, z, core = mine // (ZS * CS), mine // CS % ZS, mine % CS
    pos = jnp.stack([x, z, core]).astype(I32)
    send = lambda value, pairs: lax.ppermute(value, "tok", pairs)

    kv, give, keep = front(
        pos, tokens, qkv_weight, rate_weight, first_fast, gate_fast, second_fast
    )
    got = send(give, SWAP_C)
    up = [(i, i + 1) for i in range(SHARDS - 1)]
    before = send(kv, up)
    after = send(kv, [(j, i) for i, j in up])

    order = jnp.arange(frame_lengths.shape[0], dtype=I32)
    ends = jnp.sum(
        jnp.where(order[:, None] <= order[None, :], frame_lengths[:, None], 0), axis=0
    )
    places = mine * TOK + jnp.arange(TOK, dtype=I32)
    passed = ends[None, :] <= places[:, None]
    begin = jnp.max(jnp.where(passed, ends[None, :], 0), axis=1)
    end = jnp.min(jnp.where(passed, TOKENS, ends[None, :]), axis=1)
    shift = (mine - 1) * TOK
    row_bounds = jnp.stack([begin - shift, end - shift], axis=1)
    bounds = jnp.stack(
        [row_bounds[::QB, 0], row_bounds[QB - 1 :: QB, 1]], axis=1
    ).reshape(-1)

    weights = []
    for d in range(HS):
        cols = lax.dynamic_slice_in_dim(out_weight, (head + d) % HS * DH, DH, 1)
        weights.append(lax.ppermute(cols, "head", shift_h(d)) if d else cols)

    row = jnp.minimum((mine // CS) * ZROWS, DH - ZROWS)
    pick = lambda w, at: lax.dynamic_slice_in_dim(w[0], at, ZROWS, 0)
    old = jnp.concatenate(
        [
            jnp.where(core == 0, pick(first_fast, row), pick(gate_fast, row)),
            pick(second_fast, core * DH + row),
        ],
        axis=1,
    ).astype(F32)

    def exchange(blocks):
        return lax.all_to_all(blocks, "tok", 0, 0, axis_index_groups=CHIPS)

    total = join(keep, got)
    got = exchange(total.reshape(SLOTS, ZROWS, WIDE))
    query = project(tokens, qkv_weight, total)
    att_low = attend(0, 2, bounds, row_bounds, query, before, kv, after, query)
    fresh = renorm(old, got, [att_low, *weights])
    got = exchange(fresh)
    att_high = attend(2, 2, bounds, row_bounds, query, before, kv, after, fresh)
    half = hold(got, att_high).reshape(SLOTS * ZROWS, WIDE)
    other = send(half, SWAP_C)

    gain = fast_gain[None, :]
    result = None
    mixed = []
    dep = att_high
    for start, count, attended, at in ((0, 1, att_low, 0), (1, 1, att_low, 1), (2, 2, att_high, 0)):
        dep = apply(start, count, pos, query, half, other, attended, at, gain, dep)
        mixed.append((start, count, dep))
    for start, count, part in mixed:
        parts = [part] + [
            lax.ppermute(part, "head", shift_h(d)) for d in range(1, HS)
        ]
        result = output(start, count, parts, weights, result)
    return result


def solution(mesh):
    placed = (
        P("tok", None),
        P(None, "head"),
        P(None, "head"),
        P("head", None, None),
        P("head", None, None),
        P("head", None, None),
        P("head"),
        P("head", None),
        P(),
    )
    return jax.shard_map(
        body, mesh=mesh, in_specs=placed, out_specs=P("tok", "head"), check_vma=False
    )
```

```python
import functools
import math

import jax
import jax.numpy as jnp
from jax import lax
from jax.experimental import pallas as pl
from jax.experimental.pallas import tpu as pltpu
from jax.sharding import PartitionSpec as P

DH = 384
HID = 768
TOK = 1024
XS, ZS, CS, HS = 4, 8, 2, 4
SHARDS = XS * ZS * CS
TOKENS = TOK * SHARDS
SLOTS = XS * ZS
PACK = 2 * HID + DH
WIDE = HID + DH
KB = 256
QB = 256
BF, F32, I32 = jnp.bfloat16, jnp.float32, jnp.int32
NT = (((1,), (1,)), ((), ()))
VM = 56 * 1024 * 1024

SMEM = pl.BlockSpec(memory_space=pltpu.SMEM)
WHOLE = pl.BlockSpec(memory_space=pltpu.VMEM)
DEP = pl.BlockSpec(memory_space=pl.ANY)


def params():
    return pltpu.CompilerParams(vmem_limit_bytes=VM)


def mm(a, b):
    return jnp.dot(a, b, preferred_element_type=F32)


def sds(shape, dtype):
    return jax.ShapeDtypeStruct(shape, dtype)


SWAP_C = [(t, t ^ 1) for t in range(SHARDS)]
CHIPS = [[chip * CS + c for chip in range(SHARDS // CS)] for c in range(CS)]


def shift_h(d):
    return [(h, (h + d) % HS) for h in range(HS)]


def full(shape):
    return pl.BlockSpec(shape, lambda i: (0,) * len(shape))


def keys_kernel(t_ref, wk_ref, wv_ref, wr_ref, kv_ref, rates_ref):
    t = t_ref[...]
    kv_ref[:, :DH] = mm(t, wk_ref[...]).astype(BF)
    kv_ref[:, DH:] = mm(t, wv_ref[...]).astype(BF)
    raw = lax.dot_general(t, wr_ref[...], NT, preferred_element_type=F32)
    rates_ref[...] = (0.25 / math.sqrt(TOKENS)) * (
        jnp.maximum(raw, 0.0) + jnp.log1p(jnp.exp(-jnp.abs(raw)))
    )


def keys(tokens, qkv_weight, rate_weight):
    rows, wide = tokens.shape
    block = 256
    return pl.pallas_call(
        keys_kernel,
        grid=(rows // block,),
        in_specs=[
            pl.BlockSpec((block, wide), lambda i: (i, 0)),
            pl.BlockSpec((wide, DH), lambda i: (0, 1)),
            pl.BlockSpec((wide, DH), lambda i: (0, 2)),
            full((3, wide)),
        ],
        out_specs=[
            pl.BlockSpec((block, 2 * DH), lambda i: (i, 0)),
            pl.BlockSpec((block, 3), lambda i: (i, 0)),
        ],
        out_shape=[sds((rows, 2 * DH), BF), sds((rows, 3), F32)],
        compiler_params=params(),
        name="keys",
    )(tokens, qkv_weight, qkv_weight, rate_weight.T)


def update_kernel(pos_ref, kv_ref, r_ref, w1_ref, w3_ref, w2_ref, send_ref, keep_ref, second):
    even = pos_ref[0] == 0
    k, v = kv_ref[:, :DH], kv_ref[:, DH:]
    r = r_ref[...]
    r1, r3 = r[:, 0:1], r[:, 1:2]
    k_t = k.T
    e2_t = (r[:, 2:3] * v.astype(F32)).astype(BF).T
    chunk = 256
    for j in range(HID // chunk):
        cols = slice(j * chunk, (j + 1) * chunk)
        a = mm(k, w1_ref[0, :, cols])
        b = mm(k, w3_ref[0, :, cols])
        back = lax.dot_general(v, w2_ref[0, cols, :], NT, preferred_element_type=F32)
        sig = jax.nn.sigmoid(a)
        act = a * sig
        z = (act * b).astype(BF)
        e1 = (r1 * back * b * (sig * (1.0 + a * (1.0 - sig)))).astype(BF)
        e3 = (r3 * back * act).astype(BF)
        first = mm(k_t, e1)
        gate = mm(k_t, e3)
        second[cols, :] = mm(e2_t, z).T
        keep_ref[:, cols] = jnp.where(even, first, gate)
        send_ref[:, cols] = jnp.where(even, gate, first).astype(BF)
    low, high = second[:DH, :], second[DH:, :]
    keep_ref[:, HID:] = jnp.where(even, low, high)
    send_ref[:, HID:] = jnp.where(even, high, low).astype(BF)


def update(pos, kv, rates, first_fast, gate_fast, second_fast):
    return pl.pallas_call(
        update_kernel,
        grid=(1,),
        in_specs=[
            SMEM,
            full(kv.shape),
            full(rates.shape),
            full((1, DH, HID)),
            full((1, DH, HID)),
            full((1, HID, DH)),
        ],
        out_specs=[full((DH, WIDE)), full((DH, WIDE))],
        out_shape=[sds((DH, WIDE), BF), sds((DH, WIDE), F32)],
        scratch_shapes=[pltpu.VMEM((HID, DH), F32)],
        compiler_params=params(),
        name="update",
    )(pos, kv, rates, first_fast, gate_fast, second_fast)


def places():
    for pair in range(SLOTS // 2):
        top, mid, low = (slice(24 * pair + 8 * i, 24 * pair + 8 * i + 8) for i in range(3))
        yield 2 * pair, slice(0, HID), top, slice(0, HID)
        yield 2 * pair, slice(HID, 2 * HID), mid, slice(0, HID)
        yield 2 * pair, slice(2 * HID, PACK), top, slice(HID, WIDE)
        yield 2 * pair + 1, slice(0, HID), low, slice(0, HID)
        yield 2 * pair + 1, slice(HID, WIDE), mid, slice(HID, WIDE)
        yield 2 * pair + 1, slice(WIDE, 2 * HID), low, slice(HID, WIDE)


def join_kernel(keep_ref, got_ref, before_ref, after_ref, out_ref, total):
    total[...] = keep_ref[...] + got_ref[...].astype(F32)
    for slot, to, rows, cols in places():
        out_ref[slot, :, to] = total[rows, cols].astype(BF)
    for slot in range(1, SLOTS, 2):
        out_ref[slot, :, 2 * HID :] = jnp.zeros((8, DH), BF)


def join(keep, got, before, after):
    return pl.pallas_call(
        join_kernel,
        grid=(1,),
        in_specs=[full((DH, WIDE)), full((DH, WIDE)), DEP, DEP],
        out_specs=full((SLOTS, 8, PACK)),
        out_shape=sds((SLOTS, 8, PACK), BF),
        scratch_shapes=[pltpu.VMEM((DH, WIDE), F32)],
        compiler_params=params(),
        name="join",
    )(keep, got, before, after)


def renorm_kernel(pos_ref, old_ref, got_ref, *rest):
    out = rest[-1]
    odd = pos_ref[1] == 1
    update = got_ref[0].astype(F32)
    for s in range(1, SLOTS):
        update = update + got_ref[s].astype(F32)
    old = old_ref[...]
    fresh = old + update

    def squares(value):
        u = [
            jnp.sum(jnp.square(value[:, i * DH : (i + 1) * DH]), axis=1, keepdims=True)
            for i in range(PACK // DH)
        ]
        wide = u[2] + u[3]
        return (
            (0, HID, u[0] + u[1]),
            (HID, WIDE, jnp.where(odd, u[2], wide)),
            (WIDE, 2 * HID, jnp.where(odd, u[3], wide)),
            (2 * HID, PACK, u[4]),
        )

    for (lo, hi, w_sq), (_, _, f_sq) in zip(squares(old), squares(fresh)):
        new = (fresh[:, lo:hi] * (jnp.sqrt(w_sq) / jnp.sqrt(f_sq + 1e-6))).astype(BF)
        for s in range(SLOTS):
            out[s, :, lo:hi] = new


def renorm(pos, old, got, deps):
    shape = (SLOTS, 8, PACK)
    return pl.pallas_call(
        renorm_kernel,
        grid=(1,),
        in_specs=[SMEM, full((8, PACK)), full(shape)] + [DEP] * len(deps),
        out_specs=full(shape),
        out_shape=sds(shape, BF),
        compiler_params=params(),
        name="renorm",
    )(pos, old, got, *deps)


def unpack_kernel(got_ref, *rest):
    out, total = rest[-2:]
    for slot, to, rows, cols in places():
        total[rows, cols] = got_ref[slot, :, to].astype(F32)
    out[...] = total[...].astype(BF)


def unpack(got, deps):
    return pl.pallas_call(
        unpack_kernel,
        grid=(1,),
        in_specs=[full((SLOTS, 8, PACK))] + [DEP] * len(deps),
        out_specs=full((DH, WIDE)),
        out_shape=sds((DH, WIDE), BF),
        scratch_shapes=[pltpu.VMEM((DH, WIDE), F32)],
        compiler_params=params(),
        name="unpack",
    )(got, *deps)


def project_kernel(t_ref, w_ref, dep_ref, q_ref):
    q_ref[...] = mm(t_ref[...], w_ref[...]).astype(BF)


def project(tokens, qkv_weight, dep):
    rows, wide = tokens.shape
    block = 256
    return pl.pallas_call(
        project_kernel,
        grid=(rows // block,),
        in_specs=[
            pl.BlockSpec((block, wide), lambda i: (i, 0)),
            pl.BlockSpec((wide, DH), lambda i: (0, 0)),
            DEP,
        ],
        out_specs=pl.BlockSpec((block, DH), lambda i: (i, 0)),
        out_shape=sds((rows, DH), BF),
        compiler_params=params(),
        name="project",
    )(tokens, qkv_weight, dep)


def attend_kernel(start, bounds_ref, rows_ref, q_ref, before, mine, after, dep_ref, out_ref, s_ref):
    piece = pl.program_id(0) + start
    low, high = bounds_ref[2 * piece], bounds_ref[2 * piece + 1]
    first = lax.div(low, KB)
    last = lax.div(high + KB - 1, KB)
    q = q_ref[...]
    begin, end = rows_ref[:, 0:1], rows_ref[:, 1:2]
    per = TOK // KB
    scale = 1.0 / math.sqrt(DH)

    def segments(step, carry):
        for s, ref in enumerate((before, mine, after)):
            lo = jnp.clip(first, s * per, (s + 1) * per)
            hi = jnp.clip(last, s * per, (s + 1) * per)
            carry = lax.fori_loop(lo, hi, functools.partial(step, s, ref), carry)
        return carry

    def scores(s, ref, kb, top):
        k = ref[pl.ds(pl.multiple_of((kb - s * per) * KB, KB), KB), :DH]
        sc = lax.dot_general(q, k, NT, preferred_element_type=F32) * scale
        col = lax.broadcasted_iota(I32, (QB, KB), 1) + kb * KB
        sc = jnp.where((col >= begin) & (col < end), sc, -1e30)
        s_ref[kb] = sc
        return jnp.maximum(top, jnp.max(sc, axis=1, keepdims=True))

    top = segments(scores, jnp.full((QB, 1), -1e30, F32))

    def weigh(kb, total):
        w = jnp.exp(s_ref[kb] - top)
        s_ref[kb] = w
        return total + jnp.sum(w, axis=1, keepdims=True)

    total = lax.fori_loop(first, last, weigh, jnp.zeros((QB, 1), F32))
    inverse = 1.0 / total
    out_ref[...] = jnp.zeros_like(out_ref)

    def gather(s, ref, kb, carry):
        v = ref[pl.ds(pl.multiple_of((kb - s * per) * KB, KB), KB), DH:]
        probs = (s_ref[kb] * inverse).astype(BF)
        out_ref[...] += mm(probs, v)
        return carry

    segments(gather, 0)


def attend(start, count, bounds, row_bounds, query, before, mine, after, dep):
    whole = full((TOK, 2 * DH))
    return pl.pallas_call(
        functools.partial(attend_kernel, start),
        grid=(count,),
        in_specs=[
            SMEM,
            pl.BlockSpec((QB, 2), lambda i: (i + start, 0)),
            pl.BlockSpec((QB, DH), lambda i: (i + start, 0)),
            whole,
            whole,
            whole,
            DEP,
        ],
        out_specs=pl.BlockSpec((QB, DH), lambda i: (i, 0)),
        out_shape=sds((count * QB, DH), F32),
        scratch_shapes=[pltpu.VMEM((3 * TOK // KB, QB, KB), F32)],
        compiler_params=params(),
        name=f"attend_{start}",
    )(bounds, row_bounds, query, before, mine, after, dep)


def apply_kernel(pos_ref, q_ref, own_ref, other_ref, att_ref, gain_ref, dep_ref, out_ref):
    core = pos_ref[0]
    q = q_ref[...]
    mine = mm(q, own_ref[:, :HID])
    theirs = mm(q, other_ref[:, :HID])
    even = core == 0
    a = jnp.where(even, mine, theirs)
    b = jnp.where(even, theirs, mine)
    hidden = (a * jax.nn.sigmoid(a) * b).astype(BF)
    h0, h1 = hidden[:, :DH], hidden[:, DH:]
    h_own = jnp.where(even, h0, h1)
    h_other = jnp.where(even, h1, h0)
    applied = mm(h_own, own_ref[:, HID:]) + mm(h_other, other_ref[:, HID:])
    mean = jnp.mean(applied * applied, axis=1, keepdims=True)
    normed = applied * lax.rsqrt(mean + 1e-6) * gain_ref[...]
    out_ref[...] = (att_ref[...] + normed).astype(BF)


def apply(start, count, pos, query, own, other, attended, att_start, gain, dep):
    weight = full((DH, WIDE))
    return pl.pallas_call(
        apply_kernel,
        grid=(count,),
        in_specs=[
            SMEM,
            pl.BlockSpec((QB, DH), lambda i: (i + start, 0)),
            weight,
            weight,
            pl.BlockSpec((QB, DH), lambda i: (i + att_start, 0)),
            full((1, DH)),
            DEP,
        ],
        out_specs=pl.BlockSpec((QB, DH), lambda i: (i, 0)),
        out_shape=sds((count * QB, DH), BF),
        compiler_params=params(),
        name=f"apply_{start}",
    )(pos, query, own, other, attended, gain, dep)


def output_kernel(*refs):
    parts, weights, out = refs[:HS], refs[HS : 2 * HS], refs[-1]
    total = mm(parts[0][...], weights[0][...])
    for part, weight in zip(parts[1:], weights[1:]):
        total = total + mm(part[...], weight[...])
    out[...] = total.astype(BF)


def output(start, count, parts, weights, buffer):
    extra = [] if buffer is None else [buffer]
    return pl.pallas_call(
        output_kernel,
        grid=(count,),
        in_specs=[pl.BlockSpec((QB, DH), lambda i: (i, 0))] * HS
        + [full((DH, DH))] * HS
        + [DEP] * len(extra),
        out_specs=pl.BlockSpec((QB, DH), lambda i: (i + start, 0)),
        out_shape=sds((TOK, DH), BF),
        input_output_aliases={2 * HS: 0} if extra else {},
        compiler_params=params(),
        name=f"output_{start}",
    )(*parts, *weights, *extra)


def body(
    tokens,
    qkv_weight,
    rate_weight,
    first_fast,
    gate_fast,
    second_fast,
    fast_gain,
    out_weight,
    frame_lengths,
):
    mine = lax.axis_index("tok")
    head = lax.axis_index("head")
    chip, core = mine // CS, mine % CS
    odd = chip % 2
    send = lambda value, pairs: lax.ppermute(value, "tok", pairs)

    kv, rates = keys(tokens, qkv_weight, rate_weight)
    up = [(i, i + 1) for i in range(SHARDS - 1)]
    before = send(kv, up)
    after = send(kv, [(j, i) for i, j in up])
    pos = jnp.stack([core, odd]).astype(I32)
    give, keep = update(pos, kv, rates, first_fast, gate_fast, second_fast)
    got = send(give, SWAP_C)

    order = jnp.arange(frame_lengths.shape[0], dtype=I32)
    ends = jnp.sum(
        jnp.where(order[:, None] <= order[None, :], frame_lengths[:, None], 0), axis=0
    )
    places = mine * TOK + jnp.arange(TOK, dtype=I32)
    passed = ends[None, :] <= places[:, None]
    begin = jnp.max(jnp.where(passed, ends[None, :], 0), axis=1)
    end = jnp.min(jnp.where(passed, TOKENS, ends[None, :]), axis=1)
    shift = (mine - 1) * TOK
    row_bounds = jnp.stack([begin - shift, end - shift], axis=1)
    bounds = jnp.stack(
        [row_bounds[::QB, 0], row_bounds[QB - 1 :: QB, 1]], axis=1
    ).reshape(-1)

    weights = []
    for d in range(HS):
        cols = lax.dynamic_slice_in_dim(out_weight, (head + d) % HS * DH, DH, 1)
        weights.append(lax.ppermute(cols, "head", shift_h(d)) if d else cols)

    base = chip // 2 * 24
    wide = lambda at: jnp.where(
        core == 0,
        lax.dynamic_slice_in_dim(first_fast[0], at, 8, 0),
        lax.dynamic_slice_in_dim(gate_fast[0], at, 8, 0),
    )
    narrow = lambda at: lax.dynamic_slice_in_dim(second_fast[0], core * DH + at, 8, 0)
    middle = jnp.where(
        odd == 1,
        jnp.concatenate([narrow(base + 8), narrow(base + 16)], axis=1),
        wide(base + 8),
    )
    old = jnp.concatenate([wide(base + 16 * odd), middle, narrow(base)], axis=1).astype(F32)

    def exchange(blocks):
        return lax.all_to_all(blocks, "tok", 0, 0, axis_index_groups=CHIPS)

    total = join(keep, got, before, after)
    got = exchange(total)
    query = project(tokens, qkv_weight, total)
    att_low = attend(0, 2, bounds, row_bounds, query, before, kv, after, query)
    fresh = renorm(pos, old, got, [att_low])
    got = exchange(fresh)
    att_high = attend(2, 2, bounds, row_bounds, query, before, kv, after, fresh)
    half = unpack(got, [att_high, *weights])
    other = send(half, SWAP_C)

    gain = fast_gain[None, :]
    result, mixed = None, []
    dep = att_high
    for start, attended in ((0, att_low), (2, att_high)):
        dep = apply(start, 2, pos, query, half, other, attended, 0, gain, dep)
        mixed.append((start, dep))
    for start, part in mixed:
        parts = [part] + [
            lax.ppermute(part, "head", shift_h(d)) for d in range(1, HS)
        ]
        result = output(start, 2, parts, weights, result)
    return result


def solution(mesh):
    placed = (
        P("tok", None),
        P(None, "head"),
        P(None, "head"),
        P("head", None, None),
        P("head", None, None),
        P("head", None, None),
        P("head"),
        P("head", None),
        P(),
    )
    return jax.shard_map(
        body, mesh=mesh, in_specs=placed, out_specs=P("tok", "head"), check_vma=False
    )
```

```python
import functools
import math

import jax
import jax.numpy as jnp
from jax import lax
from jax.experimental import pallas as pl
from jax.experimental.pallas import tpu as pltpu
from jax.sharding import PartitionSpec as P

DH = 384
HID = 768
TOK = 1024
XS, ZS, CS, HS = 4, 8, 2, 4
SHARDS = XS * ZS * CS
TOKENS = TOK * SHARDS
SLOTS = XS * ZS
PACK = 2 * HID + DH
WIDE = HID + DH
KB = 256
QB = 256
BF, F32, I32 = jnp.bfloat16, jnp.float32, jnp.int32
NT = (((1,), (1,)), ((), ()))
VM = 56 * 1024 * 1024

SMEM = pl.BlockSpec(memory_space=pltpu.SMEM)
WHOLE = pl.BlockSpec(memory_space=pltpu.VMEM)
DEP = pl.BlockSpec(memory_space=pl.ANY)


def params():
    return pltpu.CompilerParams(vmem_limit_bytes=VM)


def mm(a, b):
    return jnp.dot(a, b, preferred_element_type=F32)


def sds(shape, dtype):
    return jax.ShapeDtypeStruct(shape, dtype)


SWAP_C = [(t, t ^ 1) for t in range(SHARDS)]
CHIPS = [[chip * CS + c for chip in range(SHARDS // CS)] for c in range(CS)]


def shift_h(d):
    return [(h, (h + d) % HS) for h in range(HS)]


def full(shape):
    return pl.BlockSpec(shape, lambda i: (0,) * len(shape))


def keys_kernel(t_ref, wk_ref, wv_ref, wr_ref, kv_ref, rates_ref):
    t = t_ref[...]
    kv_ref[:, :DH] = mm(t, wk_ref[...]).astype(BF)
    kv_ref[:, DH:] = mm(t, wv_ref[...]).astype(BF)
    raw = lax.dot_general(t, wr_ref[...], NT, preferred_element_type=F32)
    rates_ref[...] = (0.25 / math.sqrt(TOKENS)) * (
        jnp.maximum(raw, 0.0) + jnp.log1p(jnp.exp(-jnp.abs(raw)))
    )


def keys(tokens, qkv_weight, rate_weight):
    rows, wide = tokens.shape
    block = 512
    return pl.pallas_call(
        keys_kernel,
        grid=(rows // block,),
        in_specs=[
            pl.BlockSpec((block, wide), lambda i: (i, 0)),
            pl.BlockSpec((wide, DH), lambda i: (0, 1)),
            pl.BlockSpec((wide, DH), lambda i: (0, 2)),
            full((3, wide)),
        ],
        out_specs=[
            pl.BlockSpec((block, 2 * DH), lambda i: (i, 0)),
            pl.BlockSpec((block, 3), lambda i: (i, 0)),
        ],
        out_shape=[sds((rows, 2 * DH), BF), sds((rows, 3), F32)],
        compiler_params=params(),
        name="keys",
    )(tokens, qkv_weight, qkv_weight, rate_weight.T)


def update_kernel(pos_ref, kv_ref, r_ref, w1_ref, w3_ref, w2_ref, send_ref, keep_ref, second):
    even = pos_ref[0] == 0
    k, v = kv_ref[:, :DH], kv_ref[:, DH:]
    r = r_ref[...]
    r1, r3 = r[:, 0:1], r[:, 1:2]
    k_t = k.T
    e2_t = (r[:, 2:3] * v.astype(F32)).astype(BF).T
    chunk = 256
    for j in range(HID // chunk):
        cols = slice(j * chunk, (j + 1) * chunk)
        a = mm(k, w1_ref[0, :, cols])
        b = mm(k, w3_ref[0, :, cols])
        back = lax.dot_general(v, w2_ref[0, cols, :], NT, preferred_element_type=F32)
        sig = jax.nn.sigmoid(a)
        act = a * sig
        z = (act * b).astype(BF)
        e1 = (r1 * back * b * (sig * (1.0 + a * (1.0 - sig)))).astype(BF)
        e3 = (r3 * back * act).astype(BF)
        first = mm(k_t, e1)
        gate = mm(k_t, e3)
        second[cols, :] = mm(e2_t, z).T
        keep_ref[:, cols] = jnp.where(even, first, gate)
        send_ref[:, cols] = jnp.where(even, gate, first).astype(BF)
    low, high = second[:DH, :], second[DH:, :]
    keep_ref[:, HID:] = jnp.where(even, low, high)
    send_ref[:, HID:] = jnp.where(even, high, low).astype(BF)


def update(pos, kv, rates, first_fast, gate_fast, second_fast):
    return pl.pallas_call(
        update_kernel,
        grid=(1,),
        in_specs=[
            SMEM,
            full(kv.shape),
            full(rates.shape),
            full((1, DH, HID)),
            full((1, DH, HID)),
            full((1, HID, DH)),
        ],
        out_specs=[full((DH, WIDE)), full((DH, WIDE))],
        out_shape=[sds((DH, WIDE), BF), sds((DH, WIDE), F32)],
        scratch_shapes=[pltpu.VMEM((HID, DH), F32)],
        compiler_params=params(),
        name="update",
    )(pos, kv, rates, first_fast, gate_fast, second_fast)


def places():
    for pair in range(SLOTS // 2):
        top, mid, low = (slice(24 * pair + 8 * i, 24 * pair + 8 * i + 8) for i in range(3))
        yield 2 * pair, slice(0, HID), top, slice(0, HID)
        yield 2 * pair, slice(HID, 2 * HID), mid, slice(0, HID)
        yield 2 * pair, slice(2 * HID, PACK), top, slice(HID, WIDE)
        yield 2 * pair + 1, slice(0, HID), low, slice(0, HID)
        yield 2 * pair + 1, slice(HID, WIDE), mid, slice(HID, WIDE)
        yield 2 * pair + 1, slice(WIDE, 2 * HID), low, slice(HID, WIDE)


def join_kernel(keep_ref, got_ref, before_ref, after_ref, out_ref, total):
    total[...] = keep_ref[...] + got_ref[...].astype(F32)
    for slot, to, rows, cols in places():
        out_ref[slot, :, to] = total[rows, cols].astype(BF)
    for slot in range(1, SLOTS, 2):
        out_ref[slot, :, 2 * HID :] = jnp.zeros((8, DH), BF)


def join(keep, got, before, after):
    return pl.pallas_call(
        join_kernel,
        grid=(1,),
        in_specs=[full((DH, WIDE)), full((DH, WIDE)), DEP, DEP],
        out_specs=full((SLOTS, 8, PACK)),
        out_shape=sds((SLOTS, 8, PACK), BF),
        scratch_shapes=[pltpu.VMEM((DH, WIDE), F32)],
        compiler_params=params(),
        name="join",
    )(keep, got, before, after)


def renorm_kernel(pos_ref, old_ref, got_ref, *rest):
    out = rest[-1]
    odd = pos_ref[1] == 1
    update = got_ref[0].astype(F32)
    for s in range(1, SLOTS):
        update = update + got_ref[s].astype(F32)
    old = old_ref[...]
    fresh = old + update

    def squares(value):
        u = [
            jnp.sum(jnp.square(value[:, i * DH : (i + 1) * DH]), axis=1, keepdims=True)
            for i in range(PACK // DH)
        ]
        wide = u[2] + u[3]
        return (
            (0, HID, u[0] + u[1]),
            (HID, WIDE, jnp.where(odd, u[2], wide)),
            (WIDE, 2 * HID, jnp.where(odd, u[3], wide)),
            (2 * HID, PACK, u[4]),
        )

    for (lo, hi, w_sq), (_, _, f_sq) in zip(squares(old), squares(fresh)):
        new = (fresh[:, lo:hi] * (jnp.sqrt(w_sq) / jnp.sqrt(f_sq + 1e-6))).astype(BF)
        for s in range(SLOTS):
            out[s, :, lo:hi] = new


def renorm(pos, old, got, deps):
    shape = (SLOTS, 8, PACK)
    return pl.pallas_call(
        renorm_kernel,
        grid=(1,),
        in_specs=[SMEM, full((8, PACK)), full(shape)] + [DEP] * len(deps),
        out_specs=full(shape),
        out_shape=sds(shape, BF),
        compiler_params=params(),
        name="renorm",
    )(pos, old, got, *deps)


def unpack_kernel(got_ref, *rest):
    out, total = rest[-2:]
    for slot, to, rows, cols in places():
        total[rows, cols] = got_ref[slot, :, to].astype(F32)
    out[...] = total[...].astype(BF)


def unpack(got, deps):
    return pl.pallas_call(
        unpack_kernel,
        grid=(1,),
        in_specs=[full((SLOTS, 8, PACK))] + [DEP] * len(deps),
        out_specs=full((DH, WIDE)),
        out_shape=sds((DH, WIDE), BF),
        scratch_shapes=[pltpu.VMEM((DH, WIDE), F32)],
        compiler_params=params(),
        name="unpack",
    )(got, *deps)


def project_kernel(t_ref, w_ref, dep_ref, q_ref):
    q_ref[...] = mm(t_ref[...], w_ref[...]).astype(BF)


def project(tokens, qkv_weight, dep):
    rows, wide = tokens.shape
    block = 256
    return pl.pallas_call(
        project_kernel,
        grid=(rows // block,),
        in_specs=[
            pl.BlockSpec((block, wide), lambda i: (i, 0)),
            pl.BlockSpec((wide, DH), lambda i: (0, 0)),
            DEP,
        ],
        out_specs=pl.BlockSpec((block, DH), lambda i: (i, 0)),
        out_shape=sds((rows, DH), BF),
        compiler_params=params(),
        name="project",
    )(tokens, qkv_weight, dep)


def attend_kernel(start, pos_ref, ends_ref, q_ref, before, mine, after, *rest):
    out_ref, s_ref = rest[-2:]
    shard = pos_ref[3]
    row = lax.broadcasted_iota(I32, (QB, 1), 0)
    place = row + (shard * TOK + (pl.program_id(0) + start) * QB)
    ends = ends_ref[...]
    shift = (shard - 1) * TOK
    begin = jnp.max(jnp.where(ends <= place, ends, 0), axis=1, keepdims=True) - shift
    end = jnp.min(jnp.where(ends <= place, TOKENS, ends), axis=1, keepdims=True) - shift
    first = lax.div(jnp.min(begin), KB)
    last = lax.div(jnp.max(end) + KB - 1, KB)
    q = q_ref[...]
    per = TOK // KB
    scale = 1.0 / math.sqrt(DH)

    def segments(step, carry):
        for s, ref in enumerate((before, mine, after)):
            lo = jnp.clip(first, s * per, (s + 1) * per)
            hi = jnp.clip(last, s * per, (s + 1) * per)
            carry = lax.fori_loop(lo, hi, functools.partial(step, s, ref), carry)
        return carry

    def scores(s, ref, kb, top):
        k = ref[pl.ds(pl.multiple_of((kb - s * per) * KB, KB), KB), :DH]
        sc = lax.dot_general(q, k, NT, preferred_element_type=F32) * scale
        col = lax.broadcasted_iota(I32, (QB, KB), 1) + kb * KB
        sc = jnp.where((col >= begin) & (col < end), sc, -1e30)
        s_ref[kb] = sc
        return jnp.maximum(top, jnp.max(sc, axis=1, keepdims=True))

    top = segments(scores, jnp.full((QB, 1), -1e30, F32))

    def weigh(kb, total):
        w = jnp.exp(s_ref[kb] - top)
        s_ref[kb] = w
        return total + jnp.sum(w, axis=1, keepdims=True)

    total = lax.fori_loop(first, last, weigh, jnp.zeros((QB, 1), F32))
    inverse = 1.0 / total
    out_ref[...] = jnp.zeros_like(out_ref)

    def gather(s, ref, kb, carry):
        v = ref[pl.ds(pl.multiple_of((kb - s * per) * KB, KB), KB), DH:]
        probs = (s_ref[kb] * inverse).astype(BF)
        out_ref[...] += mm(probs, v)
        return carry

    segments(gather, 0)


def attend(start, count, pos, ends, query, before, mine, after, dep, buffer):
    whole = full((TOK, 2 * DH))
    extra = [] if buffer is None else [buffer]
    return pl.pallas_call(
        functools.partial(attend_kernel, start),
        grid=(count,),
        in_specs=[
            SMEM,
            full(ends.shape),
            pl.BlockSpec((QB, DH), lambda i: (i + start, 0)),
            whole,
            whole,
            whole,
            DEP,
        ]
        + [DEP] * len(extra),
        out_specs=pl.BlockSpec((QB, DH), lambda i: (i + start, 0)),
        out_shape=sds((TOK, DH), F32),
        input_output_aliases={7: 0} if extra else {},
        scratch_shapes=[pltpu.VMEM((3 * TOK // KB, QB, KB), F32)],
        compiler_params=params(),
        name=f"attend_{start}",
    )(pos, ends, query, before, mine, after, dep, *extra)


def apply_kernel(pos_ref, q_ref, own_ref, other_ref, att_ref, gain_ref, *outs):
    core = pos_ref[0]
    q = q_ref[...]
    mine = mm(q, own_ref[:, :HID])
    theirs = mm(q, other_ref[:, :HID])
    even = core == 0
    a = jnp.where(even, mine, theirs)
    b = jnp.where(even, theirs, mine)
    hidden = (a * jax.nn.sigmoid(a) * b).astype(BF)
    h0, h1 = hidden[:, :DH], hidden[:, DH:]
    h_own = jnp.where(even, h0, h1)
    h_other = jnp.where(even, h1, h0)
    applied = mm(h_own, own_ref[:, HID:]) + mm(h_other, other_ref[:, HID:])
    mean = jnp.mean(applied * applied, axis=1, keepdims=True)
    normed = applied * lax.rsqrt(mean + 1e-6) * gain_ref[...]
    mixed = (att_ref[...] + normed).astype(BF)
    for step in range(HS):

        @pl.when(pl.program_id(0) == step)
        def _():
            outs[step][...] = mixed


def apply(pos, query, own, other, attended, gain):
    weight = pl.BlockSpec((DH, WIDE), lambda i, pos: (0, 0))
    rows = pl.BlockSpec((QB, DH), lambda i, pos: (lax.rem(pos[2] + i + 1, HS), 0))
    return pl.pallas_call(
        apply_kernel,
        grid_spec=pltpu.PrefetchScalarGridSpec(
            num_scalar_prefetch=1,
            grid=(HS,),
            in_specs=[rows, weight, weight, rows, pl.BlockSpec((1, DH), lambda i, pos: (0, 0))],
            out_specs=[pl.BlockSpec((QB, DH), lambda i, pos: (0, 0))] * HS,
        ),
        out_shape=[sds((QB, DH), BF)] * HS,
        compiler_params=params(),
        name="apply",
    )(pos, query, own, other, attended, gain)


def output_kernel(pos_ref, *refs):
    parts, weights, outs = refs[:HS], refs[HS : 2 * HS], refs[2 * HS :]
    head = pos_ref[2]
    for e, out in enumerate(outs):
        cols = pl.ds(pl.multiple_of(lax.rem(head + e + 1, HS) * DH, DH), DH)
        total = mm(parts[0][...], weights[0][:, cols])
        for part, weight in zip(parts[1:], weights[1:]):
            total = total + mm(part[...], weight[:, cols])
        out[...] = total.astype(BF)


def output(pos, parts, weights):
    return pl.pallas_call(
        output_kernel,
        grid=(1,),
        in_specs=[SMEM] + [full((QB, DH))] * HS + [full((DH, HS * DH))] * HS,
        out_specs=[full((QB, DH))] * HS,
        out_shape=[sds((QB, DH), BF)] * HS,
        compiler_params=params(),
        name="output",
    )(pos, *parts, *weights)


def arrange_kernel(pos_ref, *refs):
    parts, out = refs[:-1], refs[-1]
    head = pos_ref[2]
    for d, part in enumerate(parts):
        rows = pl.ds(pl.multiple_of(lax.rem(head - d + HS, HS) * QB, QB), QB)
        out[rows, :] = part[...]


def arrange(pos, parts):
    return pl.pallas_call(
        arrange_kernel,
        grid=(1,),
        in_specs=[SMEM] + [full((QB, DH))] * HS,
        out_specs=full((TOK, DH)),
        out_shape=sds((TOK, DH), BF),
        compiler_params=params(),
        name="arrange",
    )(pos, *parts)


def body(
    tokens,
    qkv_weight,
    rate_weight,
    first_fast,
    gate_fast,
    second_fast,
    fast_gain,
    out_weight,
    frame_lengths,
):
    mine = lax.axis_index("tok")
    head = lax.axis_index("head")
    chip, core = mine // CS, mine % CS
    odd = chip % 2
    send = lambda value, pairs: lax.ppermute(value, "tok", pairs)

    kv, rates = keys(tokens, qkv_weight, rate_weight)
    up = [(i, i + 1) for i in range(SHARDS - 1)]
    before = send(kv, up)
    after = send(kv, [(j, i) for i, j in up])
    pos = jnp.stack([core, odd, head, mine]).astype(I32)
    give, keep = update(pos, kv, rates, first_fast, gate_fast, second_fast)
    got = send(give, SWAP_C)

    order = jnp.arange(frame_lengths.shape[0], dtype=I32)
    ends = jnp.sum(
        jnp.where(order[:, None] <= order[None, :], frame_lengths[:, None], 0),
        axis=0,
        keepdims=True,
    )

    def spread(parts):
        return [lax.ppermute(p, "head", shift_h(d)) if d else p for d, p in enumerate(parts)]

    weights = spread([out_weight] * HS)

    base = chip // 2 * 24
    wide = lambda at: jnp.where(
        core == 0,
        lax.dynamic_slice_in_dim(first_fast[0], at, 8, 0),
        lax.dynamic_slice_in_dim(gate_fast[0], at, 8, 0),
    )
    narrow = lambda at: lax.dynamic_slice_in_dim(second_fast[0], core * DH + at, 8, 0)
    middle = jnp.where(
        odd == 1,
        jnp.concatenate([narrow(base + 8), narrow(base + 16)], axis=1),
        wide(base + 8),
    )
    old = jnp.concatenate([wide(base + 16 * odd), middle, narrow(base)], axis=1).astype(F32)

    def exchange(blocks):
        return lax.all_to_all(blocks, "tok", 0, 0, axis_index_groups=CHIPS)

    total = join(keep, got, before, after)
    got = exchange(total)
    query = project(tokens, qkv_weight, total)
    att = functools.partial(attend, pos=pos, ends=ends, query=query, before=before, mine=kv, after=after)
    att_low = att(0, 2, dep=query, buffer=None)
    fresh = renorm(pos, old, got, [att_low, weights[1], weights[3]])
    got = exchange(fresh)
    attended = att(2, 2, dep=fresh, buffer=att_low)
    half = unpack(got, [attended, weights[2]])
    other = send(half, SWAP_C)

    ahead = apply(pos, query, half, other, attended, fast_gain[None, :])
    parts = spread([ahead[-1], *ahead[:-1]])
    ahead = output(pos, parts, weights)
    result = arrange(pos, spread([ahead[-1], *ahead[:-1]]))
    return result


def solution(mesh):
    placed = (
        P("tok", None),
        P(None, "head"),
        P(None, "head"),
        P("head", None, None),
        P("head", None, None),
        P("head", None, None),
        P("head"),
        P("head", None),
        P(),
    )
    return jax.shard_map(
        body, mesh=mesh, in_specs=placed, out_specs=P("tok", "head"), check_vma=False
    )
```

```python
import functools
import math

import jax
import jax.numpy as jnp
from jax import lax
from jax.experimental import pallas as pl
from jax.experimental.pallas import tpu as pltpu
from jax.sharding import PartitionSpec as P

DH = 384
HID = 768
TOK = 1024
XS, ZS, CS, HS = 4, 8, 2, 4
SHARDS = XS * ZS * CS
TOKENS = TOK * SHARDS
XROWS = DH // XS
ROWS = 16
OWNERS = XROWS // ROWS
WIDE = HID + DH
KB = 256
QB = 256
BF, F32, I32 = jnp.bfloat16, jnp.float32, jnp.int32
NT = (((1,), (1,)), ((), ()))
VM = 56 * 1024 * 1024

SMEM = pl.BlockSpec(memory_space=pltpu.SMEM)
WHOLE = pl.BlockSpec(memory_space=pltpu.VMEM)
DEP = pl.BlockSpec(memory_space=pl.ANY)


def params():
    return pltpu.CompilerParams(vmem_limit_bytes=VM)


def mm(a, b):
    return jnp.dot(a, b, preferred_element_type=F32)


def sds(shape, dtype):
    return jax.ShapeDtypeStruct(shape, dtype)


SWAP_C = [(t, t ^ 1) for t in range(SHARDS)]
ALONG_Z = [
    [(x * ZS + z) * CS + c for z in range(ZS)] for x in range(XS) for c in range(CS)
]


def shift_x(d):
    return [(t, (t + d * ZS * CS) % SHARDS) for t in range(SHARDS)]


def shift_h(d):
    return [(h, (h + d) % HS) for h in range(HS)]


def full(shape):
    return pl.BlockSpec(shape, lambda i: (0,) * len(shape))


def keys_kernel(t_ref, wk_ref, wv_ref, wr_ref, kv_ref, rates_ref):
    t = t_ref[...]
    kv_ref[:, :DH] = mm(t, wk_ref[...]).astype(BF)
    kv_ref[:, DH:] = mm(t, wv_ref[...]).astype(BF)
    raw = lax.dot_general(t, wr_ref[...], NT, preferred_element_type=F32)
    rates_ref[...] = (0.25 / math.sqrt(TOKENS)) * (
        jnp.maximum(raw, 0.0) + jnp.log1p(jnp.exp(-jnp.abs(raw)))
    )


def keys(tokens, qkv_weight, rate_weight):
    rows, wide = tokens.shape
    block = 512
    return pl.pallas_call(
        keys_kernel,
        grid=(rows // block,),
        in_specs=[
            pl.BlockSpec((block, wide), lambda i: (i, 0)),
            pl.BlockSpec((wide, DH), lambda i: (0, 1)),
            pl.BlockSpec((wide, DH), lambda i: (0, 2)),
            full((3, wide)),
        ],
        out_specs=[
            pl.BlockSpec((block, 2 * DH), lambda i: (i, 0)),
            pl.BlockSpec((block, 3), lambda i: (i, 0)),
        ],
        out_shape=[sds((rows, 2 * DH), BF), sds((rows, 3), F32)],
        compiler_params=params(),
        name="keys",
    )(tokens, qkv_weight, qkv_weight, rate_weight.T)


def update_kernel(pos_ref, kv_ref, r_ref, w1_ref, w3_ref, w2_ref, send_ref, keep_ref, second):
    even = pos_ref[0] == 0
    k, v = kv_ref[:, :DH], kv_ref[:, DH:]
    r = r_ref[...]
    r1, r3 = r[:, 0:1], r[:, 1:2]
    k_t = k.T
    e2_t = (r[:, 2:3] * v.astype(F32)).astype(BF).T
    chunk = 256
    for j in range(HID // chunk):
        cols = slice(j * chunk, (j + 1) * chunk)
        a = mm(k, w1_ref[0, :, cols])
        b = mm(k, w3_ref[0, :, cols])
        back = lax.dot_general(v, w2_ref[0, cols, :], NT, preferred_element_type=F32)
        sig = jax.nn.sigmoid(a)
        act = a * sig
        z = (act * b).astype(BF)
        e1 = (r1 * back * b * (sig * (1.0 + a * (1.0 - sig)))).astype(BF)
        e3 = (r3 * back * act).astype(BF)
        first = mm(k_t, e1)
        gate = mm(k_t, e3)
        second[cols, :] = mm(e2_t, z).T
        keep_ref[:, cols] = jnp.where(even, first, gate)
        send_ref[:, cols] = jnp.where(even, gate, first).astype(BF)
    low, high = second[:DH, :], second[DH:, :]
    keep_ref[:, HID:] = jnp.where(even, low, high)
    send_ref[:, HID:] = jnp.where(even, high, low).astype(BF)


def update(pos, kv, rates, first_fast, gate_fast, second_fast):
    return pl.pallas_call(
        update_kernel,
        grid=(1,),
        in_specs=[
            SMEM,
            full(kv.shape),
            full(rates.shape),
            full((1, DH, HID)),
            full((1, DH, HID)),
            full((1, HID, DH)),
        ],
        out_specs=[full((DH, WIDE)), full((DH, WIDE))],
        out_shape=[sds((DH, WIDE), BF), sds((DH, WIDE), F32)],
        scratch_shapes=[pltpu.VMEM((HID, DH), F32)],
        compiler_params=params(),
        name="update",
    )(pos, kv, rates, first_fast, gate_fast, second_fast)


def rs_x_kernel(pos_ref, keep_ref, got_ref, *rest):
    outs = rest[-XS:]
    x = pos_ref[1]
    for d, out in enumerate(outs):
        rows = pl.ds(pl.multiple_of(lax.rem(x + d, XS) * XROWS, XROWS), XROWS)
        out[...] = (keep_ref[rows, :] + got_ref[rows, :].astype(F32)).astype(out.dtype)


def rs_x(pos, keep, got, deps):
    return pl.pallas_call(
        rs_x_kernel,
        grid=(1,),
        in_specs=[SMEM, full((DH, WIDE)), full((DH, WIDE))] + [DEP] * len(deps),
        out_specs=[full((XROWS, WIDE))] * XS,
        out_shape=[sds((XROWS, WIDE), F32)] + [sds((XROWS, WIDE), BF)] * (XS - 1),
        compiler_params=params(),
        name="rs_x",
    )(pos, keep, got, *deps)


def rs_z_kernel(own_ref, g1, g2, g3, *rest):
    out = rest[-1]
    for o in range(OWNERS):
        rows = slice(o * ROWS, (o + 1) * ROWS)
        total = (own_ref[rows, :] + g1[rows, :].astype(F32)) + (
            g2[rows, :].astype(F32) + g3[rows, :].astype(F32)
        )
        out[o] = total.astype(BF)
    out[OWNERS:] = jnp.zeros((ZS - OWNERS, ROWS, WIDE), BF)


def rs_z(own, got, deps):
    return pl.pallas_call(
        rs_z_kernel,
        grid=(1,),
        in_specs=[full((XROWS, WIDE))] * XS + [DEP] * len(deps),
        out_specs=full((ZS, ROWS, WIDE)),
        out_shape=sds((ZS, ROWS, WIDE), BF),
        compiler_params=params(),
        name="rs_z",
    )(own, *got, *deps)


def renorm_kernel(old_ref, got_ref, *rest):
    out = rest[-1]
    update = got_ref[0].astype(F32)
    for s in range(1, ZS):
        update = update + got_ref[s].astype(F32)
    old = old_ref[...]
    fresh = old + update
    for cols in (slice(0, HID), slice(HID, WIDE)):
        w, f = old[:, cols], fresh[:, cols]
        w_sq = jnp.sum(w * w, axis=1, keepdims=True)
        f_sq = jnp.sum(f * f, axis=1, keepdims=True)
        new = (f * (jnp.sqrt(w_sq) / jnp.sqrt(f_sq + 1e-6))).astype(BF)
        for s in range(ZS):
            out[s, :, cols] = new


def renorm(old, got, deps):
    shape = (ZS, ROWS, WIDE)
    return pl.pallas_call(
        renorm_kernel,
        grid=(1,),
        in_specs=[full((ROWS, WIDE)), full(shape)] + [DEP] * len(deps),
        out_specs=full(shape),
        out_shape=sds(shape, BF),
        compiler_params=params(),
        name="renorm",
    )(old, got, *deps)


def owned_kernel(got_ref, *rest):
    out, sem = rest[-2:]
    copy = pltpu.make_async_copy(got_ref.at[pl.ds(0, OWNERS)], out, sem)
    copy.start()
    copy.wait()


def owned(got, deps):
    return pl.pallas_call(
        owned_kernel,
        in_specs=[DEP] * (1 + len(deps)),
        out_specs=DEP,
        out_shape=sds((OWNERS, ROWS, WIDE), BF),
        scratch_shapes=[pltpu.SemaphoreType.DMA],
        compiler_params=params(),
        name="owned",
    )(got, *deps)


def ag_x_kernel(pos_ref, *rest):
    blocks, out = rest[:XS], rest[-1]
    x = pos_ref[1]
    for d, block in enumerate(blocks):
        owner = lax.rem(x - d + XS, XS)
        out[pl.ds(pl.multiple_of(owner * XROWS, XROWS), XROWS), :] = block[...]


def ag_x(pos, blocks):
    return pl.pallas_call(
        ag_x_kernel,
        grid=(1,),
        in_specs=[SMEM] + [full((XROWS, WIDE))] * XS,
        out_specs=full((DH, WIDE)),
        out_shape=sds((DH, WIDE), BF),
        compiler_params=params(),
        name="ag_x",
    )(pos, *blocks)


def project_kernel(t_ref, w_ref, dep_ref, q_ref):
    q_ref[...] = mm(t_ref[...], w_ref[...]).astype(BF)


def project(tokens, qkv_weight, dep):
    rows, wide = tokens.shape
    block = 256
    return pl.pallas_call(
        project_kernel,
        grid=(rows // block,),
        in_specs=[
            pl.BlockSpec((block, wide), lambda i: (i, 0)),
            pl.BlockSpec((wide, DH), lambda i: (0, 0)),
            DEP,
        ],
        out_specs=pl.BlockSpec((block, DH), lambda i: (i, 0)),
        out_shape=sds((rows, DH), BF),
        compiler_params=params(),
        name="project",
    )(tokens, qkv_weight, dep)


def attend_kernel(start, pos_ref, ends_ref, q_ref, before, mine, after, *rest):
    out_ref, s_ref = rest[-2:]
    shard = pos_ref[3]
    row = lax.broadcasted_iota(I32, (QB, 1), 0)
    place = row + (shard * TOK + (pl.program_id(0) + start) * QB)
    ends = ends_ref[...]
    shift = (shard - 1) * TOK
    begin = jnp.max(jnp.where(ends <= place, ends, 0), axis=1, keepdims=True) - shift
    end = jnp.min(jnp.where(ends <= place, TOKENS, ends), axis=1, keepdims=True) - shift
    first = lax.div(jnp.min(begin), KB)
    last = lax.div(jnp.max(end) + KB - 1, KB)
    q = q_ref[...]
    per = TOK // KB
    scale = 1.0 / math.sqrt(DH)

    def segments(step, carry):
        for s, ref in enumerate((before, mine, after)):
            lo = jnp.clip(first, s * per, (s + 1) * per)
            hi = jnp.clip(last, s * per, (s + 1) * per)
            carry = lax.fori_loop(lo, hi, functools.partial(step, s, ref), carry)
        return carry

    def scores(s, ref, kb, top):
        k = ref[pl.ds(pl.multiple_of((kb - s * per) * KB, KB), KB), :DH]
        sc = lax.dot_general(q, k, NT, preferred_element_type=F32) * scale
        col = lax.broadcasted_iota(I32, (QB, KB), 1) + kb * KB
        sc = jnp.where((col >= begin) & (col < end), sc, -1e30)
        s_ref[kb] = sc
        for lane in range(0, KB, 128):
            top = jnp.maximum(top, sc[:, lane : lane + 128])
        return top

    top = segments(scores, jnp.full((QB, 128), -1e30, F32))
    top = jnp.max(top, axis=1, keepdims=True)

    def weigh(kb, total):
        w = jnp.exp(s_ref[kb] - top)
        s_ref[kb] = w
        for lane in range(0, KB, 128):
            total = total + w[:, lane : lane + 128]
        return total

    total = lax.fori_loop(first, last, weigh, jnp.zeros((QB, 128), F32))
    inverse = 1.0 / jnp.sum(total, axis=1, keepdims=True)
    out_ref[...] = jnp.zeros_like(out_ref)

    def gather(s, ref, kb, carry):
        v = ref[pl.ds(pl.multiple_of((kb - s * per) * KB, KB), KB), DH:]
        probs = (s_ref[kb] * inverse).astype(BF)
        out_ref[...] += mm(probs, v)
        return carry

    segments(gather, 0)


def attend(start, count, pos, ends, query, before, mine, after, dep, buffer):
    whole = full((TOK, 2 * DH))
    extra = [] if buffer is None else [buffer]
    return pl.pallas_call(
        functools.partial(attend_kernel, start),
        grid=(count,),
        in_specs=[
            SMEM,
            full(ends.shape),
            pl.BlockSpec((QB, DH), lambda i: (i + start, 0)),
            whole,
            whole,
            whole,
            DEP,
        ]
        + [DEP] * len(extra),
        out_specs=pl.BlockSpec((QB, DH), lambda i: (i + start, 0)),
        out_shape=sds((TOK, DH), F32),
        input_output_aliases={7: 0} if extra else {},
        scratch_shapes=[pltpu.VMEM((3 * TOK // KB, QB, KB), F32)],
        compiler_params=params(),
        name=f"attend_{start}",
    )(pos, ends, query, before, mine, after, dep, *extra)


def apply_kernel(pos_ref, q_ref, own_ref, other_ref, att_ref, gain_ref, *outs):
    core = pos_ref[0]
    q = q_ref[...]
    mine = mm(q, own_ref[:, :HID])
    theirs = mm(q, other_ref[:, :HID])
    even = core == 0
    a = jnp.where(even, mine, theirs)
    b = jnp.where(even, theirs, mine)
    hidden = (a * jax.nn.sigmoid(a) * b).astype(BF)
    h0, h1 = hidden[:, :DH], hidden[:, DH:]
    h_own = jnp.where(even, h0, h1)
    h_other = jnp.where(even, h1, h0)
    applied = mm(h_own, own_ref[:, HID:]) + mm(h_other, other_ref[:, HID:])
    mean = jnp.mean(applied * applied, axis=1, keepdims=True)
    normed = applied * lax.rsqrt(mean + 1e-6) * gain_ref[...]
    mixed = (att_ref[...] + normed).astype(BF)
    for step in range(HS):

        @pl.when(pl.program_id(0) == step)
        def _():
            outs[step][...] = mixed


def apply(pos, query, own, other, attended, gain):
    weight = pl.BlockSpec((DH, WIDE), lambda i, pos: (0, 0))
    rows = pl.BlockSpec((QB, DH), lambda i, pos: (lax.rem(pos[2] + i + 1, HS), 0))
    return pl.pallas_call(
        apply_kernel,
        grid_spec=pltpu.PrefetchScalarGridSpec(
            num_scalar_prefetch=1,
            grid=(HS,),
            in_specs=[rows, weight, weight, rows, pl.BlockSpec((1, DH), lambda i, pos: (0, 0))],
            out_specs=[pl.BlockSpec((QB, DH), lambda i, pos: (0, 0))] * HS,
        ),
        out_shape=[sds((QB, DH), BF)] * HS,
        compiler_params=params(),
        name="apply",
    )(pos, query, own, other, attended, gain)


def output_kernel(pos_ref, *refs):
    parts, weights, outs = refs[:HS], refs[HS : 2 * HS], refs[2 * HS :]
    total = mm(parts[0][...], weights[0][...])
    for part, weight in zip(parts[1:], weights[1:]):
        total = total + mm(part[...], weight[...])
    total = total.astype(BF)
    for step in range(HS):

        @pl.when(pl.program_id(0) == step)
        def _():
            outs[step][...] = total


def output(pos, parts, weight):
    rows = pl.BlockSpec((QB, DH), lambda i, pos: (0, 0))
    cols = [
        pl.BlockSpec(
            (DH, DH),
            lambda i, pos, d=d: (lax.rem(pos[2] - d + HS, HS), lax.rem(pos[2] + i + 1, HS)),
        )
        for d in range(HS)
    ]
    return pl.pallas_call(
        output_kernel,
        grid_spec=pltpu.PrefetchScalarGridSpec(
            num_scalar_prefetch=1,
            grid=(HS,),
            in_specs=[rows] * HS + cols,
            out_specs=[rows] * HS,
        ),
        out_shape=[sds((QB, DH), BF)] * HS,
        compiler_params=params(),
        name="output",
    )(pos, *parts, *[weight] * HS)


def arrange_kernel(pos_ref, *refs):
    parts, out, sems = refs[:HS], refs[HS], refs[HS + 1]
    head = pos_ref[2]
    copies = []
    for d, part in enumerate(parts):
        rows = pl.ds(pl.multiple_of(lax.rem(head - d + HS, HS) * QB, QB), QB)
        copies.append(pltpu.make_async_copy(part, out.at[rows, :], sems.at[d]))
    for copy in copies:
        copy.start()
    for copy in copies:
        copy.wait()


def arrange(pos, parts):
    return pl.pallas_call(
        arrange_kernel,
        in_specs=[SMEM] + [DEP] * HS,
        out_specs=DEP,
        out_shape=sds((TOK, DH), BF),
        scratch_shapes=[pltpu.SemaphoreType.DMA((HS,))],
        compiler_params=params(),
        name="arrange",
    )(pos, *parts)


def body(
    tokens,
    qkv_weight,
    rate_weight,
    first_fast,
    gate_fast,
    second_fast,
    fast_gain,
    out_weight,
    frame_lengths,
):
    mine = lax.axis_index("tok")
    head = lax.axis_index("head")
    x, z, core = mine // (ZS * CS), mine // CS % ZS, mine % CS
    send = lambda value, pairs: lax.ppermute(value, "tok", pairs)

    kv, rates = keys(tokens, qkv_weight, rate_weight)
    up = [(i, i + 1) for i in range(SHARDS - 1)]
    before = send(kv, up)
    after = send(kv, [(j, i) for i, j in up])
    pos = jnp.stack([core, x, head, mine]).astype(I32)
    give, keep = update(pos, kv, rates, first_fast, gate_fast, second_fast)
    got = send(give, SWAP_C)

    order = jnp.arange(frame_lengths.shape[0], dtype=I32)
    ends = jnp.sum(
        jnp.where(order[:, None] <= order[None, :], frame_lengths[:, None], 0),
        axis=0,
        keepdims=True,
    )

    def spread(parts):
        return [lax.ppermute(p, "head", shift_h(d)) if d else p for d, p in enumerate(parts)]

    weight = lax.all_gather(out_weight, "head", axis=0, tiled=True)

    row = jnp.minimum(x * XROWS + z * ROWS, DH - ROWS)
    pick = lambda w, at: lax.dynamic_slice_in_dim(w[0], at, ROWS, 0)
    old = jnp.concatenate(
        [
            jnp.where(core == 0, pick(first_fast, row), pick(gate_fast, row)),
            pick(second_fast, core * DH + row),
        ],
        axis=1,
    ).astype(F32)

    def exchange(blocks):
        return lax.all_to_all(blocks, "tok", 0, 0, axis_index_groups=ALONG_Z)

    own, *gives = rs_x(pos, keep, got, [before, after])
    got = [send(g, shift_x(d + 1)) for d, g in enumerate(gives)]
    query = project(tokens, qkv_weight, own)
    att = functools.partial(attend, pos=pos, ends=ends, query=query, before=before, mine=kv, after=after)
    total = rs_z(own, got, [query])
    got = exchange(total)
    att_low = att(0, 2, dep=total, buffer=None)
    fresh = renorm(old, got, [att_low])
    got = exchange(fresh)
    attended = att(2, 2, dep=fresh, buffer=att_low)
    block = owned(got, [attended, weight]).reshape(XROWS, WIDE)
    half = ag_x(pos, [block] + [send(block, shift_x(d)) for d in range(1, XS)])
    other = send(half, SWAP_C)

    ahead = apply(pos, query, half, other, attended, fast_gain[None, :])
    parts = spread([ahead[-1], *ahead[:-1]])
    ahead = output(pos, parts, weight)
    result = arrange(pos, spread([ahead[-1], *ahead[:-1]]))
    return result


def solution(mesh):
    placed = (
        P("tok", None),
        P(None, "head"),
        P(None, "head"),
        P("head", None, None),
        P("head", None, None),
        P("head", None, None),
        P("head"),
        P("head", None),
        P(),
    )
    return jax.shard_map(
        body, mesh=mesh, in_specs=placed, out_specs=P("tok", "head"), check_vma=False
    )
```

```python
import functools
import math

import jax
import jax.numpy as jnp
from jax import lax
from jax.experimental import pallas as pl
from jax.experimental.pallas import tpu as pltpu
from jax.sharding import PartitionSpec as P

DH = 384
HID = 768
TOK = 1024
XS, ZS, CS, HS = 4, 8, 2, 4
SHARDS = XS * ZS * CS
TOKENS = TOK * SHARDS
XROWS = DH // XS
ROWS = 16
OWNERS = XROWS // ROWS
WIDE = HID + DH
KB = 256
QB = 256
BF, F32, I32 = jnp.bfloat16, jnp.float32, jnp.int32
NT = (((1,), (1,)), ((), ()))
VM = 56 * 1024 * 1024

SMEM = pl.BlockSpec(memory_space=pltpu.SMEM)
WHOLE = pl.BlockSpec(memory_space=pltpu.VMEM)
DEP = pl.BlockSpec(memory_space=pl.ANY)


def params():
    return pltpu.CompilerParams(vmem_limit_bytes=VM)


def mm(a, b):
    return jnp.dot(a, b, preferred_element_type=F32)


def sds(shape, dtype):
    return jax.ShapeDtypeStruct(shape, dtype)


SWAP_C = [(t, t ^ 1) for t in range(SHARDS)]
ALONG_Z = [
    [(x * ZS + z) * CS + c for z in range(ZS)] for x in range(XS) for c in range(CS)
]


def shift_x(d):
    return [(t, (t + d * ZS * CS) % SHARDS) for t in range(SHARDS)]


def shift_h(d):
    return [(h, (h + d) % HS) for h in range(HS)]


def full(shape):
    return pl.BlockSpec(shape, lambda i: (0,) * len(shape))


def keys_kernel(t_ref, wk_ref, wv_ref, wr_ref, kv_ref, rates_ref):
    t = t_ref[...]
    kv_ref[:, :DH] = mm(t, wk_ref[...]).astype(BF)
    kv_ref[:, DH:] = mm(t, wv_ref[...]).astype(BF)
    raw = lax.dot_general(t, wr_ref[...], NT, preferred_element_type=F32)
    rates_ref[...] = (0.25 / math.sqrt(TOKENS)) * (
        jnp.maximum(raw, 0.0) + jnp.log1p(jnp.exp(-jnp.abs(raw)))
    )


def keys(tokens, qkv_weight, rate_weight):
    rows, wide = tokens.shape
    block = 512
    return pl.pallas_call(
        keys_kernel,
        grid=(rows // block,),
        in_specs=[
            pl.BlockSpec((block, wide), lambda i: (i, 0)),
            pl.BlockSpec((wide, DH), lambda i: (0, 1)),
            pl.BlockSpec((wide, DH), lambda i: (0, 2)),
            full((3, wide)),
        ],
        out_specs=[
            pl.BlockSpec((block, 2 * DH), lambda i: (i, 0)),
            pl.BlockSpec((block, 3), lambda i: (i, 0)),
        ],
        out_shape=[sds((rows, 2 * DH), BF), sds((rows, 3), F32)],
        compiler_params=params(),
        name="keys",
    )(tokens, qkv_weight, qkv_weight, rate_weight.T)


def update_kernel(pos_ref, kv_ref, r_ref, w1_ref, w3_ref, w2_ref, send_ref, keep_ref, second):
    even = pos_ref[0] == 0
    k, v = kv_ref[:, :DH], kv_ref[:, DH:]
    r = r_ref[...]
    r1, r3 = r[:, 0:1], r[:, 1:2]
    k_t = k.T
    e2_t = (r[:, 2:3] * v.astype(F32)).astype(BF).T
    chunk = 256
    for j in range(HID // chunk):
        cols = slice(j * chunk, (j + 1) * chunk)
        a = mm(k, w1_ref[0, :, cols])
        b = mm(k, w3_ref[0, :, cols])
        back = lax.dot_general(v, w2_ref[0, cols, :], NT, preferred_element_type=F32)
        sig = jax.nn.sigmoid(a)
        act = a * sig
        z = (act * b).astype(BF)
        e1 = (r1 * back * b * (sig * (1.0 + a * (1.0 - sig)))).astype(BF)
        e3 = (r3 * back * act).astype(BF)
        first = mm(k_t, e1)
        gate = mm(k_t, e3)
        second[cols, :] = mm(e2_t, z).T
        keep_ref[:, cols] = jnp.where(even, first, gate)
        send_ref[:, cols] = jnp.where(even, gate, first).astype(BF)
    low, high = second[:DH, :], second[DH:, :]
    keep_ref[:, HID:] = jnp.where(even, low, high)
    send_ref[:, HID:] = jnp.where(even, high, low).astype(BF)


def update(pos, kv, rates, first_fast, gate_fast, second_fast):
    return pl.pallas_call(
        update_kernel,
        grid=(1,),
        in_specs=[
            SMEM,
            full(kv.shape),
            full(rates.shape),
            full((1, DH, HID)),
            full((1, DH, HID)),
            full((1, HID, DH)),
        ],
        out_specs=[full((DH, WIDE)), full((DH, WIDE))],
        out_shape=[sds((DH, WIDE), BF), sds((DH, WIDE), F32)],
        scratch_shapes=[pltpu.VMEM((HID, DH), F32)],
        compiler_params=params(),
        name="update",
    )(pos, kv, rates, first_fast, gate_fast, second_fast)


def rs_x_kernel(pos_ref, keep_ref, got_ref, *rest):
    outs = rest[-XS:]
    x = pos_ref[1]
    for d, out in enumerate(outs):
        rows = pl.ds(pl.multiple_of(lax.rem(x + d, XS) * XROWS, XROWS), XROWS)
        out[...] = (keep_ref[rows, :] + got_ref[rows, :].astype(F32)).astype(out.dtype)


def rs_x(pos, keep, got, deps):
    return pl.pallas_call(
        rs_x_kernel,
        grid=(1,),
        in_specs=[SMEM, full((DH, WIDE)), full((DH, WIDE))] + [DEP] * len(deps),
        out_specs=[full((XROWS, WIDE))] * XS,
        out_shape=[sds((XROWS, WIDE), F32)] + [sds((XROWS, WIDE), BF)] * (XS - 1),
        compiler_params=params(),
        name="rs_x",
    )(pos, keep, got, *deps)


def rs_z_kernel(own_ref, g1, g2, g3, *rest):
    out = rest[-1]
    for o in range(OWNERS):
        rows = slice(o * ROWS, (o + 1) * ROWS)
        total = (own_ref[rows, :] + g1[rows, :].astype(F32)) + (
            g2[rows, :].astype(F32) + g3[rows, :].astype(F32)
        )
        out[o] = total.astype(BF)
    out[OWNERS:] = jnp.zeros((ZS - OWNERS, ROWS, WIDE), BF)


def rs_z(own, got, deps):
    return pl.pallas_call(
        rs_z_kernel,
        grid=(1,),
        in_specs=[full((XROWS, WIDE))] * XS + [DEP] * len(deps),
        out_specs=full((ZS, ROWS, WIDE)),
        out_shape=sds((ZS, ROWS, WIDE), BF),
        compiler_params=params(),
        name="rs_z",
    )(own, *got, *deps)


def renorm_kernel(old_ref, got_ref, *rest):
    out = rest[-1]
    update = got_ref[0].astype(F32)
    for s in range(1, ZS):
        update = update + got_ref[s].astype(F32)
    old = old_ref[...]
    fresh = old + update
    for cols in (slice(0, HID), slice(HID, WIDE)):
        w, f = old[:, cols], fresh[:, cols]
        w_sq = jnp.sum(w * w, axis=1, keepdims=True)
        f_sq = jnp.sum(f * f, axis=1, keepdims=True)
        new = (f * (jnp.sqrt(w_sq) / jnp.sqrt(f_sq + 1e-6))).astype(BF)
        for s in range(ZS):
            out[s, :, cols] = new


def renorm(old, got, deps):
    shape = (ZS, ROWS, WIDE)
    return pl.pallas_call(
        renorm_kernel,
        grid=(1,),
        in_specs=[full((ROWS, WIDE)), full(shape)] + [DEP] * len(deps),
        out_specs=full(shape),
        out_shape=sds(shape, BF),
        compiler_params=params(),
        name="renorm",
    )(old, got, *deps)


def owned_kernel(got_ref, *rest):
    out = rest[-1]
    for o in range(OWNERS):
        out[o * ROWS : (o + 1) * ROWS, :] = got_ref[o]


def owned(got, deps):
    return pl.pallas_call(
        owned_kernel,
        grid=(1,),
        in_specs=[full((ZS, ROWS, WIDE))] + [DEP] * len(deps),
        out_specs=full((XROWS, WIDE)),
        out_shape=sds((XROWS, WIDE), BF),
        compiler_params=params(),
        name="owned",
    )(got, *deps)


def ag_x_kernel(pos_ref, *rest):
    blocks, out = rest[:XS], rest[-1]
    x = pos_ref[1]
    for d, block in enumerate(blocks):
        owner = lax.rem(x - d + XS, XS)
        out[pl.ds(pl.multiple_of(owner * XROWS, XROWS), XROWS), :] = block[...]


def ag_x(pos, blocks, deps):
    return pl.pallas_call(
        ag_x_kernel,
        grid=(1,),
        in_specs=[SMEM] + [full((XROWS, WIDE))] * XS + [DEP] * len(deps),
        out_specs=full((DH, WIDE)),
        out_shape=sds((DH, WIDE), BF),
        compiler_params=params(),
        name="ag_x",
    )(pos, *blocks, *deps)


def project_kernel(t_ref, w_ref, *rest):
    q_ref = rest[-1]
    q_ref[...] = mm(t_ref[...], w_ref[...]).astype(BF)


def project(tokens, qkv_weight, deps):
    rows, wide = tokens.shape
    block = 256
    return pl.pallas_call(
        project_kernel,
        grid=(rows // block,),
        in_specs=[
            pl.BlockSpec((block, wide), lambda i: (i, 0)),
            pl.BlockSpec((wide, DH), lambda i: (0, 0)),
        ]
        + [DEP] * len(deps),
        out_specs=pl.BlockSpec((block, DH), lambda i: (i, 0)),
        out_shape=sds((rows, DH), BF),
        compiler_params=params(),
        name="project",
    )(tokens, qkv_weight, *deps)


def attend_kernel(ahead, pos_ref, ends_ref, q_ref, before, mine, after, dep_ref, out_ref, s_ref):
    shard = pos_ref[3]
    piece = lax.rem(pos_ref[2] + ahead, HS)
    row = lax.broadcasted_iota(I32, (QB, 1), 0)
    place = row + (shard * TOK + piece * QB)
    ends = ends_ref[...]
    shift = (shard - 1) * TOK
    begin = jnp.max(jnp.where(ends <= place, ends, 0), axis=1, keepdims=True) - shift
    end = jnp.min(jnp.where(ends <= place, TOKENS, ends), axis=1, keepdims=True) - shift
    first = lax.div(jnp.min(begin), KB)
    last = lax.div(jnp.max(end) + KB - 1, KB)
    q = q_ref[pl.ds(pl.multiple_of(piece * QB, QB), QB), :]
    per = TOK // KB
    scale = 1.0 / math.sqrt(DH)

    def segments(step, carry):
        for s, ref in enumerate((before, mine, after)):
            lo = jnp.clip(first, s * per, (s + 1) * per)
            hi = jnp.clip(last, s * per, (s + 1) * per)
            carry = lax.fori_loop(lo, hi, functools.partial(step, s, ref), carry)
        return carry

    def scores(s, ref, kb, top):
        k = ref[pl.ds(pl.multiple_of((kb - s * per) * KB, KB), KB), :DH]
        sc = lax.dot_general(q, k, NT, preferred_element_type=F32) * scale
        col = lax.broadcasted_iota(I32, (QB, KB), 1) + kb * KB
        sc = jnp.where((col >= begin) & (col < end), sc, -1e30)
        s_ref[kb] = sc
        for lane in range(0, KB, 128):
            top = jnp.maximum(top, sc[:, lane : lane + 128])
        return top

    top = segments(scores, jnp.full((QB, 128), -1e30, F32))
    top = jnp.max(top, axis=1, keepdims=True)

    def weigh(kb, total):
        w = jnp.exp(s_ref[kb] - top)
        s_ref[kb] = w
        for lane in range(0, KB, 128):
            total = total + w[:, lane : lane + 128]
        return total

    total = lax.fori_loop(first, last, weigh, jnp.zeros((QB, 128), F32))
    inverse = 1.0 / jnp.sum(total, axis=1, keepdims=True)
    out_ref[...] = jnp.zeros_like(out_ref)

    def gather(s, ref, kb, carry):
        v = ref[pl.ds(pl.multiple_of((kb - s * per) * KB, KB), KB), DH:]
        probs = (s_ref[kb] * inverse).astype(BF)
        out_ref[...] += mm(probs, v)
        return carry

    segments(gather, 0)


def attend(ahead, pos, ends, query, before, mine, after, dep):
    whole = full((TOK, 2 * DH))
    return pl.pallas_call(
        functools.partial(attend_kernel, ahead),
        grid=(1,),
        in_specs=[SMEM, full(ends.shape), full((TOK, DH)), whole, whole, whole, DEP],
        out_specs=full((QB, DH)),
        out_shape=sds((QB, DH), F32),
        scratch_shapes=[pltpu.VMEM((3 * TOK // KB, QB, KB), F32)],
        compiler_params=params(),
        name=f"attend_{ahead}",
    )(pos, ends, query, before, mine, after, dep)


def apply_kernel(aheads, pos_ref, q_ref, own_ref, other_ref, gain_ref, *rest):
    count = len(aheads)
    attended, outs = rest[:count], rest[-count:]
    even = pos_ref[0] == 0
    for ahead, att_ref, out in zip(aheads, attended, outs):
        piece = lax.rem(pos_ref[2] + ahead, HS)
        q = q_ref[pl.ds(pl.multiple_of(piece * QB, QB), QB), :]
        mine = mm(q, own_ref[:, :HID])
        theirs = mm(q, other_ref[:, :HID])
        a = jnp.where(even, mine, theirs)
        b = jnp.where(even, theirs, mine)
        hidden = (a * jax.nn.sigmoid(a) * b).astype(BF)
        h0, h1 = hidden[:, :DH], hidden[:, DH:]
        h_own = jnp.where(even, h0, h1)
        h_other = jnp.where(even, h1, h0)
        applied = mm(h_own, own_ref[:, HID:]) + mm(h_other, other_ref[:, HID:])
        mean = jnp.mean(applied * applied, axis=1, keepdims=True)
        normed = applied * lax.rsqrt(mean + 1e-6) * gain_ref[...]
        out[...] = (att_ref[...] + normed).astype(BF)


def apply(aheads, pos, query, own, other, gain, attended, deps):
    count = len(aheads)
    return pl.pallas_call(
        functools.partial(apply_kernel, aheads),
        grid=(1,),
        in_specs=[SMEM, full((TOK, DH)), full((DH, WIDE)), full((DH, WIDE)), full((1, DH))]
        + [full((QB, DH))] * count
        + [DEP] * len(deps),
        out_specs=[full((QB, DH))] * count,
        out_shape=[sds((QB, DH), BF)] * count,
        compiler_params=params(),
        name=f"apply_{count}",
    )(pos, query, own, other, gain, *attended, *deps)


def output_kernel(pos_ref, *refs):
    parts, weights, outs = refs[:HS], refs[HS : 2 * HS], refs[2 * HS :]
    head = pos_ref[2]
    for e, out in enumerate(outs):
        cols = pl.ds(pl.multiple_of(lax.rem(head + e + 1, HS) * DH, DH), DH)
        total = mm(parts[0][...], weights[0][:, cols])
        for part, weight in zip(parts[1:], weights[1:]):
            total = total + mm(part[...], weight[:, cols])
        out[...] = total.astype(BF)


def output(pos, parts, weights):
    return pl.pallas_call(
        output_kernel,
        grid=(1,),
        in_specs=[SMEM] + [full((QB, DH))] * HS + [full((DH, HS * DH))] * HS,
        out_specs=[full((QB, DH))] * HS,
        out_shape=[sds((QB, DH), BF)] * HS,
        compiler_params=params(),
        name="output",
    )(pos, *parts, *weights)


def arrange_kernel(pos_ref, *refs):
    parts, out = refs[:-1], refs[-1]
    head = pos_ref[2]
    for d, part in enumerate(parts):
        rows = pl.ds(pl.multiple_of(lax.rem(head - d + HS, HS) * QB, QB), QB)
        out[rows, :] = part[...]


def arrange(pos, parts):
    return pl.pallas_call(
        arrange_kernel,
        grid=(1,),
        in_specs=[SMEM] + [full((QB, DH))] * HS,
        out_specs=full((TOK, DH)),
        out_shape=sds((TOK, DH), BF),
        compiler_params=params(),
        name="arrange",
    )(pos, *parts)


def body(
    tokens,
    qkv_weight,
    rate_weight,
    first_fast,
    gate_fast,
    second_fast,
    fast_gain,
    out_weight,
    frame_lengths,
):
    mine = lax.axis_index("tok")
    head = lax.axis_index("head")
    x, z, core = mine // (ZS * CS), mine // CS % ZS, mine % CS
    send = lambda value, pairs: lax.ppermute(value, "tok", pairs)

    kv, rates = keys(tokens, qkv_weight, rate_weight)
    up = [(i, i + 1) for i in range(SHARDS - 1)]
    before = send(kv, up)
    after = send(kv, [(j, i) for i, j in up])
    pos = jnp.stack([core, x, head, mine]).astype(I32)
    give, keep = update(pos, kv, rates, first_fast, gate_fast, second_fast)
    got = send(give, SWAP_C)

    order = jnp.arange(frame_lengths.shape[0], dtype=I32)
    ends = jnp.sum(
        jnp.where(order[:, None] <= order[None, :], frame_lengths[:, None], 0),
        axis=0,
        keepdims=True,
    )

    def spread(parts):
        return [lax.ppermute(p, "head", shift_h(d)) if d else p for d, p in enumerate(parts)]

    weights = spread([out_weight] * HS)

    row = jnp.minimum(x * XROWS + z * ROWS, DH - ROWS)
    pick = lambda w, at: lax.dynamic_slice_in_dim(w[0], at, ROWS, 0)
    old = jnp.concatenate(
        [
            jnp.where(core == 0, pick(first_fast, row), pick(gate_fast, row)),
            pick(second_fast, core * DH + row),
        ],
        axis=1,
    ).astype(F32)

    def exchange(blocks):
        return lax.all_to_all(blocks, "tok", 0, 0, axis_index_groups=ALONG_Z)

    own, *gives = rs_x(pos, keep, got, [before, after])
    got = [send(g, shift_x(d + 1)) for d, g in enumerate(gives)]
    query = project(tokens, qkv_weight, [own, ends, old])
    att = functools.partial(attend, pos=pos, ends=ends, query=query, before=before, mine=kv, after=after)
    total = rs_z(own, got, [query])
    got = exchange(total)
    att1 = att(1, dep=total)
    fresh = renorm(old, got, [att1, weights[1], weights[3]])
    got = exchange(fresh)
    att2 = att(2, dep=fresh)
    block = owned(got, [att2])
    att3 = att(3, dep=block)
    half = ag_x(pos, [block] + [send(block, shift_x(d)) for d in range(1, XS)], [att3, weights[2]])
    other = send(half, SWAP_C)

    mix = functools.partial(
        apply, pos=pos, query=query, own=half, other=other, gain=fast_gain[None, :]
    )
    away = mix((1, 2, 3), attended=[att1, att2, att3], deps=[])
    att0 = att(0, dep=away[0])
    [home] = mix((0,), attended=[att0], deps=[away[0]])
    parts = spread([home, *away])
    ahead = output(pos, parts, weights)
    result = arrange(pos, spread([ahead[-1], *ahead[:-1]]))
    return result


def solution(mesh):
    placed = (
        P("tok", None),
        P(None, "head"),
        P(None, "head"),
        P("head", None, None),
        P("head", None, None),
        P("head", None, None),
        P("head"),
        P("head", None),
        P(),
    )
    return jax.shard_map(
        body, mesh=mesh, in_specs=placed, out_specs=P("tok", "head"), check_vma=False
    )
```

```python
import functools
import math

import jax
import jax.numpy as jnp
from jax import lax
from jax.experimental import pallas as pl
from jax.experimental.pallas import tpu as pltpu
from jax.sharding import PartitionSpec as P

DH = 384
HID = 768
TOK = 1024
XS, ZS, CS, HS = 4, 8, 2, 4
SHARDS = XS * ZS * CS
TOKENS = TOK * SHARDS
XROWS = DH // XS
ROWS = 16
OWNERS = XROWS // ROWS
WIDE = HID + DH
KB = 256
QB = 256
BF, F32, I32 = jnp.bfloat16, jnp.float32, jnp.int32
NT = (((1,), (1,)), ((), ()))
VM = 56 * 1024 * 1024

SMEM = pl.BlockSpec(memory_space=pltpu.SMEM)
WHOLE = pl.BlockSpec(memory_space=pltpu.VMEM)
DEP = pl.BlockSpec(memory_space=pl.ANY)


def params():
    return pltpu.CompilerParams(vmem_limit_bytes=VM)


def mm(a, b):
    return jnp.dot(a, b, preferred_element_type=F32)


def sds(shape, dtype):
    return jax.ShapeDtypeStruct(shape, dtype)


SWAP_C = [(t, t ^ 1) for t in range(SHARDS)]
ALONG_Z = [
    [(x * ZS + z) * CS + c for z in range(ZS)] for x in range(XS) for c in range(CS)
]


def shift_x(d):
    return [(t, (t + d * ZS * CS) % SHARDS) for t in range(SHARDS)]


def shift_h(d):
    return [(h, (h + d) % HS) for h in range(HS)]


def full(shape):
    return pl.BlockSpec(shape, lambda i: (0,) * len(shape))


def keys_kernel(t_ref, w_ref, wr_ref, kv_ref, rates_ref):
    t = t_ref[...]
    kv_ref[...] = mm(t, w_ref[...]).astype(BF)
    raw = lax.dot_general(t, wr_ref[...], NT, preferred_element_type=F32)
    rates_ref[...] = (0.25 / math.sqrt(TOKENS)) * (
        jnp.maximum(raw, 0.0) + jnp.log1p(jnp.exp(-jnp.abs(raw)))
    )


def keys(tokens, qkv_weight, rate_weight):
    rows, wide = tokens.shape
    block = 512
    return pl.pallas_call(
        keys_kernel,
        grid=(rows // block,),
        in_specs=[
            pl.BlockSpec((block, wide), lambda i: (i, 0)),
            pl.BlockSpec((pl.Element(wide), pl.Element(2 * DH)), lambda i: (0, DH)),
            full((3, wide)),
        ],
        out_specs=[
            pl.BlockSpec((block, 2 * DH), lambda i: (i, 0)),
            pl.BlockSpec((block, 3), lambda i: (i, 0)),
        ],
        out_shape=[sds((rows, 2 * DH), BF), sds((rows, 3), F32)],
        compiler_params=params(),
        name="keys",
    )(tokens, qkv_weight, rate_weight.T)


def update_kernel(pos_ref, kv_ref, r_ref, w1_ref, w3_ref, w2_ref, send_ref, keep_ref, second):
    even = pos_ref[0] == 0
    k, v = kv_ref[:, :DH], kv_ref[:, DH:]
    r = r_ref[...]
    r1, r3 = r[:, 0:1], r[:, 1:2]
    k_t = k.T
    e2_t = (r[:, 2:3] * v.astype(F32)).astype(BF).T
    chunk = 256
    for j in range(HID // chunk):
        cols = slice(j * chunk, (j + 1) * chunk)
        a = mm(k, w1_ref[0, :, cols])
        b = mm(k, w3_ref[0, :, cols])
        back = lax.dot_general(v, w2_ref[0, cols, :], NT, preferred_element_type=F32)
        sig = jax.nn.sigmoid(a)
        act = a * sig
        z = (act * b).astype(BF)
        e1 = (r1 * back * b * (sig * (1.0 + a * (1.0 - sig)))).astype(BF)
        e3 = (r3 * back * act).astype(BF)
        first = mm(k_t, e1)
        gate = mm(k_t, e3)
        second[cols, :] = mm(e2_t, z).T
        keep_ref[:, cols] = jnp.where(even, first, gate)
        send_ref[:, cols] = jnp.where(even, gate, first).astype(BF)
    low, high = second[:DH, :], second[DH:, :]
    keep_ref[:, HID:] = jnp.where(even, low, high)
    send_ref[:, HID:] = jnp.where(even, high, low).astype(BF)


def update(pos, kv, rates, first_fast, gate_fast, second_fast):
    return pl.pallas_call(
        update_kernel,
        grid=(1,),
        in_specs=[
            SMEM,
            full(kv.shape),
            full(rates.shape),
            full((1, DH, HID)),
            full((1, DH, HID)),
            full((1, HID, DH)),
        ],
        out_specs=[full((DH, WIDE)), full((DH, WIDE))],
        out_shape=[sds((DH, WIDE), BF), sds((DH, WIDE), F32)],
        scratch_shapes=[pltpu.VMEM((HID, DH), F32)],
        compiler_params=params(),
        name="update",
    )(pos, kv, rates, first_fast, gate_fast, second_fast)


def rs_x_kernel(pos_ref, keep_ref, got_ref, *rest):
    outs = rest[-XS:]
    x = pos_ref[1]
    for d, out in enumerate(outs):
        rows = pl.ds(pl.multiple_of(lax.rem(x + d, XS) * XROWS, XROWS), XROWS)
        out[...] = (keep_ref[rows, :] + got_ref[rows, :].astype(F32)).astype(out.dtype)


def rs_x(pos, keep, got, deps):
    return pl.pallas_call(
        rs_x_kernel,
        grid=(1,),
        in_specs=[SMEM, full((DH, WIDE)), full((DH, WIDE))] + [DEP] * len(deps),
        out_specs=[full((XROWS, WIDE))] * XS,
        out_shape=[sds((XROWS, WIDE), F32)] + [sds((XROWS, WIDE), BF)] * (XS - 1),
        compiler_params=params(),
        name="rs_x",
    )(pos, keep, got, *deps)


def rs_z_kernel(own_ref, g1, g2, g3, *rest):
    out = rest[-1]
    for o in range(OWNERS):
        rows = slice(o * ROWS, (o + 1) * ROWS)
        total = (own_ref[rows, :] + g1[rows, :].astype(F32)) + (
            g2[rows, :].astype(F32) + g3[rows, :].astype(F32)
        )
        out[o] = total.astype(BF)
    out[OWNERS:] = jnp.zeros((ZS - OWNERS, ROWS, WIDE), BF)


def rs_z(own, got, deps):
    return pl.pallas_call(
        rs_z_kernel,
        grid=(1,),
        in_specs=[full((XROWS, WIDE))] * XS + [DEP] * len(deps),
        out_specs=full((ZS, ROWS, WIDE)),
        out_shape=sds((ZS, ROWS, WIDE), BF),
        compiler_params=params(),
        name="rs_z",
    )(own, *got, *deps)


def renorm_kernel(old_ref, got_ref, *rest):
    out = rest[-1]
    update = got_ref[0].astype(F32)
    for s in range(1, ZS):
        update = update + got_ref[s].astype(F32)
    old = old_ref[...]
    fresh = old + update
    for cols in (slice(0, HID), slice(HID, WIDE)):
        w, f = old[:, cols], fresh[:, cols]
        w_sq = jnp.sum(w * w, axis=1, keepdims=True)
        f_sq = jnp.sum(f * f, axis=1, keepdims=True)
        new = (f * (jnp.sqrt(w_sq) / jnp.sqrt(f_sq + 1e-6))).astype(BF)
        for s in range(ZS):
            out[s, :, cols] = new


def renorm(old, got, deps):
    shape = (ZS, ROWS, WIDE)
    return pl.pallas_call(
        renorm_kernel,
        grid=(1,),
        in_specs=[full((ROWS, WIDE)), full(shape)] + [DEP] * len(deps),
        out_specs=full(shape),
        out_shape=sds(shape, BF),
        compiler_params=params(),
        name="renorm",
    )(old, got, *deps)


def hold_kernel(value_ref, dep_ref, out_ref):
    pass


def hold(value, dep):
    return pl.pallas_call(
        hold_kernel,
        in_specs=[DEP, DEP],
        out_specs=DEP,
        out_shape=sds(value.shape, value.dtype),
        input_output_aliases={0: 0},
        compiler_params=params(),
        name="hold",
    )(value, dep)


def ag_x_kernel(pos_ref, *rest):
    blocks, out = rest[:XS], rest[-1]
    x = pos_ref[1]
    for d, block in enumerate(blocks):
        owner = lax.rem(x - d + XS, XS)
        out[pl.ds(pl.multiple_of(owner * XROWS, XROWS), XROWS), :] = block[...]


def ag_x(pos, blocks, deps):
    return pl.pallas_call(
        ag_x_kernel,
        grid=(1,),
        in_specs=[SMEM] + [full((XROWS, WIDE))] * XS + [DEP] * len(deps),
        out_specs=full((DH, WIDE)),
        out_shape=sds((DH, WIDE), BF),
        compiler_params=params(),
        name="ag_x",
    )(pos, *blocks, *deps)


def project_kernel(t_ref, w_ref, *rest):
    q_ref = rest[-1]
    q_ref[...] = mm(t_ref[...], w_ref[...]).astype(BF)


def project(tokens, qkv_weight, deps):
    rows, wide = tokens.shape
    block = 256
    return pl.pallas_call(
        project_kernel,
        grid=(rows // block,),
        in_specs=[
            pl.BlockSpec((block, wide), lambda i: (i, 0)),
            pl.BlockSpec((wide, DH), lambda i: (0, 0)),
        ]
        + [DEP] * len(deps),
        out_specs=pl.BlockSpec((block, DH), lambda i: (i, 0)),
        out_shape=sds((rows, DH), BF),
        compiler_params=params(),
        name="project",
    )(tokens, qkv_weight, *deps)


def attend_kernel(ahead, pos_ref, ends_ref, q_ref, before, mine, after, dep_ref, out_ref, s_ref):
    shard = pos_ref[3]
    piece = lax.rem(pos_ref[2] + ahead, HS)
    row = lax.broadcasted_iota(I32, (QB, 1), 0)
    place = row + (shard * TOK + piece * QB)
    ends = ends_ref[...]
    shift = (shard - 1) * TOK
    begin = jnp.max(jnp.where(ends <= place, ends, 0), axis=1, keepdims=True) - shift
    end = jnp.min(jnp.where(ends <= place, TOKENS, ends), axis=1, keepdims=True) - shift
    first = lax.div(jnp.min(begin), KB)
    last = lax.div(jnp.max(end) + KB - 1, KB)
    q = q_ref[pl.ds(pl.multiple_of(piece * QB, QB), QB), :]
    per = TOK // KB
    scale = 1.0 / math.sqrt(DH)

    def segments(step, carry):
        for s, ref in enumerate((before, mine, after)):
            lo = jnp.clip(first, s * per, (s + 1) * per)
            hi = jnp.clip(last, s * per, (s + 1) * per)
            carry = lax.fori_loop(lo, hi, functools.partial(step, s, ref), carry)
        return carry

    def scores(s, ref, kb, top):
        k = ref[pl.ds(pl.multiple_of((kb - s * per) * KB, KB), KB), :DH]
        sc = lax.dot_general(q, k, NT, preferred_element_type=F32) * scale
        col = lax.broadcasted_iota(I32, (QB, KB), 1) + kb * KB
        sc = jnp.where((col >= begin) & (col < end), sc, -1e30)
        s_ref[kb] = sc
        for lane in range(0, KB, 128):
            top = jnp.maximum(top, sc[:, lane : lane + 128])
        return top

    top = segments(scores, jnp.full((QB, 128), -1e30, F32))
    top = jnp.max(top, axis=1, keepdims=True)

    def weigh(kb, total):
        w = jnp.exp(s_ref[kb] - top)
        s_ref[kb] = w
        for lane in range(0, KB, 128):
            total = total + w[:, lane : lane + 128]
        return total

    total = lax.fori_loop(first, last, weigh, jnp.zeros((QB, 128), F32))
    inverse = 1.0 / jnp.sum(total, axis=1, keepdims=True)
    out_ref[...] = jnp.zeros_like(out_ref)

    def gather(s, ref, kb, carry):
        v = ref[pl.ds(pl.multiple_of((kb - s * per) * KB, KB), KB), DH:]
        probs = (s_ref[kb] * inverse).astype(BF)
        out_ref[...] += mm(probs, v)
        return carry

    segments(gather, 0)


def attend(ahead, pos, ends, query, before, mine, after, dep):
    whole = full((TOK, 2 * DH))
    return pl.pallas_call(
        functools.partial(attend_kernel, ahead),
        grid=(1,),
        in_specs=[SMEM, full(ends.shape), full((TOK, DH)), whole, whole, whole, DEP],
        out_specs=full((QB, DH)),
        out_shape=sds((QB, DH), F32),
        scratch_shapes=[pltpu.VMEM((3 * TOK // KB, QB, KB), F32)],
        compiler_params=params(),
        name=f"attend_{ahead}",
    )(pos, ends, query, before, mine, after, dep)


def apply_kernel(aheads, pos_ref, q_ref, own_ref, other_ref, gain_ref, *rest):
    count = len(aheads)
    attended, outs = rest[:count], rest[-count:]
    even = pos_ref[0] == 0
    for ahead, att_ref, out in zip(aheads, attended, outs):
        piece = lax.rem(pos_ref[2] + ahead, HS)
        q = q_ref[pl.ds(pl.multiple_of(piece * QB, QB), QB), :]
        mine = mm(q, own_ref[:, :HID])
        theirs = mm(q, other_ref[:, :HID])
        a = jnp.where(even, mine, theirs)
        b = jnp.where(even, theirs, mine)
        hidden = (a * jax.nn.sigmoid(a) * b).astype(BF)
        h0, h1 = hidden[:, :DH], hidden[:, DH:]
        h_own = jnp.where(even, h0, h1)
        h_other = jnp.where(even, h1, h0)
        applied = mm(h_own, own_ref[:, HID:]) + mm(h_other, other_ref[:, HID:])
        mean = jnp.mean(applied * applied, axis=1, keepdims=True)
        normed = applied * lax.rsqrt(mean + 1e-6) * gain_ref[...]
        out[...] = (att_ref[...] + normed).astype(BF)


def apply(aheads, pos, query, own, other, gain, attended, deps):
    count = len(aheads)
    return pl.pallas_call(
        functools.partial(apply_kernel, aheads),
        grid=(1,),
        in_specs=[SMEM, full((TOK, DH)), full((DH, WIDE)), full((DH, WIDE)), full((1, DH))]
        + [full((QB, DH))] * count
        + [DEP] * len(deps),
        out_specs=[full((QB, DH))] * count,
        out_shape=[sds((QB, DH), BF)] * count,
        compiler_params=params(),
        name=f"apply_{count}",
    )(pos, query, own, other, gain, *attended, *deps)


def output_kernel(pos_ref, *refs):
    parts, weights, outs = refs[:HS], refs[HS : 2 * HS], refs[2 * HS :]
    head = pos_ref[2]
    for e, out in enumerate(outs):
        cols = pl.ds(pl.multiple_of(lax.rem(head + e + 1, HS) * DH, DH), DH)
        total = mm(parts[0][...], weights[0][:, cols])
        for part, weight in zip(parts[1:], weights[1:]):
            total = total + mm(part[...], weight[:, cols])
        out[...] = total.astype(BF)


def output(pos, parts, weights):
    return pl.pallas_call(
        output_kernel,
        grid=(1,),
        in_specs=[SMEM] + [full((QB, DH))] * HS + [full((DH, HS * DH))] * HS,
        out_specs=[full((QB, DH))] * HS,
        out_shape=[sds((QB, DH), BF)] * HS,
        compiler_params=params(),
        name="output",
    )(pos, *parts, *weights)


def arrange_kernel(pos_ref, *refs):
    parts, out = refs[:-1], refs[-1]
    head = pos_ref[2]
    for d, part in enumerate(parts):
        rows = pl.ds(pl.multiple_of(lax.rem(head - d + HS, HS) * QB, QB), QB)
        out[rows, :] = part[...]


def arrange(pos, parts):
    return pl.pallas_call(
        arrange_kernel,
        grid=(1,),
        in_specs=[SMEM] + [full((QB, DH))] * HS,
        out_specs=full((TOK, DH)),
        out_shape=sds((TOK, DH), BF),
        compiler_params=params(),
        name="arrange",
    )(pos, *parts)


def body(
    tokens,
    qkv_weight,
    rate_weight,
    first_fast,
    gate_fast,
    second_fast,
    fast_gain,
    out_weight,
    frame_lengths,
):
    mine = lax.axis_index("tok")
    head = lax.axis_index("head")
    x, z, core = mine // (ZS * CS), mine // CS % ZS, mine % CS
    send = lambda value, pairs: lax.ppermute(value, "tok", pairs)

    kv, rates = keys(tokens, qkv_weight, rate_weight)
    up = [(i, i + 1) for i in range(SHARDS - 1)]
    before = send(kv, up)
    after = send(kv, [(j, i) for i, j in up])
    pos = jnp.stack([core, x, head, mine]).astype(I32)
    give, keep = update(pos, kv, rates, first_fast, gate_fast, second_fast)
    got = send(give, SWAP_C)

    order = jnp.arange(frame_lengths.shape[0], dtype=I32)
    ends = jnp.sum(
        jnp.where(order[:, None] <= order[None, :], frame_lengths[:, None], 0),
        axis=0,
        keepdims=True,
    )

    def spread(parts):
        return [lax.ppermute(p, "head", shift_h(d)) if d else p for d, p in enumerate(parts)]

    weights = spread([out_weight] * HS)

    row = jnp.minimum(x * XROWS + z * ROWS, DH - ROWS)
    pick = lambda w, at: lax.dynamic_slice_in_dim(w[0], at, ROWS, 0)
    old = jnp.concatenate(
        [
            jnp.where(core == 0, pick(first_fast, row), pick(gate_fast, row)),
            pick(second_fast, core * DH + row),
        ],
        axis=1,
    ).astype(F32)

    def exchange(blocks):
        return lax.all_to_all(blocks, "tok", 0, 0, axis_index_groups=ALONG_Z)

    query = project(tokens, qkv_weight, [give])
    own, *gives = rs_x(pos, keep, got, [before, after, query])
    got = [send(g, shift_x(d + 1)) for d, g in enumerate(gives)]
    att = functools.partial(attend, pos=pos, ends=ends, query=query, before=before, mine=kv, after=after)
    att0 = att(0, dep=own)
    total = rs_z(own, got, [att0, old])
    got = exchange(total)
    att1 = att(1, dep=total)
    fresh = renorm(old, got, [att1, weights[1], weights[3]])
    got = exchange(fresh)
    att2 = att(2, dep=fresh)
    block = hold(got, att2)[:OWNERS].reshape(XROWS, WIDE)
    att3 = att(3, dep=block)
    half = ag_x(pos, [block] + [send(block, shift_x(d)) for d in range(1, XS)], [att3, weights[2]])
    other = send(half, SWAP_C)

    mix = functools.partial(
        apply, pos=pos, query=query, own=half, other=other, gain=fast_gain[None, :]
    )
    away = mix((1, 2, 3), attended=[att1, att2, att3], deps=[])
    [home] = mix((0,), attended=[att0], deps=[away[0]])
    parts = spread([home, *away])
    ahead = output(pos, parts, weights)
    result = arrange(pos, spread([ahead[-1], *ahead[:-1]]))
    return result


def solution(mesh):
    placed = (
        P("tok", None),
        P(None, "head"),
        P(None, "head"),
        P("head", None, None),
        P("head", None, None),
        P("head", None, None),
        P("head"),
        P("head", None),
        P(),
    )
    return jax.shard_map(
        body, mesh=mesh, in_specs=placed, out_specs=P("tok", "head"), check_vma=False
    )
```

```python
import functools
import math

import jax
import jax.numpy as jnp
from jax import lax
from jax.experimental import pallas as pl
from jax.experimental.pallas import tpu as pltpu
from jax.sharding import PartitionSpec as P

DH = 384
HID = 768
TOK = 1024
XS, ZS, CS, HS = 4, 8, 2, 4
SHARDS = XS * ZS * CS
TOKENS = TOK * SHARDS
XROWS = DH // XS
ROWS = 16
OWNERS = XROWS // ROWS
WIDE = HID + DH
KB = 256
QB = 256
BF, F32, I32 = jnp.bfloat16, jnp.float32, jnp.int32
NT = (((1,), (1,)), ((), ()))
VM = 56 * 1024 * 1024

SMEM = pl.BlockSpec(memory_space=pltpu.SMEM)
WHOLE = pl.BlockSpec(memory_space=pltpu.VMEM)
DEP = pl.BlockSpec(memory_space=pl.ANY)


def params():
    return pltpu.CompilerParams(vmem_limit_bytes=VM)


def mm(a, b):
    return jnp.dot(a, b, preferred_element_type=F32)


def sds(shape, dtype):
    return jax.ShapeDtypeStruct(shape, dtype)


SWAP_C = [(t, t ^ 1) for t in range(SHARDS)]
ALONG_Z = [
    [(x * ZS + z) * CS + c for z in range(ZS)] for x in range(XS) for c in range(CS)
]


def shift_x(d):
    return [(t, (t + d * ZS * CS) % SHARDS) for t in range(SHARDS)]


def shift_h(d):
    return [(h, (h + d) % HS) for h in range(HS)]


def full(shape):
    return pl.BlockSpec(shape, lambda i: (0,) * len(shape))


def keys_kernel(t_ref, w_ref, wr_ref, kv_ref, rates_ref):
    t = t_ref[...]
    kv_ref[...] = mm(t, w_ref[...]).astype(BF)
    raw = lax.dot_general(t, wr_ref[...], NT, preferred_element_type=F32)
    rates_ref[...] = (0.25 / math.sqrt(TOKENS)) * (
        jnp.maximum(raw, 0.0) + jnp.log1p(jnp.exp(-jnp.abs(raw)))
    )


def keys(tokens, qkv_weight, rate_weight):
    rows, wide = tokens.shape
    block = 512
    return pl.pallas_call(
        keys_kernel,
        grid=(rows // block,),
        in_specs=[
            pl.BlockSpec((block, wide), lambda i: (i, 0)),
            pl.BlockSpec((pl.Element(wide), pl.Element(2 * DH)), lambda i: (0, DH)),
            full((3, wide)),
        ],
        out_specs=[
            pl.BlockSpec((block, 2 * DH), lambda i: (i, 0)),
            pl.BlockSpec((block, 3), lambda i: (i, 0)),
        ],
        out_shape=[sds((rows, 2 * DH), BF), sds((rows, 3), F32)],
        compiler_params=params(),
        name="keys",
    )(tokens, qkv_weight, rate_weight.T)


def update_kernel(pos_ref, kv_ref, r_ref, w1_ref, w3_ref, w2_ref, send_ref, keep_ref, second):
    even = pos_ref[0] == 0
    k, v = kv_ref[:, :DH], kv_ref[:, DH:]
    r = r_ref[...]
    r1, r3 = r[:, 0:1], r[:, 1:2]
    k_t = k.T
    e2_t = (r[:, 2:3] * v.astype(F32)).astype(BF).T
    chunk = 256
    for j in range(HID // chunk):
        cols = slice(j * chunk, (j + 1) * chunk)
        a = mm(k, w1_ref[0, :, cols])
        b = mm(k, w3_ref[0, :, cols])
        back = lax.dot_general(v, w2_ref[0, cols, :], NT, preferred_element_type=F32)
        sig = jax.nn.sigmoid(a)
        act = a * sig
        z = (act * b).astype(BF)
        e1 = (r1 * back * b * (sig * (1.0 + a * (1.0 - sig)))).astype(BF)
        e3 = (r3 * back * act).astype(BF)
        first = mm(k_t, e1)
        gate = mm(k_t, e3)
        second[cols, :] = mm(e2_t, z).T
        keep_ref[:, cols] = jnp.where(even, first, gate)
        send_ref[:, cols] = jnp.where(even, gate, first).astype(BF)
    low, high = second[:DH, :], second[DH:, :]
    keep_ref[:, HID:] = jnp.where(even, low, high)
    send_ref[:, HID:] = jnp.where(even, high, low).astype(BF)


def update(pos, kv, rates, first_fast, gate_fast, second_fast):
    return pl.pallas_call(
        update_kernel,
        grid=(1,),
        in_specs=[
            SMEM,
            full(kv.shape),
            full(rates.shape),
            full((1, DH, HID)),
            full((1, DH, HID)),
            full((1, HID, DH)),
        ],
        out_specs=[full((DH, WIDE)), full((DH, WIDE))],
        out_shape=[sds((DH, WIDE), BF), sds((DH, WIDE), F32)],
        scratch_shapes=[pltpu.VMEM((HID, DH), F32)],
        compiler_params=params(),
        name="update",
    )(pos, kv, rates, first_fast, gate_fast, second_fast)


def rs_x_kernel(pos_ref, keep_ref, got_ref, *rest):
    outs = rest[-XS:]
    x = pos_ref[1]
    for d, out in enumerate(outs):
        rows = pl.ds(pl.multiple_of(lax.rem(x + d, XS) * XROWS, XROWS), XROWS)
        out[...] = (keep_ref[rows, :] + got_ref[rows, :].astype(F32)).astype(out.dtype)


def rs_x(pos, keep, got, deps):
    return pl.pallas_call(
        rs_x_kernel,
        grid=(1,),
        in_specs=[SMEM, full((DH, WIDE)), full((DH, WIDE))] + [DEP] * len(deps),
        out_specs=[full((XROWS, WIDE))] * XS,
        out_shape=[sds((XROWS, WIDE), F32)] + [sds((XROWS, WIDE), BF)] * (XS - 1),
        compiler_params=params(),
        name="rs_x",
    )(pos, keep, got, *deps)


def rs_z_kernel(own_ref, g1, g2, g3, *rest):
    out = rest[-1]
    for o in range(OWNERS):
        rows = slice(o * ROWS, (o + 1) * ROWS)
        total = (own_ref[rows, :] + g1[rows, :].astype(F32)) + (
            g2[rows, :].astype(F32) + g3[rows, :].astype(F32)
        )
        out[o] = total.astype(BF)
    out[OWNERS:] = jnp.zeros((ZS - OWNERS, ROWS, WIDE), BF)


def rs_z(own, got, deps):
    return pl.pallas_call(
        rs_z_kernel,
        grid=(1,),
        in_specs=[full((XROWS, WIDE))] * XS + [DEP] * len(deps),
        out_specs=full((ZS, ROWS, WIDE)),
        out_shape=sds((ZS, ROWS, WIDE), BF),
        compiler_params=params(),
        name="rs_z",
    )(own, *got, *deps)


def renorm_kernel(old_ref, got_ref, *rest):
    out = rest[-1]
    update = got_ref[0].astype(F32)
    for s in range(1, ZS):
        update = update + got_ref[s].astype(F32)
    old = old_ref[...]
    fresh = old + update
    for cols in (slice(0, HID), slice(HID, WIDE)):
        w, f = old[:, cols], fresh[:, cols]
        w_sq = jnp.sum(w * w, axis=1, keepdims=True)
        f_sq = jnp.sum(f * f, axis=1, keepdims=True)
        new = (f * (jnp.sqrt(w_sq) / jnp.sqrt(f_sq + 1e-6))).astype(BF)
        for s in range(ZS):
            out[s, :, cols] = new


def renorm(old, got, deps):
    shape = (ZS, ROWS, WIDE)
    return pl.pallas_call(
        renorm_kernel,
        grid=(1,),
        in_specs=[full((ROWS, WIDE)), full(shape)] + [DEP] * len(deps),
        out_specs=full(shape),
        out_shape=sds(shape, BF),
        compiler_params=params(),
        name="renorm",
    )(old, got, *deps)


def hold_kernel(value_ref, *rest):
    pass


def hold(value, deps):
    return pl.pallas_call(
        hold_kernel,
        in_specs=[DEP] * (1 + len(deps)),
        out_specs=DEP,
        out_shape=sds(value.shape, value.dtype),
        input_output_aliases={0: 0},
        compiler_params=params(),
        name="hold",
    )(value, *deps)


def old_rows_kernel(pos_ref, w1_ref, w3_ref, w2_ref, dep_ref, out_ref):
    core, x, mine = pos_ref[0], pos_ref[1], pos_ref[3]
    z = lax.rem(lax.div(mine, CS), ZS)
    row = pl.multiple_of(jnp.minimum(x * XROWS + z * ROWS, DH - ROWS), ROWS)
    rows = pl.ds(row, ROWS)
    w1, w3 = w1_ref[0, rows, :].astype(F32), w3_ref[0, rows, :].astype(F32)
    out_ref[:, :HID] = jnp.where(core == 0, w1, w3)
    rows = pl.ds(pl.multiple_of(core * DH + row, ROWS), ROWS)
    out_ref[:, HID:] = w2_ref[0, rows, :].astype(F32)


def old_rows(pos, first_fast, gate_fast, second_fast, dep):
    return pl.pallas_call(
        old_rows_kernel,
        grid=(1,),
        in_specs=[SMEM, full((1, DH, HID)), full((1, DH, HID)), full((1, HID, DH)), DEP],
        out_specs=full((ROWS, WIDE)),
        out_shape=sds((ROWS, WIDE), F32),
        compiler_params=params(),
        name="old_rows",
    )(pos, first_fast, gate_fast, second_fast, dep)


def project_kernel(t_ref, w_ref, *rest):
    q_ref = rest[-1]
    q_ref[...] = mm(t_ref[...], w_ref[...]).astype(BF)


def project(tokens, qkv_weight, deps):
    rows, wide = tokens.shape
    block = 256
    return pl.pallas_call(
        project_kernel,
        grid=(rows // block,),
        in_specs=[
            pl.BlockSpec((block, wide), lambda i: (i, 0)),
            pl.BlockSpec((wide, DH), lambda i: (0, 0)),
        ]
        + [DEP] * len(deps),
        out_specs=pl.BlockSpec((block, DH), lambda i: (i, 0)),
        out_shape=sds((rows, DH), BF),
        compiler_params=params(),
        name="project",
    )(tokens, qkv_weight, *deps)


def attend_kernel(ahead, pos_ref, lengths_ref, q_ref, before, mine, after, dep_ref, out_ref, s_ref):
    shard = pos_ref[3]
    piece = lax.rem(pos_ref[2] + ahead, HS)
    row = lax.broadcasted_iota(I32, (QB, 1), 0)
    place = row + (shard * TOK + piece * QB)
    lengths = lengths_ref[...].astype(F32)
    count = lengths.shape[1]
    down = jnp.broadcast_to(lengths, (count, count)).T
    upper = lax.broadcasted_iota(I32, (count, count), 0) <= lax.broadcasted_iota(
        I32, (count, count), 1
    )
    ends = jnp.sum(jnp.where(upper, down, 0.0), axis=0, keepdims=True).astype(I32)
    shift = (shard - 1) * TOK
    begin = jnp.max(jnp.where(ends <= place, ends, 0), axis=1, keepdims=True) - shift
    end = jnp.min(jnp.where(ends <= place, TOKENS, ends), axis=1, keepdims=True) - shift
    first = lax.div(jnp.min(begin), KB)
    last = lax.div(jnp.max(end) + KB - 1, KB)
    q = q_ref[pl.ds(pl.multiple_of(piece * QB, QB), QB), :]
    per = TOK // KB
    scale = 1.0 / math.sqrt(DH)

    def segments(step, carry):
        for s, ref in enumerate((before, mine, after)):
            lo = jnp.clip(first, s * per, (s + 1) * per)
            hi = jnp.clip(last, s * per, (s + 1) * per)
            carry = lax.fori_loop(lo, hi, functools.partial(step, s, ref), carry)
        return carry

    def scores(s, ref, kb, top):
        k = ref[pl.ds(pl.multiple_of((kb - s * per) * KB, KB), KB), :DH]
        sc = lax.dot_general(q, k, NT, preferred_element_type=F32) * scale
        col = lax.broadcasted_iota(I32, (QB, KB), 1) + kb * KB
        sc = jnp.where((col >= begin) & (col < end), sc, -1e30)
        s_ref[kb] = sc
        for lane in range(0, KB, 128):
            top = jnp.maximum(top, sc[:, lane : lane + 128])
        return top

    top = segments(scores, jnp.full((QB, 128), -1e30, F32))
    top = jnp.max(top, axis=1, keepdims=True)

    def weigh(kb, total):
        w = jnp.exp(s_ref[kb] - top)
        s_ref[kb] = w
        for lane in range(0, KB, 128):
            total = total + w[:, lane : lane + 128]
        return total

    total = lax.fori_loop(first, last, weigh, jnp.zeros((QB, 128), F32))
    inverse = 1.0 / jnp.sum(total, axis=1, keepdims=True)
    out_ref[...] = jnp.zeros_like(out_ref)

    def gather(s, ref, kb, carry):
        v = ref[pl.ds(pl.multiple_of((kb - s * per) * KB, KB), KB), DH:]
        probs = (s_ref[kb] * inverse).astype(BF)
        out_ref[...] += mm(probs, v)
        return carry

    segments(gather, 0)


def attend(ahead, pos, lengths, query, before, mine, after, dep):
    whole = full((TOK, 2 * DH))
    return pl.pallas_call(
        functools.partial(attend_kernel, ahead),
        grid=(1,),
        in_specs=[SMEM, full(lengths.shape), full((TOK, DH)), whole, whole, whole, DEP],
        out_specs=full((QB, DH)),
        out_shape=sds((QB, DH), F32),
        scratch_shapes=[pltpu.VMEM((3 * TOK // KB, QB, KB), F32)],
        compiler_params=params(),
        name=f"attend_{ahead}",
    )(pos, lengths, query, before, mine, after, dep)


def apply_kernel(aheads, pos_ref, q_ref, gain_ref, *rest):
    count = len(aheads)
    own_ref, other_ref = rest[-2:]
    attended, outs = rest[2 * XS : 2 * XS + count], rest[-count - 2 : -2]
    for d in range(XS):
        at = lax.rem(pos_ref[1] - d + XS, XS) * XROWS
        rows = pl.ds(pl.multiple_of(at, XROWS), XROWS)
        own_ref[rows, :] = rest[d][...]
        other_ref[rows, :] = rest[XS + d][...]
    even = pos_ref[0] == 0
    for ahead, att_ref, out in zip(aheads, attended, outs):
        piece = lax.rem(pos_ref[2] + ahead, HS)
        q = q_ref[pl.ds(pl.multiple_of(piece * QB, QB), QB), :]
        mine = mm(q, own_ref[:, :HID])
        theirs = mm(q, other_ref[:, :HID])
        a = jnp.where(even, mine, theirs)
        b = jnp.where(even, theirs, mine)
        hidden = (a * jax.nn.sigmoid(a) * b).astype(BF)
        h0, h1 = hidden[:, :DH], hidden[:, DH:]
        h_own = jnp.where(even, h0, h1)
        h_other = jnp.where(even, h1, h0)
        applied = mm(h_own, own_ref[:, HID:]) + mm(h_other, other_ref[:, HID:])
        mean = jnp.mean(applied * applied, axis=1, keepdims=True)
        normed = applied * lax.rsqrt(mean + 1e-6) * gain_ref[...]
        out[...] = (att_ref[...] + normed).astype(BF)


def apply(aheads, pos, query, gain, own, other, attended, deps):
    count = len(aheads)
    return pl.pallas_call(
        functools.partial(apply_kernel, aheads),
        grid=(1,),
        in_specs=[SMEM, full((TOK, DH)), full((1, DH))]
        + [full((XROWS, WIDE))] * (2 * XS)
        + [full((QB, DH))] * count
        + [DEP] * len(deps),
        out_specs=[full((QB, DH))] * count,
        out_shape=[sds((QB, DH), BF)] * count,
        scratch_shapes=[pltpu.VMEM((DH, WIDE), BF)] * 2,
        compiler_params=params(),
        name=f"apply_{count}",
    )(pos, query, gain, *own, *other, *attended, *deps)


def output_kernel(pos_ref, *refs):
    parts, weights, outs = refs[:HS], refs[HS : 2 * HS], refs[2 * HS :]
    head = pos_ref[2]
    for e, out in enumerate(outs):
        cols = pl.ds(pl.multiple_of(lax.rem(head + e + 1, HS) * DH, DH), DH)
        total = mm(parts[0][...], weights[0][:, cols])
        for part, weight in zip(parts[1:], weights[1:]):
            total = total + mm(part[...], weight[:, cols])
        out[...] = total.astype(BF)


def output(pos, parts, weights):
    return pl.pallas_call(
        output_kernel,
        grid=(1,),
        in_specs=[SMEM] + [full((QB, DH))] * HS + [full((DH, HS * DH))] * HS,
        out_specs=[full((QB, DH))] * HS,
        out_shape=[sds((QB, DH), BF)] * HS,
        compiler_params=params(),
        name="output",
    )(pos, *parts, *weights)


def arrange_kernel(pos_ref, *refs):
    parts, out = refs[:-1], refs[-1]
    head = pos_ref[2]
    for d, part in enumerate(parts):
        rows = pl.ds(pl.multiple_of(lax.rem(head - d + HS, HS) * QB, QB), QB)
        out[rows, :] = part[...]


def arrange(pos, parts):
    return pl.pallas_call(
        arrange_kernel,
        grid=(1,),
        in_specs=[SMEM] + [full((QB, DH))] * HS,
        out_specs=full((TOK, DH)),
        out_shape=sds((TOK, DH), BF),
        compiler_params=params(),
        name="arrange",
    )(pos, *parts)


def body(
    tokens,
    qkv_weight,
    rate_weight,
    first_fast,
    gate_fast,
    second_fast,
    fast_gain,
    out_weight,
    frame_lengths,
):
    mine = lax.axis_index("tok")
    head = lax.axis_index("head")
    x, core = mine // (ZS * CS), mine % CS
    send = lambda value, pairs: lax.ppermute(value, "tok", pairs)

    kv, rates = keys(tokens, qkv_weight, rate_weight)
    up = [(i, i + 1) for i in range(SHARDS - 1)]
    before = send(kv, up)
    after = send(kv, [(j, i) for i, j in up])
    pos = jnp.stack([core, x, head, mine]).astype(I32)
    give, keep = update(pos, kv, rates, first_fast, gate_fast, second_fast)
    got = send(give, SWAP_C)

    def spread(parts):
        return [lax.ppermute(p, "head", shift_h(d)) if d else p for d, p in enumerate(parts)]

    weights = spread([out_weight] * HS)

    def exchange(blocks):
        return lax.all_to_all(blocks, "tok", 0, 0, axis_index_groups=ALONG_Z)

    query = project(tokens, qkv_weight, [give])
    own, *gives = rs_x(pos, keep, got, [before, after, query])
    got = [send(g, shift_x(d + 1)) for d, g in enumerate(gives)]
    att = functools.partial(attend, pos=pos, lengths=frame_lengths[None, :], query=query, before=before, mine=kv, after=after)
    att0 = att(0, dep=own)
    old = old_rows(pos, first_fast, gate_fast, second_fast, own)
    total = rs_z(own, got, [att0, old])
    got = exchange(total)
    att1 = att(1, dep=total)
    fresh = renorm(old, got, [att1])
    got = exchange(fresh)
    att2 = att(2, dep=fresh)
    block = hold(got, [att2, weights[1], weights[3]])[:OWNERS].reshape(XROWS, WIDE)
    att3 = att(3, dep=block)
    near, *far = [send(block, shift_x(d)) for d in range(1, XS)]
    blocks = [block, hold(near, [att3]), *far]
    others = [send(b, SWAP_C) for b in blocks]

    mix = functools.partial(
        apply, pos=pos, query=query, gain=fast_gain[None, :], own=blocks, other=others
    )
    away = mix((1, 2, 3), attended=[att1, att2, att3], deps=[])
    [home] = mix((0,), attended=[att0], deps=[away[0]])
    parts = spread([home, *away])
    ahead = output(pos, parts, weights)
    result = arrange(pos, spread([ahead[-1], *ahead[:-1]]))
    return result


def solution(mesh):
    placed = (
        P("tok", None),
        P(None, "head"),
        P(None, "head"),
        P("head", None, None),
        P("head", None, None),
        P("head", None, None),
        P("head"),
        P("head", None),
        P(),
    )
    return jax.shard_map(
        body, mesh=mesh, in_specs=placed, out_specs=P("tok", "head"), check_vma=False
    )
```

```python
import functools
import math

import jax
import jax.numpy as jnp
from jax import lax
from jax.experimental import pallas as pl
from jax.experimental.pallas import tpu as pltpu
from jax.sharding import PartitionSpec as P

DH = 384
HID = 768
TOK = 1024
XS, ZS, CS, HS = 4, 8, 2, 4
SHARDS = XS * ZS * CS
TOKENS = TOK * SHARDS
XROWS = DH // XS
ROWS = 16
OWNERS = XROWS // ROWS
WIDE = HID + DH
KB = 512
QB = 256
BF, F32, I32 = jnp.bfloat16, jnp.float32, jnp.int32
NT = (((1,), (1,)), ((), ()))
VM = 56 * 1024 * 1024

SMEM = pl.BlockSpec(memory_space=pltpu.SMEM)
WHOLE = pl.BlockSpec(memory_space=pltpu.VMEM)
DEP = pl.BlockSpec(memory_space=pl.ANY)


def params():
    return pltpu.CompilerParams(vmem_limit_bytes=VM)


def mm(a, b):
    return jnp.dot(a, b, preferred_element_type=F32)


def sds(shape, dtype):
    return jax.ShapeDtypeStruct(shape, dtype)


SWAP_C = [(t, t ^ 1) for t in range(SHARDS)]
ALONG_Z = [
    [(x * ZS + z) * CS + c for z in range(ZS)] for x in range(XS) for c in range(CS)
]


def shift_x(d):
    return [(t, (t + d * ZS * CS) % SHARDS) for t in range(SHARDS)]


def shift_h(d):
    return [(h, (h + d) % HS) for h in range(HS)]


def full(shape):
    return pl.BlockSpec(shape, lambda i: (0,) * len(shape))


def keys_kernel(t_ref, w_ref, wr_ref, kv_ref, rates_ref):
    t = t_ref[...]
    kv_ref[...] = mm(t, w_ref[...]).astype(BF)
    raw = lax.dot_general(t, wr_ref[...], NT, preferred_element_type=F32)
    rates_ref[...] = (0.25 / math.sqrt(TOKENS)) * (
        jnp.maximum(raw, 0.0) + jnp.log1p(jnp.exp(-jnp.abs(raw)))
    )


def keys(tokens, qkv_weight, rate_weight):
    rows, wide = tokens.shape
    block = 512
    return pl.pallas_call(
        keys_kernel,
        grid=(rows // block,),
        in_specs=[
            pl.BlockSpec((block, wide), lambda i: (i, 0)),
            pl.BlockSpec((pl.Element(wide), pl.Element(2 * DH)), lambda i: (0, DH)),
            full((3, wide)),
        ],
        out_specs=[
            pl.BlockSpec((block, 2 * DH), lambda i: (i, 0)),
            pl.BlockSpec((block, 3), lambda i: (i, 0)),
        ],
        out_shape=[sds((rows, 2 * DH), BF), sds((rows, 3), F32)],
        compiler_params=params(),
        name="keys",
    )(tokens, qkv_weight, rate_weight.T)


def update_kernel(pos_ref, kv_ref, r_ref, w1_ref, w3_ref, w2_ref, send_ref, keep_ref, second):
    even = pos_ref[0] == 0
    k, v = kv_ref[:, :DH], kv_ref[:, DH:]
    r = r_ref[...]
    r1, r3 = r[:, 0:1], r[:, 1:2]
    k_t = k.T
    e2_t = (r[:, 2:3] * v.astype(F32)).astype(BF).T
    chunk = 256
    for j in range(HID // chunk):
        cols = slice(j * chunk, (j + 1) * chunk)
        a = mm(k, w1_ref[0, :, cols])
        b = mm(k, w3_ref[0, :, cols])
        back = lax.dot_general(v, w2_ref[0, cols, :], NT, preferred_element_type=F32)
        sig = jax.nn.sigmoid(a)
        act = a * sig
        z = (act * b).astype(BF)
        e1 = (r1 * back * b * (sig * (1.0 + a * (1.0 - sig)))).astype(BF)
        e3 = (r3 * back * act).astype(BF)
        first = mm(k_t, e1)
        gate = mm(k_t, e3)
        second[cols, :] = mm(e2_t, z).T
        keep_ref[:, cols] = jnp.where(even, first, gate)
        send_ref[:, cols] = jnp.where(even, gate, first).astype(BF)
    low, high = second[:DH, :], second[DH:, :]
    keep_ref[:, HID:] = jnp.where(even, low, high)
    send_ref[:, HID:] = jnp.where(even, high, low).astype(BF)


def update(pos, kv, rates, first_fast, gate_fast, second_fast):
    return pl.pallas_call(
        update_kernel,
        grid=(1,),
        in_specs=[
            SMEM,
            full(kv.shape),
            full(rates.shape),
            full((1, DH, HID)),
            full((1, DH, HID)),
            full((1, HID, DH)),
        ],
        out_specs=[full((DH, WIDE)), full((DH, WIDE))],
        out_shape=[sds((DH, WIDE), BF), sds((DH, WIDE), F32)],
        scratch_shapes=[pltpu.VMEM((HID, DH), F32)],
        compiler_params=params(),
        name="update",
    )(pos, kv, rates, first_fast, gate_fast, second_fast)


def rs_x_kernel(pos_ref, keep_ref, got_ref, *rest):
    outs = rest[-XS:]
    x = pos_ref[1]
    for d, out in enumerate(outs):
        rows = pl.ds(pl.multiple_of(lax.rem(x + d, XS) * XROWS, XROWS), XROWS)
        out[...] = (keep_ref[rows, :] + got_ref[rows, :].astype(F32)).astype(out.dtype)


def rs_x(pos, keep, got, deps):
    return pl.pallas_call(
        rs_x_kernel,
        grid=(1,),
        in_specs=[SMEM, full((DH, WIDE)), full((DH, WIDE))] + [DEP] * len(deps),
        out_specs=[full((XROWS, WIDE))] * XS,
        out_shape=[sds((XROWS, WIDE), F32)] + [sds((XROWS, WIDE), BF)] * (XS - 1),
        compiler_params=params(),
        name="rs_x",
    )(pos, keep, got, *deps)


def rs_z_kernel(own_ref, g1, g2, g3, *rest):
    out = rest[-1]
    for o in range(OWNERS):
        rows = slice(o * ROWS, (o + 1) * ROWS)
        total = (own_ref[rows, :] + g1[rows, :].astype(F32)) + (
            g2[rows, :].astype(F32) + g3[rows, :].astype(F32)
        )
        out[o] = total.astype(BF)
    out[OWNERS:] = jnp.zeros((ZS - OWNERS, ROWS, WIDE), BF)


def rs_z(own, got, deps):
    return pl.pallas_call(
        rs_z_kernel,
        grid=(1,),
        in_specs=[full((XROWS, WIDE))] * XS + [DEP] * len(deps),
        out_specs=full((ZS, ROWS, WIDE)),
        out_shape=sds((ZS, ROWS, WIDE), BF),
        compiler_params=params(),
        name="rs_z",
    )(own, *got, *deps)


def renorm_kernel(old_ref, got_ref, *rest):
    out = rest[-1]
    update = got_ref[0].astype(F32)
    for s in range(1, ZS):
        update = update + got_ref[s].astype(F32)
    old = old_ref[...]
    fresh = old + update
    for cols in (slice(0, HID), slice(HID, WIDE)):
        w, f = old[:, cols], fresh[:, cols]
        w_sq = jnp.sum(w * w, axis=1, keepdims=True)
        f_sq = jnp.sum(f * f, axis=1, keepdims=True)
        new = (f * (jnp.sqrt(w_sq) / jnp.sqrt(f_sq + 1e-6))).astype(BF)
        for s in range(ZS):
            out[s, :, cols] = new


def renorm(old, got, deps):
    shape = (ZS, ROWS, WIDE)
    return pl.pallas_call(
        renorm_kernel,
        grid=(1,),
        in_specs=[full((ROWS, WIDE)), full(shape)] + [DEP] * len(deps),
        out_specs=full(shape),
        out_shape=sds(shape, BF),
        compiler_params=params(),
        name="renorm",
    )(old, got, *deps)


def hold_kernel(value_ref, *rest):
    pass


def hold(value, deps):
    return pl.pallas_call(
        hold_kernel,
        in_specs=[DEP] * (1 + len(deps)),
        out_specs=DEP,
        out_shape=sds(value.shape, value.dtype),
        input_output_aliases={0: 0},
        compiler_params=params(),
        name="hold",
    )(value, *deps)


def project_kernel(t_ref, w_ref, *rest):
    q_ref = rest[-1]
    q_ref[...] = mm(t_ref[...], w_ref[...]).astype(BF)


def project(tokens, qkv_weight, deps):
    rows, wide = tokens.shape
    block = 256
    return pl.pallas_call(
        project_kernel,
        grid=(rows // block,),
        in_specs=[
            pl.BlockSpec((block, wide), lambda i: (i, 0)),
            pl.BlockSpec((wide, DH), lambda i: (0, 0)),
        ]
        + [DEP] * len(deps),
        out_specs=pl.BlockSpec((block, DH), lambda i: (i, 0)),
        out_shape=sds((rows, DH), BF),
        compiler_params=params(),
        name="project",
    )(tokens, qkv_weight, *deps)


def attend_kernel(
    ahead, pos_ref, lengths_ref, q_all, before, mine, after, dep_ref,
    out_ref, s_ref, kv_ref, q_ref, sems, q_sem,
):
    shard = pos_ref[3]
    piece = lax.rem(pos_ref[2] + ahead, HS)
    q_rows = pl.ds(pl.multiple_of(piece * QB, QB), QB)
    q_copy = pltpu.make_async_copy(q_all.at[q_rows, :], q_ref, q_sem)
    q_copy.start()
    row = lax.broadcasted_iota(I32, (QB, 1), 0)
    place = row + (shard * TOK + piece * QB)
    lengths = lengths_ref[...].astype(F32)
    count = lengths.shape[1]
    down = jnp.broadcast_to(lengths, (count, count)).T
    upper = lax.broadcasted_iota(I32, (count, count), 0) <= lax.broadcasted_iota(
        I32, (count, count), 1
    )
    ends = jnp.sum(jnp.where(upper, down, 0.0), axis=0, keepdims=True).astype(I32)
    shift = (shard - 1) * TOK
    begin = jnp.max(jnp.where(ends <= place, ends, 0), axis=1, keepdims=True) - shift
    end = jnp.min(jnp.where(ends <= place, TOKENS, ends), axis=1, keepdims=True) - shift
    first = lax.div(jnp.min(begin), KB)
    last = lax.div(jnp.max(end) + KB - 1, KB)
    per = TOK // KB
    scale = 1.0 / math.sqrt(DH)

    def fetch(ref, at, kb):
        rows = pl.ds(pl.multiple_of(at * KB, KB), KB)
        return pltpu.make_async_copy(ref.at[rows, :], kv_ref.at[kb], sems.at[kb])

    for s, ref in enumerate((before, mine, after)):

        def start(kb, carry, s=s, ref=ref):
            fetch(ref, kb - s * per, kb).start()
            return carry

        lo = jnp.clip(first, s * per, (s + 1) * per)
        hi = jnp.clip(last, s * per, (s + 1) * per)
        lax.fori_loop(lo, hi, start, 0)
    q_copy.wait()
    q = q_ref[...]

    def scores(kb, top):
        fetch(mine, 0, kb).wait()
        k = kv_ref[kb, :, :DH]
        sc = lax.dot_general(q, k, NT, preferred_element_type=F32) * scale
        col = lax.broadcasted_iota(I32, (QB, KB), 1) + kb * KB
        sc = jnp.where((col >= begin) & (col < end), sc, -1e30)
        s_ref[kb] = sc
        for lane in range(0, KB, 128):
            top = jnp.maximum(top, sc[:, lane : lane + 128])
        return top

    top = lax.fori_loop(first, last, scores, jnp.full((QB, 128), -1e30, F32))
    top = jnp.max(top, axis=1, keepdims=True)

    def weigh(kb, total):
        w = jnp.exp(s_ref[kb] - top)
        s_ref[kb] = w
        for lane in range(0, KB, 128):
            total = total + w[:, lane : lane + 128]
        return total

    total = lax.fori_loop(first, last, weigh, jnp.zeros((QB, 128), F32))
    inverse = 1.0 / jnp.sum(total, axis=1, keepdims=True)
    out_ref[...] = jnp.zeros_like(out_ref)

    def gather(kb, carry):
        probs = (s_ref[kb] * inverse).astype(BF)
        out_ref[...] += mm(probs, kv_ref[kb, :, DH:])
        return carry

    lax.fori_loop(first, last, gather, 0)


def first_kernel(pos_ref, w1_ref, w3_ref, w2_ref, *rest):
    ins, outs, (wide, narrow, row_sems), scratch = rest[:7], rest[7:9], rest[9:12], rest[12:]
    core, x, mine = pos_ref[0], pos_ref[1], pos_ref[3]
    z = lax.rem(lax.div(mine, CS), ZS)
    row = pl.multiple_of(jnp.minimum(x * XROWS + z * ROWS, DH - ROWS), ROWS)
    rows = pl.ds(row, ROWS)
    rows2 = pl.ds(pl.multiple_of(core * DH + row, ROWS), ROWS)
    copies = [
        pltpu.make_async_copy(w1_ref.at[0, rows, :], wide.at[0], row_sems.at[0]),
        pltpu.make_async_copy(w3_ref.at[0, rows, :], wide.at[1], row_sems.at[1]),
        pltpu.make_async_copy(w2_ref.at[0, rows2, :], narrow, row_sems.at[2]),
    ]
    for copy in copies:
        copy.start()
    attend_kernel(0, pos_ref, *ins[1:], outs[0], *scratch)
    for copy in copies:
        copy.wait()
    out_ref = outs[1]
    out_ref[:, :HID] = jnp.where(core == 0, wide[0].astype(F32), wide[1].astype(F32))
    out_ref[:, HID:] = narrow[...].astype(F32)


def attend(ahead, pos, lengths, query, before, mine, after, dep, old=()):
    blocks = 3 * TOK // KB
    kernel = functools.partial(attend_kernel, ahead)
    outs, shapes, scratch, lead = [full((QB, DH))], [sds((QB, DH), F32)], [], ()
    if old:
        kernel = first_kernel
        outs = outs + [full((ROWS, WIDE))]
        shapes = shapes + [sds((ROWS, WIDE), F32)]
        scratch = [
            pltpu.VMEM((2, ROWS, HID), BF),
            pltpu.VMEM((ROWS, DH), BF),
            pltpu.SemaphoreType.DMA((3,)),
        ]
        lead = (pos, *old)
    result = pl.pallas_call(
        kernel,
        grid=(1,),
        in_specs=([SMEM] + [DEP] * 3 if old else [])
        + [SMEM, full(lengths.shape)]
        + [DEP] * 5,
        out_specs=outs,
        out_shape=shapes,
        scratch_shapes=scratch
        + [
            pltpu.VMEM((blocks, QB, KB), F32),
            pltpu.VMEM((blocks, KB, 2 * DH), BF),
            pltpu.VMEM((QB, DH), BF),
            pltpu.SemaphoreType.DMA((blocks,)),
            pltpu.SemaphoreType.DMA,
        ],
        compiler_params=params(),
        name=f"attend_{ahead}",
    )(*lead, pos, lengths, query, before, mine, after, dep)
    return result if old else result[0]


def apply_kernel(aheads, pos_ref, q_ref, gain_ref, *rest):
    count = len(aheads)
    own_ref, other_ref = rest[-2:]
    attended, outs = rest[2 * XS : 2 * XS + count], rest[-count - 2 : -2]
    for d in range(XS):
        at = lax.rem(pos_ref[1] - d + XS, XS) * XROWS
        rows = pl.ds(pl.multiple_of(at, XROWS), XROWS)
        own_ref[rows, :] = rest[d][...]
        other_ref[rows, :] = rest[XS + d][...]
    even = pos_ref[0] == 0
    for ahead, att_ref, out in zip(aheads, attended, outs):
        piece = lax.rem(pos_ref[2] + ahead, HS)
        q = q_ref[pl.ds(pl.multiple_of(piece * QB, QB), QB), :]
        mine = mm(q, own_ref[:, :HID])
        theirs = mm(q, other_ref[:, :HID])
        a = jnp.where(even, mine, theirs)
        b = jnp.where(even, theirs, mine)
        hidden = (a * jax.nn.sigmoid(a) * b).astype(BF)
        h0, h1 = hidden[:, :DH], hidden[:, DH:]
        h_own = jnp.where(even, h0, h1)
        h_other = jnp.where(even, h1, h0)
        applied = mm(h_own, own_ref[:, HID:]) + mm(h_other, other_ref[:, HID:])
        mean = jnp.mean(applied * applied, axis=1, keepdims=True)
        normed = applied * lax.rsqrt(mean + 1e-6) * gain_ref[...]
        out[...] = (att_ref[...] + normed).astype(BF)


def apply(aheads, pos, query, gain, own, other, attended, deps):
    count = len(aheads)
    return pl.pallas_call(
        functools.partial(apply_kernel, aheads),
        grid=(1,),
        in_specs=[SMEM, full((TOK, DH)), full((1, DH))]
        + [full((XROWS, WIDE))] * (2 * XS)
        + [full((QB, DH))] * count
        + [DEP] * len(deps),
        out_specs=[full((QB, DH))] * count,
        out_shape=[sds((QB, DH), BF)] * count,
        scratch_shapes=[pltpu.VMEM((DH, WIDE), BF)] * 2,
        compiler_params=params(),
        name=f"apply_{count}",
    )(pos, query, gain, *own, *other, *attended, *deps)


def output_kernel(pos_ref, *refs):
    parts, weights, outs = refs[:HS], refs[HS : 2 * HS], refs[2 * HS :]
    head = pos_ref[2]
    for e, out in enumerate(outs):
        cols = pl.ds(pl.multiple_of(lax.rem(head + e + 1, HS) * DH, DH), DH)
        total = mm(parts[0][...], weights[0][:, cols])
        for part, weight in zip(parts[1:], weights[1:]):
            total = total + mm(part[...], weight[:, cols])
        out[...] = total.astype(BF)


def output(pos, parts, weights):
    return pl.pallas_call(
        output_kernel,
        grid=(1,),
        in_specs=[SMEM] + [full((QB, DH))] * HS + [full((DH, HS * DH))] * HS,
        out_specs=[full((QB, DH))] * HS,
        out_shape=[sds((QB, DH), BF)] * HS,
        compiler_params=params(),
        name="output",
    )(pos, *parts, *weights)


def arrange_kernel(pos_ref, *refs):
    parts, out = refs[:-1], refs[-1]
    head = pos_ref[2]
    for d, part in enumerate(parts):
        rows = pl.ds(pl.multiple_of(lax.rem(head - d + HS, HS) * QB, QB), QB)
        out[rows, :] = part[...]


def arrange(pos, parts):
    return pl.pallas_call(
        arrange_kernel,
        grid=(1,),
        in_specs=[SMEM] + [full((QB, DH))] * HS,
        out_specs=full((TOK, DH)),
        out_shape=sds((TOK, DH), BF),
        compiler_params=params(),
        name="arrange",
    )(pos, *parts)


def body(
    tokens,
    qkv_weight,
    rate_weight,
    first_fast,
    gate_fast,
    second_fast,
    fast_gain,
    out_weight,
    frame_lengths,
):
    mine = lax.axis_index("tok")
    head = lax.axis_index("head")
    x, core = mine // (ZS * CS), mine % CS
    send = lambda value, pairs: lax.ppermute(value, "tok", pairs)

    kv, rates = keys(tokens, qkv_weight, rate_weight)
    up = [(i, i + 1) for i in range(SHARDS - 1)]
    before = send(kv, up)
    after = send(kv, [(j, i) for i, j in up])
    pos = jnp.stack([core, x, head, mine]).astype(I32)
    give, keep = update(pos, kv, rates, first_fast, gate_fast, second_fast)
    got = send(give, SWAP_C)

    def spread(parts):
        return [lax.ppermute(p, "head", shift_h(d)) if d else p for d, p in enumerate(parts)]

    weights = spread([out_weight] * HS)

    def exchange(blocks):
        return lax.all_to_all(blocks, "tok", 0, 0, axis_index_groups=ALONG_Z)

    query = project(tokens, qkv_weight, [give])
    own, *gives = rs_x(pos, keep, got, [before, after, query])
    got = [send(g, shift_x(d + 1)) for d, g in enumerate(gives)]
    att = functools.partial(attend, pos=pos, lengths=frame_lengths[None, :], query=query, before=before, mine=kv, after=after)
    att0, old = att(0, dep=own, old=(first_fast, gate_fast, second_fast))
    total = rs_z(own, got, [att0, old])
    got = exchange(total)
    att1 = att(1, dep=total)
    fresh = renorm(old, got, [att1])
    got = exchange(fresh)
    att2 = att(2, dep=fresh)
    block = hold(got, [att2, weights[1], weights[3]])[:OWNERS].reshape(XROWS, WIDE)
    att3 = att(3, dep=block)
    near, *far = [send(block, shift_x(d)) for d in range(1, XS)]
    blocks = [block, hold(near, [att3]), *far]
    others = [send(b, SWAP_C) for b in blocks]

    mix = functools.partial(
        apply, pos=pos, query=query, gain=fast_gain[None, :], own=blocks, other=others
    )
    away = mix((1, 2, 3), attended=[att1, att2, att3], deps=[])
    [home] = mix((0,), attended=[att0], deps=[away[0]])
    parts = spread([home, *away])
    ahead = output(pos, parts, weights)
    result = arrange(pos, spread([ahead[-1], *ahead[:-1]]))
    return result


def solution(mesh):
    placed = (
        P("tok", None),
        P(None, "head"),
        P(None, "head"),
        P("head", None, None),
        P("head", None, None),
        P("head", None, None),
        P("head"),
        P("head", None),
        P(),
    )
    return jax.shard_map(
        body, mesh=mesh, in_specs=placed, out_specs=P("tok", "head"), check_vma=False
    )
```

```python
import functools
import math

import jax
import jax.numpy as jnp
from jax import lax
from jax.experimental import pallas as pl
from jax.experimental.pallas import tpu as pltpu
from jax.sharding import PartitionSpec as P

DH = 384
HID = 768
TOK = 1024
XS, ZS, CS, HS = 4, 8, 2, 4
SHARDS = XS * ZS * CS
TOKENS = TOK * SHARDS
XROWS = DH // XS
ROWS = 16
OWNERS = XROWS // ROWS
WIDE = HID + DH
KB = 512
QB = 256
BF, F32, I32 = jnp.bfloat16, jnp.float32, jnp.int32
NT = (((1,), (1,)), ((), ()))
VM = 56 * 1024 * 1024

SMEM = pl.BlockSpec(memory_space=pltpu.SMEM)
WHOLE = pl.BlockSpec(memory_space=pltpu.VMEM)
DEP = pl.BlockSpec(memory_space=pl.ANY)


def params():
    return pltpu.CompilerParams(vmem_limit_bytes=VM)


def mm(a, b):
    return jnp.dot(a, b, preferred_element_type=F32)


def sds(shape, dtype):
    return jax.ShapeDtypeStruct(shape, dtype)


SWAP_C = [(t, t ^ 1) for t in range(SHARDS)]
ALONG_Z = [
    [(x * ZS + z) * CS + c for z in range(ZS)] for x in range(XS) for c in range(CS)
]


def shift_x(d):
    return [(t, (t + d * ZS * CS) % SHARDS) for t in range(SHARDS)]


def shift_h(d):
    return [(h, (h + d) % HS) for h in range(HS)]


def full(shape):
    return pl.BlockSpec(shape, lambda i: (0,) * len(shape))


def keys_kernel(t_ref, w_ref, wr_ref, kv_ref, rates_ref):
    t = t_ref[...]
    kv_ref[...] = mm(t, w_ref[...]).astype(BF)
    raw = lax.dot_general(t, wr_ref[...], NT, preferred_element_type=F32)
    rates_ref[...] = (0.25 / math.sqrt(TOKENS)) * (
        jnp.maximum(raw, 0.0) + jnp.log1p(jnp.exp(-jnp.abs(raw)))
    )


def keys(tokens, qkv_weight, rate_weight):
    rows, wide = tokens.shape
    block = 512
    return pl.pallas_call(
        keys_kernel,
        grid=(rows // block,),
        in_specs=[
            pl.BlockSpec((block, wide), lambda i: (i, 0)),
            pl.BlockSpec((pl.Element(wide), pl.Element(2 * DH)), lambda i: (0, DH)),
            full((3, wide)),
        ],
        out_specs=[
            pl.BlockSpec((block, 2 * DH), lambda i: (i, 0)),
            pl.BlockSpec((block, 3), lambda i: (i, 0)),
        ],
        out_shape=[sds((rows, 2 * DH), BF), sds((rows, 3), F32)],
        compiler_params=params(),
        name="keys",
    )(tokens, qkv_weight, rate_weight.T)


def update_kernel(pos_ref, kv_ref, r_ref, w1_ref, w3_ref, w2_ref, send_ref, keep_ref, second):
    even = pos_ref[0] == 0
    k, v = kv_ref[:, :DH], kv_ref[:, DH:]
    r = r_ref[...]
    r1, r3 = r[:, 0:1], r[:, 1:2]
    k_t = k.T
    e2_t = (r[:, 2:3] * v.astype(F32)).astype(BF).T
    chunk = 256
    for j in range(HID // chunk):
        cols = slice(j * chunk, (j + 1) * chunk)
        a = mm(k, w1_ref[0, :, cols])
        b = mm(k, w3_ref[0, :, cols])
        back = lax.dot_general(v, w2_ref[0, cols, :], NT, preferred_element_type=F32)
        sig = jax.nn.sigmoid(a)
        act = a * sig
        z = (act * b).astype(BF)
        e1 = (r1 * back * b * (sig * (1.0 + a * (1.0 - sig)))).astype(BF)
        e3 = (r3 * back * act).astype(BF)
        first = mm(k_t, e1)
        gate = mm(k_t, e3)
        second[cols, :] = mm(e2_t, z).T
        keep_ref[:, cols] = jnp.where(even, first, gate)
        send_ref[:, cols] = jnp.where(even, gate, first).astype(BF)
    low, high = second[:DH, :], second[DH:, :]
    keep_ref[:, HID:] = jnp.where(even, low, high)
    send_ref[:, HID:] = jnp.where(even, high, low).astype(BF)


def update(pos, kv, rates, first_fast, gate_fast, second_fast):
    return pl.pallas_call(
        update_kernel,
        grid=(1,),
        in_specs=[
            SMEM,
            full(kv.shape),
            full(rates.shape),
            full((1, DH, HID)),
            full((1, DH, HID)),
            full((1, HID, DH)),
        ],
        out_specs=[full((DH, WIDE)), full((DH, WIDE))],
        out_shape=[sds((DH, WIDE), BF), sds((DH, WIDE), F32)],
        scratch_shapes=[pltpu.VMEM((HID, DH), F32)],
        compiler_params=params(),
        name="update",
    )(pos, kv, rates, first_fast, gate_fast, second_fast)


def rs_x_kernel(pos_ref, keep_ref, got_ref, *rest):
    outs = rest[-XS:]
    x = pos_ref[1]
    for d, out in enumerate(outs):
        rows = pl.ds(pl.multiple_of(lax.rem(x + d, XS) * XROWS, XROWS), XROWS)
        out[...] = (keep_ref[rows, :] + got_ref[rows, :].astype(F32)).astype(out.dtype)


def rs_x(pos, keep, got, deps):
    return pl.pallas_call(
        rs_x_kernel,
        grid=(1,),
        in_specs=[SMEM, full((DH, WIDE)), full((DH, WIDE))] + [DEP] * len(deps),
        out_specs=[full((XROWS, WIDE))] * XS,
        out_shape=[sds((XROWS, WIDE), F32)] + [sds((XROWS, WIDE), BF)] * (XS - 1),
        compiler_params=params(),
        name="rs_x",
    )(pos, keep, got, *deps)


def rs_z_kernel(own_ref, g1, g2, g3, *rest):
    out = rest[-1]
    for o in range(OWNERS):
        rows = slice(o * ROWS, (o + 1) * ROWS)
        total = (own_ref[rows, :] + g1[rows, :].astype(F32)) + (
            g2[rows, :].astype(F32) + g3[rows, :].astype(F32)
        )
        out[o] = total.astype(BF)
    out[OWNERS:] = jnp.zeros((ZS - OWNERS, ROWS, WIDE), BF)


def rs_z(own, got, deps):
    return pl.pallas_call(
        rs_z_kernel,
        grid=(1,),
        in_specs=[full((XROWS, WIDE))] * XS + [DEP] * len(deps),
        out_specs=full((ZS, ROWS, WIDE)),
        out_shape=sds((ZS, ROWS, WIDE), BF),
        compiler_params=params(),
        name="rs_z",
    )(own, *got, *deps)


def renorm_kernel(old_ref, got_ref, *rest):
    out = rest[-1]
    update = got_ref[0].astype(F32)
    for s in range(1, ZS):
        update = update + got_ref[s].astype(F32)
    old = old_ref[...]
    fresh = old + update
    for cols in (slice(0, HID), slice(HID, WIDE)):
        w, f = old[:, cols], fresh[:, cols]
        w_sq = jnp.sum(w * w, axis=1, keepdims=True)
        f_sq = jnp.sum(f * f, axis=1, keepdims=True)
        new = (f * (jnp.sqrt(w_sq) / jnp.sqrt(f_sq + 1e-6))).astype(BF)
        for s in range(ZS):
            out[s, :, cols] = new


def renorm(old, got, deps):
    shape = (ZS, ROWS, WIDE)
    return pl.pallas_call(
        renorm_kernel,
        grid=(1,),
        in_specs=[full((ROWS, WIDE)), full(shape)] + [DEP] * len(deps),
        out_specs=full(shape),
        out_shape=sds(shape, BF),
        compiler_params=params(),
        name="renorm",
    )(old, got, *deps)


def hold_kernel(value_ref, *rest):
    pass


def hold(value, deps):
    return pl.pallas_call(
        hold_kernel,
        in_specs=[DEP] * (1 + len(deps)),
        out_specs=DEP,
        out_shape=sds(value.shape, value.dtype),
        input_output_aliases={0: 0},
        compiler_params=params(),
        name="hold",
    )(value, *deps)


def project_kernel(t_ref, w_ref, *rest):
    q_ref = rest[-1]
    q_ref[...] = mm(t_ref[...], w_ref[...]).astype(BF)


def project(tokens, qkv_weight, deps):
    rows, wide = tokens.shape
    block = 256
    return pl.pallas_call(
        project_kernel,
        grid=(rows // block,),
        in_specs=[
            pl.BlockSpec((block, wide), lambda i: (i, 0)),
            pl.BlockSpec((wide, DH), lambda i: (0, 0)),
        ]
        + [DEP] * len(deps),
        out_specs=pl.BlockSpec((block, DH), lambda i: (i, 0)),
        out_shape=sds((rows, DH), BF),
        compiler_params=params(),
        name="project",
    )(tokens, qkv_weight, *deps)


def attend_kernel(
    ahead, pos_ref, lengths_ref, q_all, before, mine, after, dep_ref,
    out_ref, s_ref, kv_ref, q_ref, sems, q_sem,
):
    shard = pos_ref[3]
    piece = lax.rem(pos_ref[2] + ahead, HS)
    q_rows = pl.ds(pl.multiple_of(piece * QB, QB), QB)
    q_copy = pltpu.make_async_copy(q_all.at[q_rows, :], q_ref, q_sem)
    q_copy.start()
    row = lax.broadcasted_iota(I32, (QB, 1), 0)
    place = row + (shard * TOK + piece * QB)
    lengths = lengths_ref[...].astype(F32)
    count = lengths.shape[1]
    down = jnp.broadcast_to(lengths, (count, count)).T
    upper = lax.broadcasted_iota(I32, (count, count), 0) <= lax.broadcasted_iota(
        I32, (count, count), 1
    )
    ends = jnp.sum(jnp.where(upper, down, 0.0), axis=0, keepdims=True).astype(I32)
    shift = (shard - 1) * TOK
    begin = jnp.max(jnp.where(ends <= place, ends, 0), axis=1, keepdims=True) - shift
    end = jnp.min(jnp.where(ends <= place, TOKENS, ends), axis=1, keepdims=True) - shift
    first = lax.div(jnp.min(begin), KB)
    last = lax.div(jnp.max(end) + KB - 1, KB)
    per = TOK // KB
    scale = 1.0 / math.sqrt(DH)

    def fetch(ref, at, kb):
        rows = pl.ds(pl.multiple_of(at * KB, KB), KB)
        return pltpu.make_async_copy(ref.at[rows, :], kv_ref.at[kb], sems.at[kb])

    for s, ref in enumerate((before, mine, after)):

        def start(kb, carry, s=s, ref=ref):
            fetch(ref, kb - s * per, kb).start()
            return carry

        lo = jnp.clip(first, s * per, (s + 1) * per)
        hi = jnp.clip(last, s * per, (s + 1) * per)
        lax.fori_loop(lo, hi, start, 0)
    q_copy.wait()
    q = q_ref[...]

    def scores(kb, top):
        fetch(mine, 0, kb).wait()
        k = kv_ref[kb, :, :DH]
        sc = lax.dot_general(q, k, NT, preferred_element_type=F32) * scale
        col = lax.broadcasted_iota(I32, (QB, KB), 1) + kb * KB
        sc = jnp.where((col >= begin) & (col < end), sc, -1e30)
        s_ref[kb] = sc
        for lane in range(0, KB, 128):
            top = jnp.maximum(top, sc[:, lane : lane + 128])
        return top

    top = lax.fori_loop(first, last, scores, jnp.full((QB, 128), -1e30, F32))
    top = jnp.max(top, axis=1, keepdims=True)

    def weigh(kb, total):
        w = jnp.exp(s_ref[kb] - top)
        s_ref[kb] = w
        for lane in range(0, KB, 128):
            total = total + w[:, lane : lane + 128]
        return total

    total = lax.fori_loop(first, last, weigh, jnp.zeros((QB, 128), F32))
    inverse = 1.0 / jnp.sum(total, axis=1, keepdims=True)
    out_ref[...] = jnp.zeros_like(out_ref)

    def gather(kb, carry):
        probs = (s_ref[kb] * inverse).astype(BF)
        out_ref[...] += mm(probs, kv_ref[kb, :, DH:])
        return carry

    lax.fori_loop(first, last, gather, 0)


def first_kernel(pos_ref, w1_ref, w3_ref, w2_ref, *rest):
    ins, outs, (wide, narrow, row_sems), scratch = rest[:7], rest[7:9], rest[9:12], rest[12:]
    core, x, mine = pos_ref[0], pos_ref[1], pos_ref[3]
    z = lax.rem(lax.div(mine, CS), ZS)
    row = pl.multiple_of(jnp.minimum(x * XROWS + z * ROWS, DH - ROWS), ROWS)
    rows = pl.ds(row, ROWS)
    rows2 = pl.ds(pl.multiple_of(core * DH + row, ROWS), ROWS)
    copies = [
        pltpu.make_async_copy(w1_ref.at[0, rows, :], wide.at[0], row_sems.at[0]),
        pltpu.make_async_copy(w3_ref.at[0, rows, :], wide.at[1], row_sems.at[1]),
        pltpu.make_async_copy(w2_ref.at[0, rows2, :], narrow, row_sems.at[2]),
    ]
    for copy in copies:
        copy.start()
    attend_kernel(0, pos_ref, *ins[1:], outs[0], *scratch)
    for copy in copies:
        copy.wait()
    out_ref = outs[1]
    out_ref[:, :HID] = jnp.where(core == 0, wide[0].astype(F32), wide[1].astype(F32))
    out_ref[:, HID:] = narrow[...].astype(F32)


def attend(ahead, pos, lengths, query, before, mine, after, dep, old=()):
    blocks = 3 * TOK // KB
    kernel = functools.partial(attend_kernel, ahead)
    outs, shapes, scratch, lead = [full((QB, DH))], [sds((QB, DH), F32)], [], ()
    if old:
        kernel = first_kernel
        outs = outs + [full((ROWS, WIDE))]
        shapes = shapes + [sds((ROWS, WIDE), F32)]
        scratch = [
            pltpu.VMEM((2, ROWS, HID), BF),
            pltpu.VMEM((ROWS, DH), BF),
            pltpu.SemaphoreType.DMA((3,)),
        ]
        lead = (pos, *old)
    result = pl.pallas_call(
        kernel,
        grid=(1,),
        in_specs=([SMEM] + [DEP] * 3 if old else [])
        + [SMEM, full(lengths.shape)]
        + [DEP] * 5,
        out_specs=outs,
        out_shape=shapes,
        scratch_shapes=scratch
        + [
            pltpu.VMEM((blocks, QB, KB), F32),
            pltpu.VMEM((blocks, KB, 2 * DH), BF),
            pltpu.VMEM((QB, DH), BF),
            pltpu.SemaphoreType.DMA((blocks,)),
            pltpu.SemaphoreType.DMA,
        ],
        compiler_params=params(),
        name=f"attend_{ahead}",
    )(*lead, pos, lengths, query, before, mine, after, dep)
    return result if old else result[0]


def apply_kernel(aheads, pos_ref, q_ref, gain_ref, *rest):
    count = len(aheads)
    own_ref, other_ref = rest[-2:]
    attended, outs = rest[2 * XS : 2 * XS + count], rest[-count - 2 : -2]
    for d in range(XS):
        at = lax.rem(pos_ref[1] - d + XS, XS) * XROWS
        rows = pl.ds(pl.multiple_of(at, XROWS), XROWS)
        own_ref[rows, :] = rest[d][...]
        other_ref[rows, :] = rest[XS + d][...]
    even = pos_ref[0] == 0
    for ahead, att_ref, out in zip(aheads, attended, outs):
        piece = lax.rem(pos_ref[2] + ahead, HS)
        q = q_ref[pl.ds(pl.multiple_of(piece * QB, QB), QB), :]
        mine = mm(q, own_ref[:, :HID])
        theirs = mm(q, other_ref[:, :HID])
        a = jnp.where(even, mine, theirs)
        b = jnp.where(even, theirs, mine)
        hidden = (a * jax.nn.sigmoid(a) * b).astype(BF)
        h0, h1 = hidden[:, :DH], hidden[:, DH:]
        h_own = jnp.where(even, h0, h1)
        h_other = jnp.where(even, h1, h0)
        applied = mm(h_own, own_ref[:, HID:]) + mm(h_other, other_ref[:, HID:])
        mean = jnp.mean(applied * applied, axis=1, keepdims=True)
        normed = applied * lax.rsqrt(mean + 1e-6) * gain_ref[...]
        out[...] = (att_ref[...] + normed).astype(BF)


def apply(aheads, pos, query, gain, own, other, attended, deps):
    count = len(aheads)
    return pl.pallas_call(
        functools.partial(apply_kernel, aheads),
        grid=(1,),
        in_specs=[SMEM, full((TOK, DH)), full((1, DH))]
        + [full((XROWS, WIDE))] * (2 * XS)
        + [full((QB, DH))] * count
        + [DEP] * len(deps),
        out_specs=[full((QB, DH))] * count,
        out_shape=[sds((QB, DH), BF)] * count,
        scratch_shapes=[pltpu.VMEM((DH, WIDE), BF)] * 2,
        compiler_params=params(),
        name=f"apply_{count}",
    )(pos, query, gain, *own, *other, *attended, *deps)


def output_kernel(pos_ref, *refs):
    parts, weights, outs = refs[:HS], refs[HS : 2 * HS], refs[2 * HS :]
    head = pos_ref[2]
    for e, out in enumerate(outs):
        cols = pl.ds(pl.multiple_of(lax.rem(head + e + 1, HS) * DH, DH), DH)
        total = mm(parts[0][...], weights[0][:, cols])
        for part, weight in zip(parts[1:], weights[1:]):
            total = total + mm(part[...], weight[:, cols])
        out[...] = total.astype(BF)


def output(pos, parts, weights):
    return pl.pallas_call(
        output_kernel,
        grid=(1,),
        in_specs=[SMEM] + [full((QB, DH))] * HS + [full((DH, HS * DH))] * HS,
        out_specs=[full((QB, DH))] * HS,
        out_shape=[sds((QB, DH), BF)] * HS,
        compiler_params=params(),
        name="output",
    )(pos, *parts, *weights)


def arrange_kernel(pos_ref, *refs):
    parts, out = refs[:-1], refs[-1]
    head = pos_ref[2]
    for d, part in enumerate(parts):
        rows = pl.ds(pl.multiple_of(lax.rem(head - d + HS, HS) * QB, QB), QB)
        out[rows, :] = part[...]


def arrange(pos, parts):
    return pl.pallas_call(
        arrange_kernel,
        grid=(1,),
        in_specs=[SMEM] + [full((QB, DH))] * HS,
        out_specs=full((TOK, DH)),
        out_shape=sds((TOK, DH), BF),
        compiler_params=params(),
        name="arrange",
    )(pos, *parts)


def body(
    tokens,
    qkv_weight,
    rate_weight,
    first_fast,
    gate_fast,
    second_fast,
    fast_gain,
    out_weight,
    frame_lengths,
):
    mine = lax.axis_index("tok")
    head = lax.axis_index("head")
    x, core = mine // (ZS * CS), mine % CS
    send = lambda value, pairs: lax.ppermute(value, "tok", pairs)

    kv, rates = keys(tokens, qkv_weight, rate_weight)
    up = [(i, i + 1) for i in range(SHARDS - 1)]
    before = send(kv, up)
    after = send(kv, [(j, i) for i, j in up])
    pos = jnp.stack([core, x, head, mine]).astype(I32)
    give, keep = update(pos, kv, rates, first_fast, gate_fast, second_fast)
    got = send(give, SWAP_C)

    def spread(parts):
        return [lax.ppermute(p, "head", shift_h(d)) if d else p for d, p in enumerate(parts)]

    weights = spread([out_weight] * HS)

    def exchange(blocks):
        return lax.all_to_all(blocks, "tok", 0, 0, axis_index_groups=ALONG_Z)

    query = project(tokens, qkv_weight, [give])
    own, *gives = rs_x(pos, keep, got, [before, after, query])
    got = [send(g, shift_x(d + 1)) for d, g in enumerate(gives)]
    att = functools.partial(attend, pos=pos, lengths=frame_lengths[None, :], query=query, before=before, mine=kv, after=after)
    att0, old = att(0, dep=own, old=(first_fast, gate_fast, second_fast))
    total = rs_z(own, got, [att0, old])
    got = exchange(total)
    att1 = att(1, dep=total)
    fresh = renorm(old, got, [att1, weights[1], weights[3]])
    got = exchange(fresh)
    att2 = att(2, dep=fresh)
    block = hold(got, [att2])[:OWNERS].reshape(XROWS, WIDE)
    att3 = att(3, dep=block)
    near, *far = [send(block, shift_x(d)) for d in range(1, XS)]
    blocks = [block, hold(near, [att3, weights[2]]), *far]
    others = [send(b, SWAP_C) for b in blocks]

    mix = functools.partial(
        apply, pos=pos, query=query, gain=fast_gain[None, :], own=blocks, other=others
    )
    away = mix((1, 2, 3), attended=[att1, att2, att3], deps=[])
    [home] = mix((0,), attended=[att0], deps=[away[0]])
    parts = spread([home, *away])
    ahead = output(pos, parts, weights)
    result = arrange(pos, spread([ahead[-1], *ahead[:-1]]))
    return result


def solution(mesh):
    placed = (
        P("tok", None),
        P(None, "head"),
        P(None, "head"),
        P("head", None, None),
        P("head", None, None),
        P("head", None, None),
        P("head"),
        P("head", None),
        P(),
    )
    return jax.shard_map(
        body, mesh=mesh, in_specs=placed, out_specs=P("tok", "head"), check_vma=False
    )
```

```python
import functools
import math

import jax
import jax.numpy as jnp
from jax import lax
from jax.experimental import pallas as pl
from jax.experimental.pallas import tpu as pltpu
from jax.sharding import PartitionSpec as P

DH = 384
HID = 768
TOK = 1024
XS, ZS, CS, HS = 4, 8, 2, 4
SHARDS = XS * ZS * CS
TOKENS = TOK * SHARDS
XROWS = DH // XS
ROWS = 16
OWNERS = XROWS // ROWS
WIDE = HID + DH
KB = 512
QB = 256
BF, F32, I32 = jnp.bfloat16, jnp.float32, jnp.int32
NT = (((1,), (1,)), ((), ()))
VM = 56 * 1024 * 1024

SMEM = pl.BlockSpec(memory_space=pltpu.SMEM)
WHOLE = pl.BlockSpec(memory_space=pltpu.VMEM)
DEP = pl.BlockSpec(memory_space=pl.ANY)


def params():
    return pltpu.CompilerParams(vmem_limit_bytes=VM)


def mm(a, b):
    return jnp.dot(a, b, preferred_element_type=F32)


def sds(shape, dtype):
    return jax.ShapeDtypeStruct(shape, dtype)


SWAP_C = [(t, t ^ 1) for t in range(SHARDS)]
ALONG_Z = [
    [(x * ZS + z) * CS + c for z in range(ZS)] for x in range(XS) for c in range(CS)
]


def shift_x(d):
    return [(t, (t + d * ZS * CS) % SHARDS) for t in range(SHARDS)]


def shift_h(d):
    return [(h, (h + d) % HS) for h in range(HS)]


def full(shape):
    return pl.BlockSpec(shape, lambda i: (0,) * len(shape))


def keys_kernel(t_ref, w_ref, wr_ref, kv_ref, rates_ref):
    t = t_ref[...]
    kv_ref[...] = mm(t, w_ref[...]).astype(BF)
    raw = lax.dot_general(t, wr_ref[...], NT, preferred_element_type=F32)
    rates_ref[...] = (0.25 / math.sqrt(TOKENS)) * (
        jnp.maximum(raw, 0.0) + jnp.log1p(jnp.exp(-jnp.abs(raw)))
    )


def keys(tokens, qkv_weight, rate_weight):
    rows, wide = tokens.shape
    block = 512
    return pl.pallas_call(
        keys_kernel,
        grid=(rows // block,),
        in_specs=[
            pl.BlockSpec((block, wide), lambda i: (i, 0)),
            pl.BlockSpec((pl.Element(wide), pl.Element(2 * DH)), lambda i: (0, DH)),
            full((3, wide)),
        ],
        out_specs=[
            pl.BlockSpec((block, 2 * DH), lambda i: (i, 0)),
            pl.BlockSpec((block, 3), lambda i: (i, 0)),
        ],
        out_shape=[sds((rows, 2 * DH), BF), sds((rows, 3), F32)],
        compiler_params=params(),
        name="keys",
    )(tokens, qkv_weight, rate_weight.T)


def update_kernel(pos_ref, kv_ref, r_ref, w1_ref, w3_ref, w2_ref, send_ref, keep_ref, second):
    even = pos_ref[0] == 0
    k, v = kv_ref[:, :DH], kv_ref[:, DH:]
    r = r_ref[...]
    r1, r3 = r[:, 0:1], r[:, 1:2]
    k_t = k.T
    e2_t = (r[:, 2:3] * v.astype(F32)).astype(BF).T
    chunk = 256
    for j in range(HID // chunk):
        cols = slice(j * chunk, (j + 1) * chunk)
        a = mm(k, w1_ref[0, :, cols])
        b = mm(k, w3_ref[0, :, cols])
        back = lax.dot_general(v, w2_ref[0, cols, :], NT, preferred_element_type=F32)
        sig = jax.nn.sigmoid(a)
        act = a * sig
        z = (act * b).astype(BF)
        e1 = (r1 * back * b * (sig * (1.0 + a * (1.0 - sig)))).astype(BF)
        e3 = (r3 * back * act).astype(BF)
        first = mm(k_t, e1)
        gate = mm(k_t, e3)
        second[cols, :] = mm(e2_t, z).T
        keep_ref[:, cols] = jnp.where(even, first, gate)
        send_ref[:, cols] = jnp.where(even, gate, first).astype(BF)
    low, high = second[:DH, :], second[DH:, :]
    keep_ref[:, HID:] = jnp.where(even, low, high)
    send_ref[:, HID:] = jnp.where(even, high, low).astype(BF)


def update(pos, kv, rates, first_fast, gate_fast, second_fast):
    return pl.pallas_call(
        update_kernel,
        grid=(1,),
        in_specs=[
            SMEM,
            full(kv.shape),
            full(rates.shape),
            full((1, DH, HID)),
            full((1, DH, HID)),
            full((1, HID, DH)),
        ],
        out_specs=[full((DH, WIDE)), full((DH, WIDE))],
        out_shape=[sds((DH, WIDE), BF), sds((DH, WIDE), F32)],
        scratch_shapes=[pltpu.VMEM((HID, DH), F32)],
        compiler_params=params(),
        name="update",
    )(pos, kv, rates, first_fast, gate_fast, second_fast)


def rs_x_kernel(pos_ref, keep_ref, got_ref, *rest):
    outs = rest[-XS:]
    x = pos_ref[1]
    for d, out in enumerate(outs):
        rows = pl.ds(pl.multiple_of(lax.rem(x + d, XS) * XROWS, XROWS), XROWS)
        out[...] = (keep_ref[rows, :] + got_ref[rows, :].astype(F32)).astype(out.dtype)


def rs_x(pos, keep, got, deps):
    return pl.pallas_call(
        rs_x_kernel,
        grid=(1,),
        in_specs=[SMEM, full((DH, WIDE)), full((DH, WIDE))] + [DEP] * len(deps),
        out_specs=[full((XROWS, WIDE))] * XS,
        out_shape=[sds((XROWS, WIDE), F32)] + [sds((XROWS, WIDE), BF)] * (XS - 1),
        compiler_params=params(),
        name="rs_x",
    )(pos, keep, got, *deps)


def rs_z_kernel(own_ref, g1, g2, g3, *rest):
    out = rest[-1]
    for o in range(OWNERS):
        rows = slice(o * ROWS, (o + 1) * ROWS)
        total = (own_ref[rows, :] + g1[rows, :].astype(F32)) + (
            g2[rows, :].astype(F32) + g3[rows, :].astype(F32)
        )
        out[o] = total.astype(BF)
    out[OWNERS:] = jnp.zeros((ZS - OWNERS, ROWS, WIDE), BF)


def rs_z(own, got, deps):
    return pl.pallas_call(
        rs_z_kernel,
        grid=(1,),
        in_specs=[full((XROWS, WIDE))] * XS + [DEP] * len(deps),
        out_specs=full((ZS, ROWS, WIDE)),
        out_shape=sds((ZS, ROWS, WIDE), BF),
        compiler_params=params(),
        name="rs_z",
    )(own, *got, *deps)


def renorm_kernel(old_ref, got_ref, *rest):
    out = rest[-1]
    update = got_ref[0].astype(F32)
    for s in range(1, ZS):
        update = update + got_ref[s].astype(F32)
    old = old_ref[...]
    fresh = old + update
    for cols in (slice(0, HID), slice(HID, WIDE)):
        w, f = old[:, cols], fresh[:, cols]
        w_sq = jnp.sum(w * w, axis=1, keepdims=True)
        f_sq = jnp.sum(f * f, axis=1, keepdims=True)
        new = (f * (jnp.sqrt(w_sq) / jnp.sqrt(f_sq + 1e-6))).astype(BF)
        for s in range(ZS):
            out[s, :, cols] = new


def renorm(old, got, deps):
    shape = (ZS, ROWS, WIDE)
    return pl.pallas_call(
        renorm_kernel,
        grid=(1,),
        in_specs=[full((ROWS, WIDE)), full(shape)] + [DEP] * len(deps),
        out_specs=full(shape),
        out_shape=sds(shape, BF),
        compiler_params=params(),
        name="renorm",
    )(old, got, *deps)


def hold_kernel(value_ref, *rest):
    pass


def hold(value, deps):
    return pl.pallas_call(
        hold_kernel,
        in_specs=[DEP] * (1 + len(deps)),
        out_specs=DEP,
        out_shape=sds(value.shape, value.dtype),
        input_output_aliases={0: 0},
        compiler_params=params(),
        name="hold",
    )(value, *deps)


def project_kernel(t_ref, w_ref, *rest):
    q_ref = rest[-1]
    q_ref[...] = mm(t_ref[...], w_ref[...]).astype(BF)


def project(tokens, qkv_weight, deps):
    rows, wide = tokens.shape
    block = 256
    return pl.pallas_call(
        project_kernel,
        grid=(rows // block,),
        in_specs=[
            pl.BlockSpec((block, wide), lambda i: (i, 0)),
            pl.BlockSpec((wide, DH), lambda i: (0, 0)),
        ]
        + [DEP] * len(deps),
        out_specs=pl.BlockSpec((block, DH), lambda i: (i, 0)),
        out_shape=sds((rows, DH), BF),
        compiler_params=params(),
        name="project",
    )(tokens, qkv_weight, *deps)


def attend_kernel(
    ahead, pos_ref, lengths_ref, q_all, before, mine, after, dep_ref,
    out_ref, s_ref, kv_ref, q_ref, sems, q_sem,
):
    shard = pos_ref[3]
    piece = lax.rem(pos_ref[2] + ahead, HS)
    q_rows = pl.ds(pl.multiple_of(piece * QB, QB), QB)
    q_copy = pltpu.make_async_copy(q_all.at[q_rows, :], q_ref, q_sem)
    q_copy.start()
    row = lax.broadcasted_iota(I32, (QB, 1), 0)
    place = row + (shard * TOK + piece * QB)
    lengths = lengths_ref[...].astype(F32)
    count = lengths.shape[1]
    down = jnp.broadcast_to(lengths, (count, count)).T
    upper = lax.broadcasted_iota(I32, (count, count), 0) <= lax.broadcasted_iota(
        I32, (count, count), 1
    )
    ends = jnp.sum(jnp.where(upper, down, 0.0), axis=0, keepdims=True).astype(I32)
    shift = (shard - 1) * TOK
    begin = jnp.max(jnp.where(ends <= place, ends, 0), axis=1, keepdims=True) - shift
    end = jnp.min(jnp.where(ends <= place, TOKENS, ends), axis=1, keepdims=True) - shift
    first = lax.div(jnp.min(begin), KB)
    last = lax.div(jnp.max(end) + KB - 1, KB)
    per = TOK // KB
    scale = 1.0 / math.sqrt(DH)

    def fetch(ref, at, kb):
        rows = pl.ds(pl.multiple_of(at * KB, KB), KB)
        return pltpu.make_async_copy(ref.at[rows, :], kv_ref.at[kb], sems.at[kb])

    for s, ref in enumerate((before, mine, after)):

        def start(kb, carry, s=s, ref=ref):
            fetch(ref, kb - s * per, kb).start()
            return carry

        lo = jnp.clip(first, s * per, (s + 1) * per)
        hi = jnp.clip(last, s * per, (s + 1) * per)
        lax.fori_loop(lo, hi, start, 0)
    q_copy.wait()
    q = q_ref[...]

    def scores(kb, top):
        fetch(mine, 0, kb).wait()
        k = kv_ref[kb, :, :DH]
        sc = lax.dot_general(q, k, NT, preferred_element_type=F32) * scale
        col = lax.broadcasted_iota(I32, (QB, KB), 1) + kb * KB
        sc = jnp.where((col >= begin) & (col < end), sc, -1e30)
        s_ref[kb] = sc
        for lane in range(0, KB, 128):
            top = jnp.maximum(top, sc[:, lane : lane + 128])
        return top

    top = lax.fori_loop(first, last, scores, jnp.full((QB, 128), -1e30, F32))
    top = jnp.max(top, axis=1, keepdims=True)

    def weigh(kb, total):
        w = jnp.exp(s_ref[kb] - top)
        s_ref[kb] = w
        for lane in range(0, KB, 128):
            total = total + w[:, lane : lane + 128]
        return total

    total = lax.fori_loop(first, last, weigh, jnp.zeros((QB, 128), F32))
    inverse = 1.0 / jnp.sum(total, axis=1, keepdims=True)
    out_ref[...] = jnp.zeros_like(out_ref)

    def gather(kb, carry):
        probs = (s_ref[kb] * inverse).astype(BF)
        out_ref[...] += mm(probs, kv_ref[kb, :, DH:])
        return carry

    lax.fori_loop(first, last, gather, 0)


def first_kernel(pos_ref, w1_ref, w3_ref, w2_ref, *rest):
    ins, outs, (wide, narrow, row_sems), scratch = rest[:7], rest[7:9], rest[9:12], rest[12:]
    core, x, mine = pos_ref[0], pos_ref[1], pos_ref[3]
    z = lax.rem(lax.div(mine, CS), ZS)
    row = pl.multiple_of(jnp.minimum(x * XROWS + z * ROWS, DH - ROWS), ROWS)
    rows = pl.ds(row, ROWS)
    rows2 = pl.ds(pl.multiple_of(core * DH + row, ROWS), ROWS)
    copies = [
        pltpu.make_async_copy(w1_ref.at[0, rows, :], wide.at[0], row_sems.at[0]),
        pltpu.make_async_copy(w3_ref.at[0, rows, :], wide.at[1], row_sems.at[1]),
        pltpu.make_async_copy(w2_ref.at[0, rows2, :], narrow, row_sems.at[2]),
    ]
    for copy in copies:
        copy.start()
    attend_kernel(0, pos_ref, *ins[1:], outs[0], *scratch)
    for copy in copies:
        copy.wait()
    out_ref = outs[1]
    out_ref[:, :HID] = jnp.where(core == 0, wide[0].astype(F32), wide[1].astype(F32))
    out_ref[:, HID:] = narrow[...].astype(F32)


def attend(ahead, pos, lengths, query, before, mine, after, dep, old=()):
    blocks = 3 * TOK // KB
    kernel = functools.partial(attend_kernel, ahead)
    outs, shapes, scratch, lead = [full((QB, DH))], [sds((QB, DH), F32)], [], ()
    if old:
        kernel = first_kernel
        outs = outs + [full((ROWS, WIDE))]
        shapes = shapes + [sds((ROWS, WIDE), F32)]
        scratch = [
            pltpu.VMEM((2, ROWS, HID), BF),
            pltpu.VMEM((ROWS, DH), BF),
            pltpu.SemaphoreType.DMA((3,)),
        ]
        lead = (pos, *old)
    result = pl.pallas_call(
        kernel,
        grid=(1,),
        in_specs=([SMEM] + [DEP] * 3 if old else [])
        + [SMEM, full(lengths.shape)]
        + [DEP] * 5,
        out_specs=outs,
        out_shape=shapes,
        scratch_shapes=scratch
        + [
            pltpu.VMEM((blocks, QB, KB), F32),
            pltpu.VMEM((blocks, KB, 2 * DH), BF),
            pltpu.VMEM((QB, DH), BF),
            pltpu.SemaphoreType.DMA((blocks,)),
            pltpu.SemaphoreType.DMA,
        ],
        compiler_params=params(),
        name=f"attend_{ahead}",
    )(*lead, pos, lengths, query, before, mine, after, dep)
    return result if old else result[0]


def apply_kernel(aheads, pos_ref, q_ref, gain_ref, *rest):
    count = len(aheads)
    own_ref, other_ref = rest[-2:]
    attended, outs = rest[2 * XS : 2 * XS + count], rest[-count - 2 : -2]
    for d in range(XS):
        at = lax.rem(pos_ref[1] - d + XS, XS) * XROWS
        rows = pl.ds(pl.multiple_of(at, XROWS), XROWS)
        own_ref[rows, :] = rest[d][...]
        other_ref[rows, :] = rest[XS + d][...]
    even = pos_ref[0] == 0
    for ahead, att_ref, out in zip(aheads, attended, outs):
        piece = lax.rem(pos_ref[2] + ahead, HS)
        q = q_ref[pl.ds(pl.multiple_of(piece * QB, QB), QB), :]
        mine = mm(q, own_ref[:, :HID])
        theirs = mm(q, other_ref[:, :HID])
        a = jnp.where(even, mine, theirs)
        b = jnp.where(even, theirs, mine)
        hidden = (a * jax.nn.sigmoid(a) * b).astype(BF)
        h0, h1 = hidden[:, :DH], hidden[:, DH:]
        h_own = jnp.where(even, h0, h1)
        h_other = jnp.where(even, h1, h0)
        applied = mm(h_own, own_ref[:, HID:]) + mm(h_other, other_ref[:, HID:])
        mean = jnp.mean(applied * applied, axis=1, keepdims=True)
        normed = applied * lax.rsqrt(mean + 1e-6) * gain_ref[...]
        out[...] = (att_ref[...] + normed).astype(BF)


def apply(aheads, pos, query, gain, own, other, attended, deps):
    count = len(aheads)
    return pl.pallas_call(
        functools.partial(apply_kernel, aheads),
        grid=(1,),
        in_specs=[SMEM, full((TOK, DH)), full((1, DH))]
        + [full((XROWS, WIDE))] * (2 * XS)
        + [full((QB, DH))] * count
        + [DEP] * len(deps),
        out_specs=[full((QB, DH))] * count,
        out_shape=[sds((QB, DH), BF)] * count,
        scratch_shapes=[pltpu.VMEM((DH, WIDE), BF)] * 2,
        compiler_params=params(),
        name=f"apply_{count}",
    )(pos, query, gain, *own, *other, *attended, *deps)


def output_kernel(pos_ref, *refs):
    parts, weights, outs = refs[:HS], refs[HS : 2 * HS], refs[2 * HS :]
    head = pos_ref[2]
    for e, out in enumerate(outs):
        cols = pl.ds(pl.multiple_of(lax.rem(head + e + 1, HS) * DH, DH), DH)
        total = mm(parts[0][...], weights[0][:, cols])
        for part, weight in zip(parts[1:], weights[1:]):
            total = total + mm(part[...], weight[:, cols])
        out[...] = total.astype(BF)


def output(pos, parts, weights):
    return pl.pallas_call(
        output_kernel,
        grid=(1,),
        in_specs=[SMEM] + [full((QB, DH))] * HS + [full((DH, HS * DH))] * HS,
        out_specs=[full((QB, DH))] * HS,
        out_shape=[sds((QB, DH), BF)] * HS,
        compiler_params=params(),
        name="output",
    )(pos, *parts, *weights)


def arrange_kernel(pos_ref, *refs):
    parts, out = refs[:-1], refs[-1]
    head = pos_ref[2]
    for d, part in enumerate(parts):
        rows = pl.ds(pl.multiple_of(lax.rem(head - d + HS, HS) * QB, QB), QB)
        out[rows, :] = part[...]


def arrange(pos, parts):
    return pl.pallas_call(
        arrange_kernel,
        grid=(1,),
        in_specs=[SMEM] + [full((QB, DH))] * HS,
        out_specs=full((TOK, DH)),
        out_shape=sds((TOK, DH), BF),
        compiler_params=params(),
        name="arrange",
    )(pos, *parts)


def body(
    tokens,
    qkv_weight,
    rate_weight,
    first_fast,
    gate_fast,
    second_fast,
    fast_gain,
    out_weight,
    frame_lengths,
):
    mine = lax.axis_index("tok")
    head = lax.axis_index("head")
    x, core = mine // (ZS * CS), mine % CS
    send = lambda value, pairs: lax.ppermute(value, "tok", pairs)

    kv, rates = keys(tokens, qkv_weight, rate_weight)
    up = [(i, i + 1) for i in range(SHARDS - 1)]
    before = send(kv, up)
    after = send(kv, [(j, i) for i, j in up])
    pos = jnp.stack([core, x, head, mine]).astype(I32)
    give, keep = update(pos, kv, rates, first_fast, gate_fast, second_fast)
    got = send(give, SWAP_C)

    def spread(parts):
        return [lax.ppermute(p, "head", shift_h(d)) if d else p for d, p in enumerate(parts)]

    weights = spread([out_weight] * HS)

    def exchange(blocks):
        return lax.all_to_all(blocks, "tok", 0, 0, axis_index_groups=ALONG_Z)

    own, *gives = rs_x(pos, keep, got, [before, after])
    got = [send(g, shift_x(d + 1)) for d, g in enumerate(gives)]
    query = project(tokens, qkv_weight, [own])
    att = functools.partial(attend, pos=pos, lengths=frame_lengths[None, :], query=query, before=before, mine=kv, after=after)
    att0, old = att(0, dep=own, old=(first_fast, gate_fast, second_fast))
    total = rs_z(own, got, [att0, old])
    got = exchange(total)
    att1 = att(1, dep=total)
    fresh = renorm(old, got, [att1, weights[1], weights[3]])
    got = exchange(fresh)
    att2 = att(2, dep=fresh)
    block = hold(got, [att2])[:OWNERS].reshape(XROWS, WIDE)
    att3 = att(3, dep=block)
    near, *far = [send(block, shift_x(d)) for d in range(1, XS)]
    blocks = [block, hold(near, [att3, weights[2]]), *far]
    others = [send(b, SWAP_C) for b in blocks]

    mix = functools.partial(
        apply, pos=pos, query=query, gain=fast_gain[None, :], own=blocks, other=others
    )
    away = mix((1, 2, 3), attended=[att1, att2, att3], deps=[])
    [home] = mix((0,), attended=[att0], deps=[away[0]])
    parts = spread([home, *away])
    ahead = output(pos, parts, weights)
    result = arrange(pos, spread([ahead[-1], *ahead[:-1]]))
    return result


def solution(mesh):
    placed = (
        P("tok", None),
        P(None, "head"),
        P(None, "head"),
        P("head", None, None),
        P("head", None, None),
        P("head", None, None),
        P("head"),
        P("head", None),
        P(),
    )
    return jax.shard_map(
        body, mesh=mesh, in_specs=placed, out_specs=P("tok", "head"), check_vma=False
    )
```
